128 devices in a mesh: gx: 8 (over x, z_hi), gy: 16 (over z_lo, y, core).
Axes of the slice: x: 4, y: 4, z: 4 (z_hi: 2, z_lo: 2; z = z_hi * 2 + z_lo), core: 2. Of those that a mesh axis runs over, the one named last changes fastest.
Arguments:
- links: float32 [4, 3, 3, 2, 16, 32, 6, 128], P(None, None, None, None, 'gx', 'gy'), may hold values from -1 to 1, as said below
- incoming: float32 [4, 3, 3, 2, 16, 32, 4, 128], P(None, None, None, None, 'gx', 'gy'), may hold values from -6 to 6
Outputs:
- force: float32 [4, 3, 3, 2, 16, 32, 4, 128], P(None, None, None, None, 'gx', 'gy')
The draws below stay inside these ranges and needn't reach their ends.
Inputs may be any that keep to these rules, and one draw needn't show every extreme that they name: `links`: each link is a special unitary 3 x 3 matrix.
All inputs are finite; a program needn't handle non-finite values.
Results may differ from the reference program's by a relative error of at most 0.0003.
Values sent between devices are 32-bit elements; how exact they have to be, the bound alone decides.
No kernel may reach another device: no remote copies, remote signals or barrier semaphores. Data moves between devices by JAX's collectives and lax.ppermute only.
A program may use at most 128 MiB of HBM per device.

```python
from functools import partial
import jax
import jax.numpy as jnp
from jax import lax

Z = 128
TS = 4
NX = 16
NY = 32


phase_rows = [[0.0, 0.6, -0.6], [0.3, 0.0, -0.3], [0.6, 0.9, -1.5], [0.9, 0.3, -1.2]]


def special_unitary(matrix):
    row_one = matrix[..., 0, :]
    row_one = row_one / jnp.sqrt(jnp.sum(jnp.abs(row_one) ** 2, axis=-1, keepdims=True))
    row_two = matrix[..., 1, :]
    row_two = row_two - jnp.sum(jnp.conj(row_one) * row_two, axis=-1, keepdims=True) * row_one
    row_two = row_two / jnp.sqrt(jnp.sum(jnp.abs(row_two) ** 2, axis=-1, keepdims=True))
    row_three = jnp.conj(jnp.cross(row_one, row_two))
    return jnp.stack([row_one, row_two, row_three], axis=-2)


def matmul_three(former, latter):
    return jnp.einsum('...ij,...jk->...ik', former, latter, precision=lax.Precision.HIGHEST)


def draw_links(key, part):
    gauge_key, noise_key = jax.random.split(jax.random.fold_in(key, 17))
    real_key, imag_key = jax.random.split(gauge_key)
    noise_real_key, noise_imag_key = jax.random.split(noise_key)
    gauge_shape = (NX, NY, TS + 3, Z, 3, 3)
    noise_shape = (4, NX, NY, TS + 2, Z, 3, 3)
    identity = jnp.eye(3, dtype=jnp.float32)
    gauge_real = jax.random.normal(real_key, gauge_shape, jnp.float32)
    gauge_imag = jax.random.normal(imag_key, gauge_shape, jnp.float32)
    noise_real = jax.random.normal(noise_real_key, noise_shape, jnp.float32)
    noise_imag = jax.random.normal(noise_imag_key, noise_shape, jnp.float32)
    gauge = special_unitary(gauge_real + 1j * gauge_imag)
    noise = special_unitary(6.0 * identity + noise_real + 1j * noise_imag)
    coord_x = jnp.arange(NX, dtype=jnp.int32)[:, None, None, None]
    coord_y = jnp.arange(NY, dtype=jnp.int32)[None, :, None, None]
    coord_t = jnp.arange(TS + 2, dtype=jnp.int32)[None, None, :, None]
    coord_z = jnp.arange(Z, dtype=jnp.int32)[None, None, None, :]
    parity = (coord_x + coord_y + coord_t + coord_z) % 2
    sign = 1.0 - 2.0 * parity.astype(jnp.float32)
    table = jnp.array(phase_rows, dtype=jnp.float32)
    angle = table[:, None, None, None, None, :] * sign[None, :, :, :, :, None]
    backbone = jnp.exp(1j * angle)[..., :, None] * identity
    core = matmul_three(backbone, noise)
    here = gauge[:, :, :TS + 2]
    aheads = [jnp.roll(here, -1, axis=0), jnp.roll(here, -1, axis=1), jnp.roll(here, -1, axis=3), gauge[:, :, 1:TS + 3]]
    result = []
    for direction in range(4):
        ahead_dagger = jnp.conj(jnp.swapaxes(aheads[direction], -1, -2))
        result.append(matmul_three(matmul_three(here, core[direction]), ahead_dagger))
    unitary = jnp.stack(result, axis=0)
    stacked = jnp.stack([jnp.real(unitary), jnp.imag(unitary)], axis=-1).astype(jnp.float32)
    return jnp.transpose(stacked, (0, 5, 6, 7, 1, 2, 3, 4))


def shard_levels(rng, shape, cuts, least, largest):
    level, own = 1.0, jax.random.fold_in(rng, 6)
    for position, shards_of in cuts:
        steps = jnp.exp(jax.random.uniform(jax.random.fold_in(own, position), (shards_of,), jnp.float32, least / len(cuts), largest / len(cuts)))
        level = level * jnp.repeat(steps, shape[position] // shards_of).reshape([-1 if axis == position else 1 for axis in range(len(shape))])
    return level


def gaussian(rng, dims, scale, limit, cuts=(), kind=jnp.bfloat16):
    values = scale * jax.random.normal(rng, dims, jnp.float32)
    if cuts:
        values = values * shard_levels(rng, dims, cuts, -0.22, 0.18)
    return jnp.clip(values, -limit, limit).astype(kind)


def setup_inputs(seed: int = 0) -> dict:
    arg_keys = jax.random.split(jax.random.key(seed), 3)
    links = draw_links(jax.random.fold_in(arg_keys[2], 71), 0)
    incoming = gaussian(arg_keys[1], (4, 3, 3, 2, NX, NY, TS, Z), 1.0, 6.0, ((4, 8), (5, 16)), jnp.float32)
    return {"links": links, "incoming": incoming}


smear_weight = 0.2

def product(former, latter):
    former_real, former_imag = former
    latter_real, latter_imag = latter
    real_part = lax.optimization_barrier(jnp.sum(former_real[:, :, None] * latter_real[None] - former_imag[:, :, None] * latter_imag[None], axis=1))
    imag_part = lax.optimization_barrier(jnp.sum(former_real[:, :, None] * latter_imag[None] + former_imag[:, :, None] * latter_real[None], axis=1))
    return (real_part, imag_part)

def adjoint(matrix):
    return (jnp.swapaxes(matrix[0], 0, 1), -jnp.swapaxes(matrix[1], 0, 1))

def summed(former, latter):
    return (former[0] + latter[0], former[1] + latter[1])

def unit_step(which, sign):
    vector = [0, 0, 0, 0]
    vector[which] = sign
    return vector

def offset_list():
    result = [(0, 0, 0, 0)]
    for first in range(4):
        result.append(tuple(unit_step(first, 1)))
        result.append(tuple(unit_step(first, -1)))
        for second in range(4):
            if second != first:
                vector = unit_step(first, 1)
                vector[second] = -1
                result.append(tuple(vector))
    return result

def smeared_term(pieces, incoming, direction):

    def take(which, offset):
        block = pieces[str(tuple(offset))][which]
        return (block[:, :, 0], block[:, :, 1])
    anchor = [0, 0, 0, 0]
    ahead = unit_step(direction, 1)
    own = take(direction, anchor)
    staple = None
    for other in range(4):
        if other == direction:
            continue
        beside = unit_step(other, 1)
        behind = unit_step(other, -1)
        diagonal = [behind[k] + ahead[k] for k in range(4)]
        upper = product(product(take(other, anchor), take(direction, beside)), adjoint(take(other, ahead)))
        lower = product(product(adjoint(take(other, behind)), take(direction, behind)), take(other, diagonal))
        both = summed(upper, lower)
        staple = both if staple is None else summed(staple, both)
    staple = (smear_weight * staple[0], smear_weight * staple[1])
    omega = product(staple, adjoint(own))
    flipped = adjoint(omega)
    anti_real = 0.5 * (omega[0] - flipped[0])
    anti_imag = 0.5 * (omega[1] - flipped[1])
    identity = jnp.eye(3, dtype=jnp.float32)[:, :, None, None, None, None]
    trace_real = anti_real[0, 0] + anti_real[1, 1] + anti_real[2, 2]
    trace_imag = anti_imag[0, 0] + anti_imag[1, 1] + anti_imag[2, 2]
    anti = (anti_real - identity * trace_real / 3.0, anti_imag - identity * trace_imag / 3.0)
    result = (jnp.broadcast_to(identity, anti[0].shape), jnp.zeros_like(anti[1]))
    for order in range(6, 0, -1):
        stepped = product(anti, result)
        result = (identity + stepped[0] / order, stepped[1] / order)
    smeared = product(result, own)
    target = incoming[direction]
    return jnp.sum(target[:, :, 0] * smeared[0] + target[:, :, 1] * smeared[1])

def smear_loss(padded, incoming):
    region_x = padded.shape[4] - 2
    region_y = padded.shape[5] - 2
    slab = incoming.shape[6]
    depth = padded.shape[7]
    wrapped = jnp.concatenate([padded[..., depth - 1:], padded, padded[..., :1]], axis=7)
    pieces = {}
    for offset in offset_list():
        pieces[str(offset)] = wrapped[:, :, :, :, 1 + offset[0]:1 + offset[0] + region_x, 1 + offset[1]:1 + offset[1] + region_y, 1 + offset[3]:1 + offset[3] + slab, 1 + offset[2]:1 + offset[2] + depth]
    total = jnp.float32(0.0)
    for direction in range(4):
        total = total + jax.checkpoint(partial(smeared_term, direction=direction))(pieces, incoming)
    return total

def reference(links, incoming):
    slab = incoming.shape[6]

    def whole_loss(field):
        padded = jnp.pad(field, ((0, 0),) * 4 + ((1, 1), (1, 1)) + ((0, 0), (0, 0)), mode='wrap')
        return smear_loss(padded, incoming)
    grads = jax.grad(whole_loss)(links)
    return grads[:, :, :, :, :, :, 1:1 + slab]
```

```python
import jax
import jax.numpy as jnp
from jax import lax
from jax.experimental import pallas as pl
from jax.experimental.pallas import tpu as pltpu
from jax.sharding import PartitionSpec as P

smear_weight = 0.2
NC, NA = 18, 8
ROWS = 12
VM = 40 * 2**20
O, YP, YM, ZP, ZM, ZPYM, ZMYP = range(7)
buffer_of = {(0, 0): O, (1, 0): YP, (-1, 0): YM, (0, 1): ZP, (0, -1): ZM, (-1, 1): ZPYM, (1, -1): ZMYP}
base_dir = {ZPYM: 1, ZMYP: 2}
PAIRS = [(m, n) for m in range(4) for n in range(m + 1, 4)]
UPPER = [(0, 1), (0, 2), (1, 2)]


def total(terms):
    plus = [a * b for s, a, b in terms if s > 0]
    minus = [a * b for s, a, b in terms if s < 0]
    if not plus:
        value = -minus[0]
        minus = minus[1:]
    else:
        value = plus[0]
        for other in plus[1:]:
            value = value + other
    for other in minus:
        value = value - other
    return value


def entry(left, right, i, k, dag_left=False, dag_right=False, want=(True, True)):
    real, imag = [], []
    for j in range(3):
        ar, ai = left[j][i] if dag_left else left[i][j]
        br, bi = right[k][j] if dag_right else right[j][k]
        sa = -1 if dag_left else 1
        sb = -1 if dag_right else 1
        if ar is not None and br is not None:
            real.append((1, ar, br))
        if ai is not None and bi is not None:
            real.append((-sa * sb, ai, bi))
        if ar is not None and bi is not None:
            imag.append((sb, ar, bi))
        if ai is not None and br is not None:
            imag.append((sa, ai, br))
    return (total(real) if want[0] else None, total(imag) if want[1] else None)


def mm(left, right, dag_left=False, dag_right=False):
    return [[entry(left, right, i, k, dag_left, dag_right) for k in range(3)] for i in range(3)]


def madd(a, b):
    return [[(a[i][j][0] + b[i][j][0], a[i][j][1] + b[i][j][1]) for j in range(3)] for i in range(3)]


def msub(a, b):
    return [[(a[i][j][0] - b[i][j][0], a[i][j][1] - b[i][j][1]) for j in range(3)] for i in range(3)]


def skew(m):
    out = [m[i][i][1] + m[i][i][1] for i in range(3)]
    for i, j in UPPER:
        out += [m[i][j][0] - m[j][i][0], m[i][j][1] + m[j][i][1]]
    return out


def skew_product(left, right, dag_right=False):
    return skew(mm(left, right, False, dag_right))


def unpack8(v):
    return [v[0], v[1], -v[0] - v[1]] + list(v[2:])


def anti(v):
    out = [[None] * 3 for _ in range(3)]
    for i in range(3):
        out[i][i] = (None, v[i])
    for k, (i, j) in enumerate(UPPER):
        r, s = v[3 + 2 * k], v[4 + 2 * k]
        out[i][j] = (r, s)
        out[j][i] = (-r, s)
    return out


def carried(u, v):
    half = mm(u, anti(v))
    diag = [entry(half, u, i, i, False, True, (False, True))[1] for i in range(2)]
    out = [diag[0], diag[1], -diag[0] - diag[1]]
    for i, j in UPPER:
        out += list(entry(half, u, i, j, False, True))
    return out


def third_row(m):
    row = []
    for j in range(3):
        p, q = (j + 1) % 3, (j + 2) % 3
        ar, ai = m[0][p]
        br, bi = m[1][q]
        cr, ci = m[0][q]
        dr, di = m[1][p]
        row.append(
            (ar * br - ai * bi - cr * dr + ci * di, cr * di + ci * dr - ar * bi - ai * br)
        )
    return row


def comp(d, i, j, ri):
    return ((d * 3 + i) * 3 + j) * 2 + ri


def place(c, xe):
    return (c * 4 + xe) * ROWS


def load_matrix(read):
    return [[(read(i, j, 0), read(i, j, 1)) for j in range(3)] for i in range(3)]


def pack_y_body(links, up, down):
    for d in range(4):
        for q in range(12):
            c = d * 18 + q
            for x in range(2):
                base = (c * 2 + x) * ROWS
                to = pl.ds(((d * 12 + q) * 2 + x) * 4, 4)
                up[to, :] = links[pl.ds(base + 3, 4, stride=2), :]
                down[to, :] = links[pl.ds(base + 2, 4, stride=2), :]
    for q in range(12):
        for x in range(2):
            to = pl.ds(384 + q * 2 + x, 1)
            up[to, :] = links[pl.ds(((18 + q) * 2 + x) * ROWS + 11, 1), :]
            down[to, :] = links[pl.ds(((54 + q) * 2 + x) * ROWS, 1), :]


def pack_x_body(links, ynext, yprev, up, down):
    for d in range(4):
        for q in range(12):
            c = d * 18 + q
            to = pl.ds((d * 12 + q) * 8, 8)
            up[to, :] = links[pl.ds((c * 2 + 1) * ROWS + 2, 8), :]
            down[to, :] = links[pl.ds(c * 2 * ROWS + 2, 8), :]
    for q in range(12):
        at = 384 + q * 6
        up[pl.ds(at, 2), :] = links[pl.ds((q * 2 + 1) * ROWS + 10, 2), :]
        down[pl.ds(at, 2), :] = links[pl.ds((54 + q) * 2 * ROWS, 2), :]
        up[pl.ds(at + 2, 4), :] = ynext[pl.ds(q * 8 + 4, 4), :]
        down[pl.ds(at + 2, 4), :] = yprev[pl.ds((12 + q) * 8, 4), :]


def two_rows(read):
    m = [[(read((i * 3 + j) * 2), read((i * 3 + j) * 2 + 1)) for j in range(3)] for i in range(2)]
    return m + [third_row(m)]


def put(write, m):
    for i in range(3):
        for j in range(3):
            for ri in range(2):
                write((i * 3 + j) * 2 + ri, m[i][j][ri])


def roll_z(v, by):
    return pltpu.roll(v, (128 - by) % 128, 1)


def fill_y(bufs, n, dirs_p, dirs_m):
    for x in (1, 2):
        for d in range(4):
            for k in range(n):
                at = place(d * n + k, x)
                if d in dirs_p:
                    bufs[YP][pl.ds(at, 6, stride=2), :] = bufs[O][pl.ds(at + 1, 6, stride=2), :]
                if d in dirs_m:
                    bufs[YM][pl.ds(at + 1, 6, stride=2), :] = bufs[O][pl.ds(at, 6, stride=2), :]


def fill_z(bufs, n):
    for d in range(4):
        for k in range(n):
            c = d * n + k
            for x in (1, 2):
                at = place(c, x)
                zp, zm = bufs[ZP], bufs[ZM]
                if d != 2:
                    zp[pl.ds(at + 2, 8), :] = roll_z(bufs[O][pl.ds(at + 2, 8), :], 1)
                if d == 3:
                    zp[pl.ds(at, 2), :] = roll_z(bufs[O][pl.ds(at, 2), :], 1)
                zm[pl.ds(at + 2, 8), :] = roll_z(bufs[O][pl.ds(at + 2, 8), :], -1)
                if d == 2:
                    zm[pl.ds(at + 10, 2), :] = roll_z(bufs[O][pl.ds(at + 10, 2), :], -1)


def fill_mixed(bufs, n):
    for k in range(n):
        for x in (1, 2):
            bufs[ZPYM][pl.ds(place(k, x) + 2, 8), :] = roll_z(bufs[YM][pl.ds(place(n + k, x) + 2, 8), :], 1)
            bufs[ZMYP][pl.ds(place(k, x) + 2, 8), :] = roll_z(bufs[YP][pl.ds(place(2 * n + k, x) + 2, 8), :], -1)


def fill_edges(bufs, n):
    for k in range(n):
        low, high = place(k, 0), place(2 * n + k, 3)
        bufs[ZP][pl.ds(low + 2, 8), :] = roll_z(bufs[O][pl.ds(low + 2, 8), :], 1)
        bufs[ZM][pl.ds(high + 2, 8), :] = roll_z(bufs[O][pl.ds(high + 2, 8), :], -1)
        bufs[YP][pl.ds(low + 2, 4, stride=2), :] = bufs[O][pl.ds(low + 3, 4, stride=2), :]
        side = place(n + k, 3)
        bufs[YM][pl.ds(side + 3, 4, stride=2), :] = bufs[O][pl.ds(side + 2, 4, stride=2), :]


def fill_links_local(links, bufs):
    for c in range(72):
        for x in range(2):
            source, to = (c * 2 + x) * ROWS, place(c, x + 1)
            bufs[O][pl.ds(to, 8), :] = links[pl.ds(source, 8), :]
            bufs[O][pl.ds(to + 8, 4), :] = links[pl.ds(source + 8, 4), :]
    fill_y(bufs, NC, (0, 2, 3), (0, 1, 2, 3))
    fill_z(bufs, NC)


def fill_links_y(ynext, yprev, bufs):
    for d in range(4):
        for source, buf, off in ((ynext, YP, 3), (yprev, YM, 2)):
            if buf == YP and d == 1:
                continue
            m = two_rows(lambda q: source[pl.ds((d * 12 + q) * 8, 8), :])

            def write(q, v):
                for x in range(2):
                    bufs[buf][pl.ds(place(d * NC + q, x + 1) + off, 4, stride=2), :] = v[4 * x : 4 * x + 4]

            put(write, m)
    for source, buf, d, row in ((ynext, YP, 3, 1), (yprev, YM, 1, 10)):
        m = two_rows(lambda q: source[pl.ds(384 + q * 2, 2), :])

        def write_row(q, v):
            for x in range(2):
                bufs[buf][pl.ds(place(d * NC + q, x + 1) + row, 1), :] = v[x : x + 1]

        put(write_row, m)
    fill_mixed(bufs, NC)


def fill_links_x(xnext, xprev, bufs):
    for d in range(4):
        for source, xe in ((xnext, 3), (xprev, 0)):
            if xe == 3 and d == 0:
                continue
            m = two_rows(lambda q: source[pl.ds((d * 12 + q) * 8, 8), :])

            def write(q, v):
                bufs[O][pl.ds(place(d * NC + q, xe) + 2, 8), :] = v

            put(write, m)
    for source, d, xe, row, buf, cd, off in ((xnext, 3, 3, 0, YM, 1, 2), (xprev, 0, 0, 10, YP, 0, 3)):
        m = two_rows(lambda q: source[pl.ds(384 + q * 6, 2), :])

        def write_edge(q, v):
            bufs[O][pl.ds(place(d * NC + q, xe) + row, 2), :] = v

        put(write_edge, m)
        m = two_rows(lambda q: source[pl.ds(384 + q * 6 + 2, 4), :])

        def write_corner(q, v):
            bufs[buf][pl.ds(place(cd * NC + q, xe) + off, 4, stride=2), :] = v

        put(write_corner, m)
    fill_edges(bufs, NC)


def fill_lambda_local(lam, bufs):
    zero = jnp.zeros((2, 128), jnp.float32)
    for c in range(32):
        for x in range(2):
            to = place(c, x + 1)
            bufs[O][pl.ds(to + 2, 8), :] = lam[pl.ds((c * 2 + x) * 8, 8), :]
            bufs[O][pl.ds(to, 2), :] = zero
            bufs[O][pl.ds(to + 10, 2), :] = zero
    fill_y(bufs, NA, (0, 2, 3), (0, 1, 2, 3))
    fill_z(bufs, NA)


def fill_lambda_y(ynext, yprev, bufs):
    zero = jnp.zeros((1, 128), jnp.float32)
    for d in range(4):
        for k in range(NA):
            for x in range(2):
                source = pl.ds((d * NA + k) * 8 + x * 4, 4)
                to = place(d * NA + k, x + 1)
                bufs[YP][pl.ds(to + 3, 4, stride=2), :] = ynext[source, :]
                bufs[YM][pl.ds(to + 2, 4, stride=2), :] = yprev[source, :]
                if d == 3:
                    bufs[YP][pl.ds(to + 1, 1), :] = zero
                if d == 1:
                    bufs[YM][pl.ds(to + 10, 1), :] = zero
    fill_mixed(bufs, NA)


def fill_lambda_x(xnext, xprev, bufs):
    zero = jnp.zeros((2, 128), jnp.float32)
    for d in range(4):
        for k in range(NA):
            source = pl.ds((d * NA + k) * 8, 8)
            high, low = place(d * NA + k, 3), place(d * NA + k, 0)
            bufs[O][pl.ds(high + 2, 8), :] = xnext[source, :]
            bufs[O][pl.ds(low + 2, 8), :] = xprev[source, :]
            if d == 3:
                bufs[O][pl.ds(high, 2), :] = zero
            if d == 0:
                bufs[O][pl.ds(low + 10, 2), :] = zero
    for k in range(NA):
        corner = pl.ds(256 + k * 4, 4)
        bufs[YM][pl.ds(place(NA + k, 3) + 2, 4, stride=2), :] = xnext[corner, :]
        bufs[YP][pl.ds(place(k, 0) + 3, 4, stride=2), :] = xprev[corner, :]
    fill_edges(bufs, NA)


def step(*signed):
    vector = [0, 0, 0, 0]
    for which, sign in signed:
        vector[which] += sign
    return vector


def where(bufs, n, d, offset, x):
    key = buffer_of[(offset[1], offset[2])]
    row = 2 + 2 * offset[3]
    dd = d - base_dir.get(key, 0)
    shift = (x + 1 + offset[0]) * ROWS

    def read(k):
        return bufs[key][pl.ds(place(dd * n + k, 0) + row + shift, 8), :]

    return read


def link(bufs, d, offset, x):
    read = where(bufs, NC, d, offset, x)
    return load_matrix(lambda i, j, ri: read((i * 3 + j) * 2 + ri))


def lam_at(bufs, d, offset, x):
    read = where(bufs, NA, d, offset, x)
    return unpack8([read(k) for k in range(NA)])


def exponent_force(v, u, target, clow):
    a = v[:3]
    off = [(v[3 + 2 * k], v[4 + 2 * k]) for k in range(3)]
    norm = [r * r + s * s for r, s in off]
    sd = [
        -(a[0] * a[0] + norm[0] + norm[1]),
        -(a[1] * a[1] + norm[0] + norm[2]),
        -(a[2] * a[2] + norm[1] + norm[2]),
    ]
    (r0, s0), (r1, s1), (r2, s2) = off
    so = [
        (a[2] * s0 - (r1 * r2 + s1 * s2), -a[2] * r0 - (s1 * r2 - r1 * s2)),
        (a[1] * s1 + (r0 * r2 - s0 * s2), -a[1] * r1 + (r0 * s2 + s0 * r2)),
        (a[0] * s2 - (r0 * r1 + s0 * s1), -a[0] * r2 - (r0 * s1 - s0 * r1)),
    ]
    c = 0.5 * (sd[0] + sd[1] + sd[2])
    cross = [off[k][1] * so[k][0] - off[k][0] * so[k][1] for k in range(3)]
    dd = (a[0] * sd[0] + a[1] * sd[1] + a[2] * sd[2] + 2.0 * (cross[0] + cross[1] + cross[2])) * (1.0 / 3.0)
    p0r = 1.0 - dd * dd * (1.0 / 720.0)
    p0i = dd * (1.0 / 6.0 + c * (1.0 / 120.0))
    p1r = 1.0 + c * (1.0 / 6.0 + c * (1.0 / 120.0))
    p1i = dd * (1.0 / 24.0 + c * (1.0 / 360.0))
    p2r = 0.5 + c * (1.0 / 24.0 + c * (1.0 / 720.0))
    p2i = dd * (1.0 / 120.0)
    m = mm(target, u, False, True)
    hd = [m[i][i][0] for i in range(3)]
    kd = [m[i][i][1] for i in range(3)]
    ho = [(0.5 * (m[i][j][0] + m[j][i][0]), 0.5 * (m[i][j][1] - m[j][i][1])) for i, j in UPPER]
    ko = [(0.5 * (m[i][j][0] - m[j][i][0]), 0.5 * (m[i][j][1] + m[j][i][1])) for i, j in UPPER]
    t0r = hd[0] + hd[1] + hd[2]
    t0i = -(kd[0] + kd[1] + kd[2])

    def dots(x, y, xo, yo):
        diag = x[0] * y[0] + x[1] * y[1] + x[2] * y[2]
        rest = [xo[k][0] * yo[k][0] + xo[k][1] * yo[k][1] for k in range(3)]
        return diag + 2.0 * (rest[0] + rest[1] + rest[2])

    def crossed(x, y, xo, yo):
        diag = x[0] * y[0] + x[1] * y[1] + x[2] * y[2]
        rest = [yo[k][1] * xo[k][0] - yo[k][0] * xo[k][1] for k in range(3)]
        return diag + 2.0 * (rest[0] + rest[1] + rest[2])

    t1r = dots(kd, a, ko, off)
    t1i = crossed(hd, a, ho, off)
    t2r = dots(hd, sd, ho, so)
    t2i = -crossed(sd, kd, so, ko)
    by_c = (
        t1r * (1.0 / 6.0 + c * (1.0 / 60.0))
        + t2r * (1.0 / 24.0 + c * (1.0 / 360.0))
        - dd * (t0i * (1.0 / 120.0) + t1i * (1.0 / 360.0))
    )
    by_d = -(
        dd * t0r * (1.0 / 360.0)
        + t0i * (1.0 / 6.0 + c * (1.0 / 120.0))
        + t1i * (1.0 / 24.0 + c * (1.0 / 360.0))
        + t2i * (1.0 / 120.0)
    )
    herm = [[None] * 3 for _ in range(3)]
    for i in range(3):
        herm[i][i] = (-(p2r * hd[i] + p2i * kd[i]), None)
    for k, (i, j) in enumerate(UPPER):
        re = -(p2r * ho[k][0] + p2i * ko[k][1])
        im = p2i * ko[k][0] - p2r * ho[k][1]
        herm[i][j] = (re, im)
        herm[j][i] = (re, -im)
    amat = anti(v)
    g = skew(mm(amat, herm))
    lam = [p1r * kd[i] - p1i * hd[i] + g[i] - by_c * a[i] + by_d * sd[i] for i in range(3)]
    for k in range(3):
        lam.append(p1r * ko[k][0] + p1i * ho[k][1] + g[3 + 2 * k] - by_c * off[k][0] - by_d * so[k][1])
        lam.append(p1r * ko[k][1] - p1i * ho[k][0] + g[4 + 2 * k] - by_c * off[k][1] + by_d * so[k][0])
    mean = (lam[0] + lam[1] + lam[2]) * (1.0 / 3.0)
    lam = [smear_weight * (lam[i] - mean) for i in range(3)] + [smear_weight * lam[k] for k in range(3, 9)]
    edag = [[None] * 3 for _ in range(3)]
    for i in range(3):
        edag[i][i] = (p0r - p1i * a[i] + p2r * sd[i], -(p0i + p1r * a[i] + p2i * sd[i]))
    for k, (i, j) in enumerate(UPPER):
        r, s = off[k]
        sr, si = so[k]
        edag[i][j] = (
            (p2r * sr - p1i * s) + (p2i * si - p1r * r),
            (p1i * r - p2i * sr) + (p2r * si - p1r * s),
        )
        edag[j][i] = (
            (p2r * sr - p1i * s) - (p2i * si - p1r * r),
            -(p1i * r + p2i * sr) - (p2r * si + p1r * s),
        )
    direct = msub(mm(edag, target), mm(anti(lam), clow))
    return lam, direct


def take_incoming(incoming, inner):
    for c in range(144):
        inner[pl.ds(c * 8, 4, stride=2), :] = incoming[pl.ds(c * 8, 4), :]
        inner[pl.ds(c * 8 + 1, 4, stride=2), :] = incoming[pl.ds(c * 8 + 4, 4), :]


def forward(bufs, inner, loops, omega, lam_out, direct, x):
    here = [0, 0, 0, 0]
    for p, (m, n) in enumerate(PAIRS):
        a, d = link(bufs, m, here, x), link(bufs, n, here, x)
        b, c = link(bufs, n, step((m, 1)), x), link(bufs, m, step((n, 1)), x)
        loop = mm(mm(a, b), mm(d, c), False, True)
        for i in range(3):
            for j in range(3):
                for ri in range(2):
                    omega[pl.ds(((p * 18 + (i * 3 + j) * 2 + ri) * 2 + x) * 8, 8), :] = loop[i][j][ri]
        for k, v in enumerate(skew(loop)):
            loops[pl.ds((p * 9 + k) * 8, 8), :] = v
    for m in range(4):
        low = None
        for n in range(4):
            if n == m:
                continue
            e, g = link(bufs, n, step((n, -1)), x), link(bufs, m, step((n, -1)), x)
            h = link(bufs, n, step((n, -1), (m, 1)), x)
            term = mm(mm(e, g, True, False), h)
            low = term if low is None else madd(low, term)
        u = link(bufs, m, here, x)
        v = skew_product(low, u, True)
        for p, (f, s) in enumerate(PAIRS):
            if m == f:
                v = [v[k] - loops[pl.ds((p * 9 + k) * 8, 8), :] for k in range(9)]
            if m == s:
                v = [v[k] + loops[pl.ds((p * 9 + k) * 8, 8), :] for k in range(9)]
        mean = (v[0] + v[1] + v[2]) * (1.0 / 3.0)
        v = [(0.5 * smear_weight) * (v[k] - mean) for k in range(3)] + [
            (0.5 * smear_weight) * v[k] for k in range(3, 9)
        ]
        target = load_matrix(lambda i, j, ri: inner[pl.ds((comp(m, i, j, ri) * 2 + x) * 8, 8), :])
        lam, force = exponent_force(v, u, target, low)
        for k, v in enumerate(lam[:2] + lam[3:]):
            lam_out[pl.ds(((m * NA + k) * 2 + x) * 8, 8), :] = v
        for i in range(3):
            for j in range(3):
                for ri in range(2):
                    direct[pl.ds((comp(m, i, j, ri) * 2 + x) * 8, 8), :] = force[i][j][ri]


def pack_lambda_y(lam, up, down):
    for c in range(32):
        for x in range(2):
            to = pl.ds(c * 8 + x * 4, 4)
            up[to, :] = lam[pl.ds((c * 2 + x) * 8 + 1, 4, stride=2), :]
            down[to, :] = lam[pl.ds((c * 2 + x) * 8, 4, stride=2), :]


def forward_body(*refs):
    links, incoming, ynext, yprev, xnext, xprev = refs[:6]
    bufs, (omega, lam, direct, up, down) = refs[6:13], refs[13:18]
    loops, inner = refs[18:]
    fill_links_local(links, bufs)
    fill_links_y(ynext, yprev, bufs)
    fill_links_x(xnext, xprev, bufs)
    take_incoming(incoming, inner)

    @pl.loop(0, 2)
    def _(x):
        forward(bufs, inner, loops, omega, lam, direct, x)

    pack_lambda_y(lam, up, down)


def pack_lambda_x_body(lam, ynext, yprev, up, down):
    for c in range(32):
        to = pl.ds(c * 8, 8)
        up[to, :] = lam[pl.ds((c * 2 + 1) * 8, 8), :]
        down[to, :] = lam[pl.ds(c * 16, 8), :]
    for k in range(NA):
        to = pl.ds(256 + k * 4, 4)
        up[to, :] = ynext[pl.ds(k * 8 + 4, 4), :]
        down[to, :] = yprev[pl.ds((NA + k) * 8, 4), :]


def backward(bufs, lams, omega, direct, sums, result, x):
    here = [0, 0, 0, 0]
    started = set()

    def gather(d, m):
        for i in range(3):
            for j in range(3):
                for ri in range(2):
                    at = pl.ds(comp(d, i, j, ri) * 8, 8)
                    sums[at, :] = sums[at, :] + m[i][j][ri] if d in started else m[i][j][ri]
        started.add(d)

    for p, (m, n) in enumerate(PAIRS):
        la, ld = lam_at(lams, m, here, x), lam_at(lams, n, here, x)
        lb = carried(link(bufs, m, here, x), lam_at(lams, n, step((m, 1)), x))
        lc = carried(link(bufs, n, here, x), lam_at(lams, m, step((n, 1)), x))
        loop = load_matrix(
            lambda i, j, ri: omega[pl.ds(((p * 18 + (i * 3 + j) * 2 + ri) * 2 + x) * 8, 8), :]
        )
        z = [ld[k] - la[k] for k in range(9)]
        first = anti([z[k] + lc[k] for k in range(9)])
        second = anti([lb[k] - z[k] for k in range(9)])
        gather(m, msub(mm(first, loop, False, True), mm(loop, anti(lb), True, False)))
        gather(n, msub(mm(second, loop), mm(loop, anti(lc))))
    for m in range(4):
        f = load_matrix(lambda i, j, ri: sums[pl.ds(comp(m, i, j, ri) * 8, 8), :])
        force = mm(f, link(bufs, m, here, x))
        for n in range(4):
            if n == m:
                continue
            back = step((n, -1))
            e, g, h = link(bufs, n, back, x), link(bufs, m, back, x), link(bufs, n, step((n, -1), (m, 1)), x)
            le, lg, lh = (
                lam_at(lams, n, back, x),
                lam_at(lams, m, back, x),
                lam_at(lams, n, step((n, -1), (m, 1)), x),
            )
            inside = madd(mm(anti([lg[k] - le[k] for k in range(9)]), g), mm(g, anti(lh)))
            force = madd(force, mm(mm(e, inside, True, False), h))
        for i in range(3):
            for j in range(3):
                for ri in range(2):
                    at = pl.ds((comp(m, i, j, ri) * 2 + x) * 8, 8)
                    result[at, :] = force[i][j][ri] + direct[at, :]


def give_force(result, out):
    for c in range(144):
        out[pl.ds(c * 8, 4), :] = result[pl.ds(c * 8, 4, stride=2), :]
        out[pl.ds(c * 8 + 4, 4), :] = result[pl.ds(c * 8 + 1, 4, stride=2), :]


def backward_body(*refs):
    bufs, (omega, lam, direct, ynext, yprev, xnext, xprev, out) = refs[:7], refs[7:15]
    lams, (sums, result) = refs[15:22], refs[22:]
    fill_lambda_local(lam, lams)
    fill_lambda_y(ynext, yprev, lams)
    fill_lambda_x(xnext, xprev, lams)

    @pl.loop(0, 2)
    def _(x):
        backward(bufs, lams, omega, direct, sums, result, x)

    give_force(result, out)


def rows(n):
    return jax.ShapeDtypeStruct((n, 128), jnp.float32)


def buffer_rows(n):
    return [(n if key in base_dir else 4 * n) * 4 * ROWS for key in range(7)]


def call(body, outs, args, scratch=()):
    return pl.pallas_call(
        body,
        out_shape=tuple(rows(n) for n in outs),
        in_specs=[pl.BlockSpec(memory_space=pltpu.VMEM)] * len(args),
        out_specs=(pl.BlockSpec(memory_space=pltpu.VMEM),) * len(outs),
        scratch_shapes=[pltpu.VMEM((n, 128), jnp.float32) for n in scratch],
        compiler_params=pltpu.CompilerParams(vmem_limit_bytes=VM),
    )(*args)


def shifted(shard, axis, by):
    length = lax.axis_size(axis)
    return lax.ppermute(shard, axis, [(i, (i + by) % length) for i in range(length)])


def body(links, incoming):
    links = jnp.transpose(links, (0, 1, 2, 3, 4, 6, 5, 7)).reshape(144 * ROWS, 128)
    shape = incoming.shape
    incoming = incoming.reshape(1152, 128)
    up, down = call(pack_y_body, (408, 408), (links,))
    yprev, ynext = shifted(up, "gy", 1), shifted(down, "gy", -1)
    up, down = call(pack_x_body, (456, 456), (links, ynext, yprev))
    xprev, xnext = shifted(up, "gx", 1), shifted(down, "gx", -1)
    *kept, up, down = call(
        forward_body,
        buffer_rows(NC) + [6 * 18 * 16, 32 * 16, 1152, 256, 256],
        (links, incoming, ynext, yprev, xnext, xprev),
        (54 * 8, 1152),
    )
    yprev, ynext = shifted(up, "gy", 1), shifted(down, "gy", -1)
    up, down = call(pack_lambda_x_body, (288, 288), (kept[8], ynext, yprev))
    xprev, xnext = shifted(up, "gx", 1), shifted(down, "gx", -1)
    (out,) = call(
        backward_body,
        (1152,),
        (*kept, ynext, yprev, xnext, xprev),
        buffer_rows(NA) + [72 * 8, 1152],
    )
    return out.reshape(shape)


def solution(mesh):
    placed = P(None, None, None, None, "gx", "gy", None, None)
    return jax.shard_map(body, mesh=mesh, in_specs=(placed, placed), out_specs=placed, check_vma=False)
```

```python
import jax
import jax.numpy as jnp
from jax import lax
from jax.experimental import pallas as pl
from jax.experimental.pallas import tpu as pltpu
from jax.sharding import PartitionSpec as P

smear_weight = 0.2
NC, NA = 18, 8
ROWS = 12
VM = 40 * 2**20
O, YP, YM, ZP, ZM, ZPYM, ZMYP = range(7)
buffer_of = {(0, 0): O, (1, 0): YP, (-1, 0): YM, (0, 1): ZP, (0, -1): ZM, (-1, 1): ZPYM, (1, -1): ZMYP}
base_dir = {ZPYM: 1, ZMYP: 2}
PAIRS = [(m, n) for m in range(4) for n in range(m + 1, 4)]
DOWN_Y = [0, 2, 3]
UPPER = [(0, 1), (0, 2), (1, 2)]


def total(terms):
    plus = [a * b for s, a, b in terms if s > 0]
    minus = [a * b for s, a, b in terms if s < 0]
    if not plus:
        value = -minus[0]
        minus = minus[1:]
    else:
        value = plus[0]
        for other in plus[1:]:
            value = value + other
    for other in minus:
        value = value - other
    return value


def entry(left, right, i, k, dag_left=False, dag_right=False, want=(True, True)):
    real, imag = [], []
    for j in range(3):
        ar, ai = left[j][i] if dag_left else left[i][j]
        br, bi = right[k][j] if dag_right else right[j][k]
        sa = -1 if dag_left else 1
        sb = -1 if dag_right else 1
        if ar is not None and br is not None:
            real.append((1, ar, br))
        if ai is not None and bi is not None:
            real.append((-sa * sb, ai, bi))
        if ar is not None and bi is not None:
            imag.append((sb, ar, bi))
        if ai is not None and br is not None:
            imag.append((sa, ai, br))
    return (total(real) if want[0] else None, total(imag) if want[1] else None)


def mm(left, right, dag_left=False, dag_right=False):
    return [[entry(left, right, i, k, dag_left, dag_right) for k in range(3)] for i in range(3)]


def madd(a, b):
    return [[(a[i][j][0] + b[i][j][0], a[i][j][1] + b[i][j][1]) for j in range(3)] for i in range(3)]


def msub(a, b):
    return [[(a[i][j][0] - b[i][j][0], a[i][j][1] - b[i][j][1]) for j in range(3)] for i in range(3)]


def skew(m):
    out = [m[i][i][1] + m[i][i][1] for i in range(3)]
    for i, j in UPPER:
        out += [m[i][j][0] - m[j][i][0], m[i][j][1] + m[j][i][1]]
    return out


def skew_product(left, right, dag_right=False):
    return skew(mm(left, right, False, dag_right))


def unpack8(v):
    return [v[0], v[1], -v[0] - v[1]] + list(v[2:])


def anti(v):
    out = [[None] * 3 for _ in range(3)]
    for i in range(3):
        out[i][i] = (None, v[i])
    for k, (i, j) in enumerate(UPPER):
        r, s = v[3 + 2 * k], v[4 + 2 * k]
        out[i][j] = (r, s)
        out[j][i] = (-r, s)
    return out


def carried(u, v):
    half = mm(u, anti(v))
    diag = [entry(half, u, i, i, False, True, (False, True))[1] for i in range(2)]
    out = [diag[0], diag[1], -diag[0] - diag[1]]
    for i, j in UPPER:
        out += list(entry(half, u, i, j, False, True))
    return out


def third_row(m):
    row = []
    for j in range(3):
        p, q = (j + 1) % 3, (j + 2) % 3
        ar, ai = m[0][p]
        br, bi = m[1][q]
        cr, ci = m[0][q]
        dr, di = m[1][p]
        row.append(
            (ar * br - ai * bi - cr * dr + ci * di, cr * di + ci * dr - ar * bi - ai * br)
        )
    return row


def comp(d, i, j, ri):
    return ((d * 3 + i) * 3 + j) * 2 + ri


def place(c, xe):
    return (c * 4 + xe) * ROWS


def load_matrix(read):
    return [[(read(i, j, 0), read(i, j, 1)) for j in range(3)] for i in range(3)]


def pack_y(up, down, n, read_up, read_down):
    for d in range(4):
        for q in range(n):
            for x in range(2):
                up[pl.ds(((d * n + q) * 2 + x) * 4, 4), :] = read_up(d, q, x)
                if d != 1:
                    down[pl.ds(((DOWN_Y.index(d) * n + q) * 2 + x) * 4, 4), :] = read_down(d, q, x)


def pack_first_body(links, yup, ydown, xdown, corner):
    def reader(row):
        return lambda d, q, x: links[pl.ds(((d * 18 + q) * 2 + x) * ROWS + row, 4, stride=2), :]

    pack_y(yup, ydown, 12, reader(3), reader(2))
    for q in range(12):
        for x in range(2):
            yup[pl.ds(384 + q * 2 + x, 1), :] = links[pl.ds(((18 + q) * 2 + x) * ROWS + 11, 1), :]
            ydown[pl.ds(288 + q * 2 + x, 1), :] = links[pl.ds(((54 + q) * 2 + x) * ROWS, 1), :]
        for d in range(1, 4):
            xdown[pl.ds(((d - 1) * 12 + q) * 8, 8), :] = links[pl.ds((d * 18 + q) * 2 * ROWS + 2, 8), :]
        xdown[pl.ds(288 + q * 2, 2), :] = links[pl.ds((54 + q) * 2 * ROWS, 2), :]
        corner[pl.ds(q * 4, 4), :] = links[pl.ds((18 + q) * 2 * ROWS + 3, 4, stride=2), :]


def pack_x_body(links, ynext, up):
    for q in range(12):
        for d in range(4):
            up[pl.ds((d * 12 + q) * 8, 8), :] = links[pl.ds(((d * 18 + q) * 2 + 1) * ROWS + 2, 8), :]
        up[pl.ds(384 + q * 2, 2), :] = links[pl.ds((q * 2 + 1) * ROWS + 10, 2), :]
        up[pl.ds(408 + q * 4, 4), :] = ynext[pl.ds(q * 8 + 4, 4), :]


def pack_lambda_x_body(lam, ynext, yprev, up, down):
    for c in range(32):
        up[pl.ds(c * 8, 8), :] = lam[pl.ds((c * 2 + 1) * 8, 8), :]
        if c >= NA:
            down[pl.ds((c - NA) * 8, 8), :] = lam[pl.ds(c * 16, 8), :]
    for k in range(NA):
        up[pl.ds(256 + k * 4, 4), :] = ynext[pl.ds(k * 8 + 4, 4), :]
        down[pl.ds(192 + k * 4, 4), :] = yprev[pl.ds((NA + k) * 8, 4), :]


def two_rows(read):
    m = [[(read((i * 3 + j) * 2), read((i * 3 + j) * 2 + 1)) for j in range(3)] for i in range(2)]
    return m + [third_row(m)]


def put(write, m):
    for i in range(3):
        for j in range(3):
            for ri in range(2):
                write((i * 3 + j) * 2 + ri, m[i][j][ri])


def roll_z(v, by):
    return pltpu.roll(v, (128 - by) % 128, 1)


def fill_y(bufs, n, dirs_p, dirs_m):
    for x in (1, 2):
        for d in range(4):
            for k in range(n):
                at = place(d * n + k, x)
                if d in dirs_p:
                    bufs[YP][pl.ds(at, 6, stride=2), :] = bufs[O][pl.ds(at + 1, 6, stride=2), :]
                if d in dirs_m:
                    bufs[YM][pl.ds(at + 1, 6, stride=2), :] = bufs[O][pl.ds(at, 6, stride=2), :]


def fill_z(bufs, n):
    for d in range(4):
        for k in range(n):
            c = d * n + k
            for x in (1, 2):
                at = place(c, x)
                zp, zm = bufs[ZP], bufs[ZM]
                if d != 2:
                    zp[pl.ds(at + 2, 8), :] = roll_z(bufs[O][pl.ds(at + 2, 8), :], 1)
                if d == 3:
                    zp[pl.ds(at, 2), :] = roll_z(bufs[O][pl.ds(at, 2), :], 1)
                zm[pl.ds(at + 2, 8), :] = roll_z(bufs[O][pl.ds(at + 2, 8), :], -1)
                if d == 2:
                    zm[pl.ds(at + 10, 2), :] = roll_z(bufs[O][pl.ds(at + 10, 2), :], -1)


def fill_mixed(bufs, n):
    for k in range(n):
        for x in (1, 2):
            bufs[ZPYM][pl.ds(place(k, x) + 2, 8), :] = roll_z(bufs[YM][pl.ds(place(n + k, x) + 2, 8), :], 1)
            bufs[ZMYP][pl.ds(place(k, x) + 2, 8), :] = roll_z(bufs[YP][pl.ds(place(2 * n + k, x) + 2, 8), :], -1)


def fill_edges(bufs, n):
    for k in range(n):
        low, high = place(k, 0), place(2 * n + k, 3)
        bufs[ZP][pl.ds(low + 2, 8), :] = roll_z(bufs[O][pl.ds(low + 2, 8), :], 1)
        bufs[ZM][pl.ds(high + 2, 8), :] = roll_z(bufs[O][pl.ds(high + 2, 8), :], -1)
        bufs[YP][pl.ds(low + 2, 4, stride=2), :] = bufs[O][pl.ds(low + 3, 4, stride=2), :]
        side = place(n + k, 3)
        bufs[YM][pl.ds(side + 3, 4, stride=2), :] = bufs[O][pl.ds(side + 2, 4, stride=2), :]


def fill_links_local(links, bufs):
    for c in range(72):
        for x in range(2):
            source, to = (c * 2 + x) * ROWS, place(c, x + 1)
            bufs[O][pl.ds(to, 8), :] = links[pl.ds(source, 8), :]
            bufs[O][pl.ds(to + 8, 4), :] = links[pl.ds(source + 8, 4), :]
    fill_y(bufs, NC, (0, 2, 3), (0, 1, 2, 3))
    fill_z(bufs, NC)


def fill_links_y(ynext, yprev, bufs):
    for d in range(4):
        for source, buf, off in ((ynext, YP, 3), (yprev, YM, 2)):
            if buf == YP and d == 1:
                continue
            slot = DOWN_Y.index(d) if buf == YP else d
            m = two_rows(lambda q: source[pl.ds((slot * 12 + q) * 8, 8), :])

            def write(q, v):
                for x in range(2):
                    bufs[buf][pl.ds(place(d * NC + q, x + 1) + off, 4, stride=2), :] = v[4 * x : 4 * x + 4]

            put(write, m)
    for source, buf, d, row, at in ((ynext, YP, 3, 1, 288), (yprev, YM, 1, 10, 384)):
        m = two_rows(lambda q: source[pl.ds(at + q * 2, 2), :])

        def write_row(q, v):
            for x in range(2):
                bufs[buf][pl.ds(place(d * NC + q, x + 1) + row, 1), :] = v[x : x + 1]

        put(write_row, m)
    fill_mixed(bufs, NC)


def fill_links_x(xnext, corner, xprev, bufs):
    for d in range(4):
        for source, xe in ((xnext, 3), (xprev, 0)):
            if xe == 3 and d == 0:
                continue
            slot = d - 1 if xe == 3 else d
            m = two_rows(lambda q: source[pl.ds((slot * 12 + q) * 8, 8), :])

            def write(q, v):
                bufs[O][pl.ds(place(d * NC + q, xe) + 2, 8), :] = v

            put(write, m)
    for source, d, xe, row, at in ((xnext, 3, 3, 0, 288), (xprev, 0, 0, 10, 384)):
        m = two_rows(lambda q: source[pl.ds(at + q * 2, 2), :])

        def write_edge(q, v):
            bufs[O][pl.ds(place(d * NC + q, xe) + row, 2), :] = v

        put(write_edge, m)
    for source, at, buf, d, xe, off in ((corner, 0, YM, 1, 3, 2), (xprev, 408, YP, 0, 0, 3)):
        m = two_rows(lambda q: source[pl.ds(at + q * 4, 4), :])

        def write_corner(q, v):
            bufs[buf][pl.ds(place(d * NC + q, xe) + off, 4, stride=2), :] = v

        put(write_corner, m)
    fill_edges(bufs, NC)


def fill_lambda_local(lam, bufs):
    zero = jnp.zeros((2, 128), jnp.float32)
    for c in range(32):
        for x in range(2):
            to = place(c, x + 1)
            bufs[O][pl.ds(to + 2, 8), :] = lam[pl.ds((c * 2 + x) * 8, 8), :]
            bufs[O][pl.ds(to, 2), :] = zero
            bufs[O][pl.ds(to + 10, 2), :] = zero
    fill_y(bufs, NA, (0, 2, 3), (0, 1, 2, 3))
    fill_z(bufs, NA)


def fill_lambda_y(ynext, yprev, bufs):
    zero = jnp.zeros((1, 128), jnp.float32)
    for d in range(4):
        for k in range(NA):
            for x in range(2):
                to = place(d * NA + k, x + 1)
                if d != 1:
                    source = pl.ds((DOWN_Y.index(d) * NA + k) * 8 + x * 4, 4)
                    bufs[YP][pl.ds(to + 3, 4, stride=2), :] = ynext[source, :]
                bufs[YM][pl.ds(to + 2, 4, stride=2), :] = yprev[pl.ds((d * NA + k) * 8 + x * 4, 4), :]
                if d == 3:
                    bufs[YP][pl.ds(to + 1, 1), :] = zero
                if d == 1:
                    bufs[YM][pl.ds(to + 10, 1), :] = zero
    fill_mixed(bufs, NA)


def fill_lambda_x(xnext, xprev, bufs):
    zero = jnp.zeros((2, 128), jnp.float32)
    for d in range(4):
        for k in range(NA):
            high, low = place(d * NA + k, 3), place(d * NA + k, 0)
            if d != 0:
                bufs[O][pl.ds(high + 2, 8), :] = xnext[pl.ds(((d - 1) * NA + k) * 8, 8), :]
            bufs[O][pl.ds(low + 2, 8), :] = xprev[pl.ds((d * NA + k) * 8, 8), :]
            if d == 3:
                bufs[O][pl.ds(high, 2), :] = zero
            if d == 0:
                bufs[O][pl.ds(low + 10, 2), :] = zero
    for k in range(NA):
        bufs[YM][pl.ds(place(NA + k, 3) + 2, 4, stride=2), :] = xnext[pl.ds(192 + k * 4, 4), :]
        bufs[YP][pl.ds(place(k, 0) + 3, 4, stride=2), :] = xprev[pl.ds(256 + k * 4, 4), :]
    fill_edges(bufs, NA)


def step(*signed):
    vector = [0, 0, 0, 0]
    for which, sign in signed:
        vector[which] += sign
    return vector


def where(bufs, n, d, offset, x):
    key = buffer_of[(offset[1], offset[2])]
    row = 2 + 2 * offset[3]
    dd = d - base_dir.get(key, 0)
    shift = (x + 1 + offset[0]) * ROWS

    def read(k):
        return bufs[key][pl.ds(place(dd * n + k, 0) + row + shift, 8), :]

    return read


def link(bufs, d, offset, x):
    read = where(bufs, NC, d, offset, x)
    return load_matrix(lambda i, j, ri: read((i * 3 + j) * 2 + ri))


def lam_at(bufs, d, offset, x):
    read = where(bufs, NA, d, offset, x)
    return unpack8([read(k) for k in range(NA)])


def exponent_force(v, u, target, clow):
    a = v[:3]
    off = [(v[3 + 2 * k], v[4 + 2 * k]) for k in range(3)]
    norm = [r * r + s * s for r, s in off]
    sd = [
        -(a[0] * a[0] + norm[0] + norm[1]),
        -(a[1] * a[1] + norm[0] + norm[2]),
        -(a[2] * a[2] + norm[1] + norm[2]),
    ]
    (r0, s0), (r1, s1), (r2, s2) = off
    so = [
        (a[2] * s0 - (r1 * r2 + s1 * s2), -a[2] * r0 - (s1 * r2 - r1 * s2)),
        (a[1] * s1 + (r0 * r2 - s0 * s2), -a[1] * r1 + (r0 * s2 + s0 * r2)),
        (a[0] * s2 - (r0 * r1 + s0 * s1), -a[0] * r2 - (r0 * s1 - s0 * r1)),
    ]
    c = 0.5 * (sd[0] + sd[1] + sd[2])
    cross = [off[k][1] * so[k][0] - off[k][0] * so[k][1] for k in range(3)]
    dd = (a[0] * sd[0] + a[1] * sd[1] + a[2] * sd[2] + 2.0 * (cross[0] + cross[1] + cross[2])) * (1.0 / 3.0)
    p0r = 1.0 - dd * dd * (1.0 / 720.0)
    p0i = dd * (1.0 / 6.0 + c * (1.0 / 120.0))
    p1r = 1.0 + c * (1.0 / 6.0 + c * (1.0 / 120.0))
    p1i = dd * (1.0 / 24.0 + c * (1.0 / 360.0))
    p2r = 0.5 + c * (1.0 / 24.0 + c * (1.0 / 720.0))
    p2i = dd * (1.0 / 120.0)
    m = mm(target, u, False, True)
    hd = [m[i][i][0] for i in range(3)]
    kd = [m[i][i][1] for i in range(3)]
    ho = [(0.5 * (m[i][j][0] + m[j][i][0]), 0.5 * (m[i][j][1] - m[j][i][1])) for i, j in UPPER]
    ko = [(0.5 * (m[i][j][0] - m[j][i][0]), 0.5 * (m[i][j][1] + m[j][i][1])) for i, j in UPPER]
    t0r = hd[0] + hd[1] + hd[2]
    t0i = -(kd[0] + kd[1] + kd[2])

    def dots(x, y, xo, yo):
        diag = x[0] * y[0] + x[1] * y[1] + x[2] * y[2]
        rest = [xo[k][0] * yo[k][0] + xo[k][1] * yo[k][1] for k in range(3)]
        return diag + 2.0 * (rest[0] + rest[1] + rest[2])

    def crossed(x, y, xo, yo):
        diag = x[0] * y[0] + x[1] * y[1] + x[2] * y[2]
        rest = [yo[k][1] * xo[k][0] - yo[k][0] * xo[k][1] for k in range(3)]
        return diag + 2.0 * (rest[0] + rest[1] + rest[2])

    t1r = dots(kd, a, ko, off)
    t1i = crossed(hd, a, ho, off)
    t2r = dots(hd, sd, ho, so)
    t2i = -crossed(sd, kd, so, ko)
    by_c = (
        t1r * (1.0 / 6.0 + c * (1.0 / 60.0))
        + t2r * (1.0 / 24.0 + c * (1.0 / 360.0))
        - dd * (t0i * (1.0 / 120.0) + t1i * (1.0 / 360.0))
    )
    by_d = -(
        dd * t0r * (1.0 / 360.0)
        + t0i * (1.0 / 6.0 + c * (1.0 / 120.0))
        + t1i * (1.0 / 24.0 + c * (1.0 / 360.0))
        + t2i * (1.0 / 120.0)
    )
    herm = [[None] * 3 for _ in range(3)]
    for i in range(3):
        herm[i][i] = (-(p2r * hd[i] + p2i * kd[i]), None)
    for k, (i, j) in enumerate(UPPER):
        re = -(p2r * ho[k][0] + p2i * ko[k][1])
        im = p2i * ko[k][0] - p2r * ho[k][1]
        herm[i][j] = (re, im)
        herm[j][i] = (re, -im)
    amat = anti(v)
    g = skew(mm(amat, herm))
    lam = [p1r * kd[i] - p1i * hd[i] + g[i] - by_c * a[i] + by_d * sd[i] for i in range(3)]
    for k in range(3):
        lam.append(p1r * ko[k][0] + p1i * ho[k][1] + g[3 + 2 * k] - by_c * off[k][0] - by_d * so[k][1])
        lam.append(p1r * ko[k][1] - p1i * ho[k][0] + g[4 + 2 * k] - by_c * off[k][1] + by_d * so[k][0])
    mean = (lam[0] + lam[1] + lam[2]) * (1.0 / 3.0)
    lam = [smear_weight * (lam[i] - mean) for i in range(3)] + [smear_weight * lam[k] for k in range(3, 9)]
    edag = [[None] * 3 for _ in range(3)]
    for i in range(3):
        edag[i][i] = (p0r - p1i * a[i] + p2r * sd[i], -(p0i + p1r * a[i] + p2i * sd[i]))
    for k, (i, j) in enumerate(UPPER):
        r, s = off[k]
        sr, si = so[k]
        edag[i][j] = (
            (p2r * sr - p1i * s) + (p2i * si - p1r * r),
            (p1i * r - p2i * sr) + (p2r * si - p1r * s),
        )
        edag[j][i] = (
            (p2r * sr - p1i * s) - (p2i * si - p1r * r),
            -(p1i * r + p2i * sr) - (p2r * si + p1r * s),
        )
    direct = msub(mm(edag, target), mm(anti(lam), clow))
    return lam, direct


def plane_fields(m, n):
    here = step()
    return [(m, here), (n, here), (n, step((m, 1))), (m, step((n, 1)))]


def lower_fields(m, n):
    back = step((n, -1))
    return [(n, back), (m, back), (n, step((n, -1), (m, 1)))]


def level(fields, x):
    found = 0
    for _, offset in fields:
        if x + offset[0] not in (0, 1):
            found = 2
        elif offset[1]:
            found = max(found, 1)
    return found


LOWERS = [(m, n) for m in range(4) for n in range(4) if n != m]


def items(wanted):
    planes = [(p, m, n, x) for x in range(2) for p, (m, n) in enumerate(PAIRS) if level(plane_fields(m, n), x) == wanted]
    lowers = [(m, n, x) for x in range(2) for m, n in LOWERS if level(lower_fields(m, n), x) == wanted]
    return planes, lowers


def cells(n, k, x):
    return pl.ds((n + k) * 16 + x * 8, 8)


def load_cells(ref, n, x):
    return load_matrix(lambda i, j, ri: ref[cells(n, (i * 3 + j) * 2 + ri, x), :])


def store_cells(ref, n, x, m):
    for i in range(3):
        for j in range(3):
            for ri in range(2):
                ref[cells(n, (i * 3 + j) * 2 + ri, x), :] = m[i][j][ri]


def take_incoming(incoming, inner):
    for c in range(144):
        inner[pl.ds(c * 8, 4, stride=2), :] = incoming[pl.ds(c * 8, 4), :]
        inner[pl.ds(c * 8 + 1, 4, stride=2), :] = incoming[pl.ds(c * 8 + 4, 4), :]


def forward_items(wanted, bufs, omega, loops, low):
    planes, lowers = items(wanted)
    begun = {(m, x) for w in range(wanted) for m, _, x in items(w)[1]}
    for p, m, n, x in planes:
        a, d, b, c = [link(bufs, which, offset, x) for which, offset in plane_fields(m, n)]
        loop = mm(mm(a, b), mm(d, c), False, True)
        store_cells(omega, p * 18, x, loop)
        for k, v in enumerate(skew(loop)):
            loops[cells(p * 9, k, x), :] = v
    for m in range(4):
        for x in range(2):
            value = load_cells(low, m * 18, x) if (m, x) in begun else None
            mine = [n for mm_, n, xx in lowers if (mm_, xx) == (m, x)]
            if not mine:
                continue
            for n in mine:
                e, g, h = [link(bufs, which, offset, x) for which, offset in lower_fields(m, n)]
                term = mm(mm(e, g, True, False), h)
                value = term if value is None else madd(value, term)
            store_cells(low, m * 18, x, value)


def finish_forward(bufs, inner, loops, low, lam_out, direct):
    for x in range(2):
        for m in range(4):
            u = link(bufs, m, step(), x)
            below = load_cells(low, m * 18, x)
            v = skew_product(below, u, True)
            for p, (f, s) in enumerate(PAIRS):
                if m == f:
                    v = [v[k] - loops[cells(p * 9, k, x), :] for k in range(9)]
                if m == s:
                    v = [v[k] + loops[cells(p * 9, k, x), :] for k in range(9)]
            mean = (v[0] + v[1] + v[2]) * (1.0 / 3.0)
            v = [(0.5 * smear_weight) * (v[k] - mean) for k in range(3)] + [
                (0.5 * smear_weight) * v[k] for k in range(3, 9)
            ]
            lam, force = exponent_force(v, u, load_cells(inner, m * 18, x), below)
            for k, v in enumerate(lam[:2] + lam[3:]):
                lam_out[cells(m * NA, k, x), :] = v
            store_cells(direct, m * 18, x, force)


def backward_items(wanted, bufs, lams, omega, sums, acc):
    planes, lowers = items(wanted)
    begun = {(d, x) for w in range(wanted) for _, m, n, x in items(w)[0] for d in (m, n)}

    def gather(d, x, m):
        store_cells(sums, d * 18, x, madd(load_cells(sums, d * 18, x), m) if (d, x) in begun else m)
        begun.add((d, x))

    for p, m, n, x in planes:
        fields = plane_fields(m, n)
        a, d = [link(bufs, which, offset, x) for which, offset in fields[:2]]
        la, ld, lb, lc = [lam_at(lams, which, offset, x) for which, offset in fields]
        lb, lc = carried(a, lb), carried(d, lc)
        loop = load_cells(omega, p * 18, x)
        z = [ld[k] - la[k] for k in range(9)]
        first = anti([z[k] + lc[k] for k in range(9)])
        second = anti([lb[k] - z[k] for k in range(9)])
        gather(m, x, msub(mm(first, loop, False, True), mm(loop, anti(lb), True, False)))
        gather(n, x, msub(mm(second, loop), mm(loop, anti(lc))))
    for m in range(4):
        for x in range(2):
            mine = [n for mm_, n, xx in lowers if (mm_, xx) == (m, x)]
            if not mine:
                continue
            force = load_cells(acc, m * 18, x)
            for n in mine:
                fields = lower_fields(m, n)
                e, g, h = [link(bufs, which, offset, x) for which, offset in fields]
                le, lg, lh = [lam_at(lams, which, offset, x) for which, offset in fields]
                inside = madd(mm(anti([lg[k] - le[k] for k in range(9)]), g), mm(g, anti(lh)))
                force = madd(force, mm(mm(e, inside, True, False), h))
            store_cells(acc, m * 18, x, force)


def finish_backward(bufs, sums, acc, out):
    for x in range(2):
        for m in range(4):
            f = load_cells(sums, m * 18, x)
            force = madd(mm(f, link(bufs, m, step(), x)), load_cells(acc, m * 18, x))
            store_cells(acc, m * 18, x, force)
            for k in range(18):
                at = ((m * 18 + k) * 2 + x) * 8
                out[pl.ds(at, 4), :] = acc[pl.ds(at, 4, stride=2), :]
                out[pl.ds(at + 4, 4), :] = acc[pl.ds(at + 1, 4, stride=2), :]


def links_local_body(*refs):
    links, incoming = refs[:2]
    bufs, (inner, omega, loops, low) = refs[2:9], refs[9:]
    fill_links_local(links, bufs)
    take_incoming(incoming, inner)
    forward_items(0, bufs, omega, loops, low)


def links_y_body(*refs):
    ynext, yprev = refs[:2]
    bufs, (omega, loops, low) = refs[12:19], refs[19:]
    fill_links_y(ynext, yprev, bufs)
    forward_items(1, bufs, omega, loops, low)


def links_x_body(*refs):
    xnext, corner, xprev, inner = refs[:4]
    bufs, (omega, loops, low, lam, direct, up, down) = refs[14:21], refs[21:]
    fill_links_x(xnext, corner, xprev, bufs)
    forward_items(2, bufs, omega, loops, low)
    finish_forward(bufs, inner, loops, low, lam, direct)

    def reader(row):
        return lambda d, q, x: lam[pl.ds(((d * NA + q) * 2 + x) * 8 + row, 4, stride=2), :]

    pack_y(up, down, NA, reader(1), reader(0))


def lambda_local_body(*refs):
    bufs, (omega, lam) = refs[:7], refs[7:9]
    acc, lams, sums = refs[10], refs[11:18], refs[18]
    fill_lambda_local(lam, lams)
    backward_items(0, bufs, lams, omega, sums, acc)


def lambda_y_body(*refs):
    bufs, (omega, ynext, yprev) = refs[:7], refs[7:10]
    acc, lams, sums = refs[19], refs[20:27], refs[27]
    fill_lambda_y(ynext, yprev, lams)
    backward_items(1, bufs, lams, omega, sums, acc)


def lambda_x_body(*refs):
    bufs, (omega, xnext, xprev) = refs[:7], refs[7:10]
    out, acc, lams, sums = refs[19], refs[20], refs[21:28], refs[28]
    fill_lambda_x(xnext, xprev, lams)
    backward_items(2, bufs, lams, omega, sums, acc)
    finish_backward(bufs, sums, acc, out)


def rows(n):
    return jax.ShapeDtypeStruct((n, 128), jnp.float32)


def buffer_rows(n):
    return [(n if key in base_dir else 4 * n) * 4 * ROWS for key in range(7)]


def call(body, args, outs, kept=(), cost=0, first=0):
    shapes = [rows(n) for n in outs]
    shapes[first:first] = [rows(a.shape[0]) for a in kept]
    return pl.pallas_call(
        body,
        out_shape=tuple(shapes),
        in_specs=[pl.BlockSpec(memory_space=pltpu.VMEM)] * (len(args) + len(kept)),
        out_specs=(pl.BlockSpec(memory_space=pltpu.VMEM),) * len(shapes),
        input_output_aliases={len(args) + k: first + k for k in range(len(kept))},
        cost_estimate=pl.CostEstimate(flops=cost, bytes_accessed=0, transcendentals=0) if cost else None,
        compiler_params=pltpu.CompilerParams(vmem_limit_bytes=VM),
    )(*args, *kept)


def shifted(shard, axis, by):
    length = lax.axis_size(axis)
    return lax.ppermute(shard, axis, [(i, (i + by) % length) for i in range(length)])


def diagonal(shard, by_x, by_y):
    nx, ny = lax.axis_size("gx"), lax.axis_size("gy")
    pairs = [(i * ny + j, (i + by_x) % nx * ny + (j + by_y) % ny) for i in range(nx) for j in range(ny)]
    return lax.ppermute(shard, ("gx", "gy"), pairs)


def body(links, incoming):
    links = jnp.transpose(links, (0, 1, 2, 3, 4, 6, 5, 7)).reshape(144 * ROWS, 128)
    shape = incoming.shape
    incoming = incoming.reshape(1152, 128)
    yup, ydown, xdown, corner = call(pack_first_body, (links,), (408, 312, 312, 48))
    yprev, ynext = shifted(yup, "gy", 1), shifted(ydown, "gy", -1)
    xnext, corner = shifted(xdown, "gx", -1), diagonal(corner, -1, 1)
    (xup,) = call(pack_x_body, (links, ynext), (456,))
    xprev = shifted(xup, "gx", 1)
    inner, *kept = (lambda r: (r[7], *r[:7], *r[8:]))(
        call(links_local_body, (links, incoming), buffer_rows(NC) + [1152, 1728, 864, 1152])
    )
    kept = call(links_y_body, (ynext, yprev), (), kept)
    r = call(links_x_body, (xnext, corner, xprev, inner), (512, 1152, 256, 192), kept)
    bufs, omega, (lam, acc, yup, ydown) = r[:7], r[7], r[10:]
    yprev, ynext = shifted(yup, "gy", 1), shifted(ydown, "gy", -1)
    kept = call(lambda_local_body, (*bufs, omega, lam), buffer_rows(NA) + [1152], (acc,))
    xup, xdown = call(pack_lambda_x_body, (lam, ynext, yprev), (288, 224))
    xprev, xnext = shifted(xup, "gx", 1), shifted(xdown, "gx", -1)
    kept = call(lambda_y_body, (*bufs, omega, ynext, yprev), (), kept)
    out = call(lambda_x_body, (*bufs, omega, xnext, xprev), (1152,), kept, first=1)[0]
    return out.reshape(shape)


def solution(mesh):
    placed = P(None, None, None, None, "gx", "gy", None, None)
    return jax.shard_map(body, mesh=mesh, in_specs=(placed, placed), out_specs=placed, check_vma=False)
```

```python
import jax
import jax.numpy as jnp
from jax import lax
from jax.experimental import pallas as pl
from jax.experimental.pallas import tpu as pltpu
from jax.sharding import PartitionSpec as P

smear_weight = 0.2
NC, NA = 18, 8
ROWS = 12
VM = 8 * 2**20
O, YP, YM, ZP, ZM, ZPYM, ZMYP = range(7)
buffer_of = {(0, 0): O, (1, 0): YP, (-1, 0): YM, (0, 1): ZP, (0, -1): ZM, (-1, 1): ZPYM, (1, -1): ZMYP}
base_dir = {ZPYM: 1, ZMYP: 2}
PAIRS = [(m, n) for m in range(4) for n in range(m + 1, 4)]
DOWN_Y = [0, 2, 3]
UPPER = [(0, 1), (0, 2), (1, 2)]


def total(terms):
    plus = [a * b for s, a, b in terms if s > 0]
    minus = [a * b for s, a, b in terms if s < 0]
    if not plus:
        value = -minus[0]
        minus = minus[1:]
    else:
        value = plus[0]
        for other in plus[1:]:
            value = value + other
    for other in minus:
        value = value - other
    return value


def entry(left, right, i, k, dag_left=False, dag_right=False, want=(True, True)):
    real, imag = [], []
    for j in range(3):
        ar, ai = left[j][i] if dag_left else left[i][j]
        br, bi = right[k][j] if dag_right else right[j][k]
        sa = -1 if dag_left else 1
        sb = -1 if dag_right else 1
        if ar is not None and br is not None:
            real.append((1, ar, br))
        if ai is not None and bi is not None:
            real.append((-sa * sb, ai, bi))
        if ar is not None and bi is not None:
            imag.append((sb, ar, bi))
        if ai is not None and br is not None:
            imag.append((sa, ai, br))
    return (total(real) if want[0] else None, total(imag) if want[1] else None)


def mm(left, right, dag_left=False, dag_right=False):
    return [[entry(left, right, i, k, dag_left, dag_right) for k in range(3)] for i in range(3)]


def madd(a, b):
    return [[(a[i][j][0] + b[i][j][0], a[i][j][1] + b[i][j][1]) for j in range(3)] for i in range(3)]


def msub(a, b):
    return [[(a[i][j][0] - b[i][j][0], a[i][j][1] - b[i][j][1]) for j in range(3)] for i in range(3)]


def skew(m):
    out = [m[i][i][1] + m[i][i][1] for i in range(3)]
    for i, j in UPPER:
        out += [m[i][j][0] - m[j][i][0], m[i][j][1] + m[j][i][1]]
    return out


def skew_product(left, right, dag_right=False):
    return skew(mm(left, right, False, dag_right))


def unpack8(v):
    return [v[0], v[1], -v[0] - v[1]] + list(v[2:])


def anti(v):
    out = [[None] * 3 for _ in range(3)]
    for i in range(3):
        out[i][i] = (None, v[i])
    for k, (i, j) in enumerate(UPPER):
        r, s = v[3 + 2 * k], v[4 + 2 * k]
        out[i][j] = (r, s)
        out[j][i] = (-r, s)
    return out


def carried(u, v):
    half = mm(u, anti(v))
    diag = [entry(half, u, i, i, False, True, (False, True))[1] for i in range(2)]
    out = [diag[0], diag[1], -diag[0] - diag[1]]
    for i, j in UPPER:
        out += list(entry(half, u, i, j, False, True))
    return out


def third_row(m):
    row = []
    for j in range(3):
        p, q = (j + 1) % 3, (j + 2) % 3
        ar, ai = m[0][p]
        br, bi = m[1][q]
        cr, ci = m[0][q]
        dr, di = m[1][p]
        row.append(
            (ar * br - ai * bi - cr * dr + ci * di, cr * di + ci * dr - ar * bi - ai * br)
        )
    return row


def comp(d, i, j, ri):
    return ((d * 3 + i) * 3 + j) * 2 + ri


def place(c, xe):
    return (c * 4 + xe) * ROWS


def load_matrix(read):
    return [[(read(i, j, 0), read(i, j, 1)) for j in range(3)] for i in range(3)]


def pack_y(up, down, n, read_up, read_down):
    for d in range(4):
        for q in range(n):
            for x in range(2):
                up[pl.ds(((d * n + q) * 2 + x) * 4, 4), :] = read_up(d, q, x)
                if d != 1:
                    down[pl.ds(((DOWN_Y.index(d) * n + q) * 2 + x) * 4, 4), :] = read_down(d, q, x)


def pack_first_body(links, yup, ydown, xdown, corner):
    def reader(row):
        return lambda d, q, x: links[pl.ds(((d * 18 + q) * 2 + x) * ROWS + row, 4, stride=2), :]

    pack_y(yup, ydown, 12, reader(3), reader(2))
    for q in range(12):
        for x in range(2):
            yup[pl.ds(384 + q * 2 + x, 1), :] = links[pl.ds(((18 + q) * 2 + x) * ROWS + 11, 1), :]
            ydown[pl.ds(288 + q * 2 + x, 1), :] = links[pl.ds(((54 + q) * 2 + x) * ROWS, 1), :]
        for d in range(1, 4):
            xdown[pl.ds(((d - 1) * 12 + q) * 8, 8), :] = links[pl.ds((d * 18 + q) * 2 * ROWS + 2, 8), :]
        xdown[pl.ds(288 + q * 2, 2), :] = links[pl.ds((54 + q) * 2 * ROWS, 2), :]
        corner[pl.ds(q * 4, 4), :] = links[pl.ds((18 + q) * 2 * ROWS + 3, 4, stride=2), :]


def pack_x_body(links, ynext, yprev, xnext, corner, after, up):
    for q in range(12):
        for d in range(4):
            up[pl.ds((d * 12 + q) * 8, 8), :] = links[pl.ds(((d * 18 + q) * 2 + 1) * ROWS + 2, 8), :]
        up[pl.ds(384 + q * 2, 2), :] = links[pl.ds((q * 2 + 1) * ROWS + 10, 2), :]
        up[pl.ds(408 + q * 4, 4), :] = ynext[pl.ds(q * 8 + 4, 4), :]


def pack_lambda_x_body(lam, ynext, yprev, after, up, down):
    for c in range(32):
        up[pl.ds(c * 8, 8), :] = lam[pl.ds((c * 2 + 1) * 8, 8), :]
        if c >= NA:
            down[pl.ds((c - NA) * 8, 8), :] = lam[pl.ds(c * 16, 8), :]
    for k in range(NA):
        up[pl.ds(256 + k * 4, 4), :] = ynext[pl.ds(k * 8 + 4, 4), :]
        down[pl.ds(192 + k * 4, 4), :] = yprev[pl.ds((NA + k) * 8, 4), :]


def two_rows(read):
    m = [[(read((i * 3 + j) * 2), read((i * 3 + j) * 2 + 1)) for j in range(3)] for i in range(2)]
    return m + [third_row(m)]


def put(write, m):
    for i in range(3):
        for j in range(3):
            for ri in range(2):
                write((i * 3 + j) * 2 + ri, m[i][j][ri])


def roll_z(v, by):
    return pltpu.roll(v, (128 - by) % 128, 1)


def fill_y(bufs, n, dirs_p, dirs_m):
    for x in (1, 2):
        for d in range(4):
            for k in range(n):
                at = place(d * n + k, x)
                if d in dirs_p:
                    bufs[YP][pl.ds(at, 6, stride=2), :] = bufs[O][pl.ds(at + 1, 6, stride=2), :]
                if d in dirs_m:
                    bufs[YM][pl.ds(at + 1, 6, stride=2), :] = bufs[O][pl.ds(at, 6, stride=2), :]


def fill_z(bufs, n):
    for d in range(4):
        for k in range(n):
            c = d * n + k
            for x in (1, 2):
                at = place(c, x)
                zp, zm = bufs[ZP], bufs[ZM]
                if d != 2:
                    zp[pl.ds(at + 2, 8), :] = roll_z(bufs[O][pl.ds(at + 2, 8), :], 1)
                if d == 3:
                    zp[pl.ds(at, 2), :] = roll_z(bufs[O][pl.ds(at, 2), :], 1)
                zm[pl.ds(at + 2, 8), :] = roll_z(bufs[O][pl.ds(at + 2, 8), :], -1)
                if d == 2:
                    zm[pl.ds(at + 10, 2), :] = roll_z(bufs[O][pl.ds(at + 10, 2), :], -1)


def fill_mixed(bufs, n):
    for k in range(n):
        for x in (1, 2):
            bufs[ZPYM][pl.ds(place(k, x) + 2, 8), :] = roll_z(bufs[YM][pl.ds(place(n + k, x) + 2, 8), :], 1)
            bufs[ZMYP][pl.ds(place(k, x) + 2, 8), :] = roll_z(bufs[YP][pl.ds(place(2 * n + k, x) + 2, 8), :], -1)


def fill_high(bufs, n):
    for k in range(n):
        high, side = place(2 * n + k, 3), place(n + k, 3)
        bufs[ZM][pl.ds(high + 2, 8), :] = roll_z(bufs[O][pl.ds(high + 2, 8), :], -1)
        bufs[YM][pl.ds(side + 3, 4, stride=2), :] = bufs[O][pl.ds(side + 2, 4, stride=2), :]


def fill_low(bufs, n):
    for k in range(n):
        low = place(k, 0)
        bufs[ZP][pl.ds(low + 2, 8), :] = roll_z(bufs[O][pl.ds(low + 2, 8), :], 1)
        bufs[YP][pl.ds(low + 2, 4, stride=2), :] = bufs[O][pl.ds(low + 3, 4, stride=2), :]


def fill_links_local(links, bufs):
    for c in range(72):
        for x in range(2):
            source, to = (c * 2 + x) * ROWS, place(c, x + 1)
            bufs[O][pl.ds(to, 8), :] = links[pl.ds(source, 8), :]
            bufs[O][pl.ds(to + 8, 4), :] = links[pl.ds(source + 8, 4), :]
    fill_y(bufs, NC, (0, 2, 3), (0, 1, 2, 3))
    fill_z(bufs, NC)


def fill_links_y(ynext, yprev, bufs):
    for d in range(4):
        for source, buf, off in ((ynext, YP, 3), (yprev, YM, 2)):
            if buf == YP and d == 1:
                continue
            slot = DOWN_Y.index(d) if buf == YP else d
            m = two_rows(lambda q: source[pl.ds((slot * 12 + q) * 8, 8), :])

            def write(q, v):
                for x in range(2):
                    bufs[buf][pl.ds(place(d * NC + q, x + 1) + off, 4, stride=2), :] = v[4 * x : 4 * x + 4]

            put(write, m)
    for source, buf, d, row, at in ((ynext, YP, 3, 1, 288), (yprev, YM, 1, 10, 384)):
        m = two_rows(lambda q: source[pl.ds(at + q * 2, 2), :])

        def write_row(q, v):
            for x in range(2):
                bufs[buf][pl.ds(place(d * NC + q, x + 1) + row, 1), :] = v[x : x + 1]

        put(write_row, m)
    fill_mixed(bufs, NC)


def fill_column(source, slots, corner, at, bufs, xe, edge, corner_to):
    for slot, d in enumerate(slots):
        m = two_rows(lambda q: source[pl.ds((slot * 12 + q) * 8, 8), :])

        def write(q, v):
            bufs[O][pl.ds(place(d * NC + q, xe) + 2, 8), :] = v

        put(write, m)
    d, row = edge
    m = two_rows(lambda q: source[pl.ds(len(slots) * 96 + q * 2, 2), :])

    def write_edge(q, v):
        bufs[O][pl.ds(place(d * NC + q, xe) + row, 2), :] = v

    put(write_edge, m)
    buf, corner_dir, off = corner_to
    m = two_rows(lambda q: corner[pl.ds(at + q * 4, 4), :])

    def write_corner(q, v):
        bufs[buf][pl.ds(place(corner_dir * NC + q, xe) + off, 4, stride=2), :] = v

    put(write_corner, m)


def fill_links_next(xnext, corner, bufs):
    fill_column(xnext, (1, 2, 3), corner, 0, bufs, 3, (3, 0), (YM, 1, 2))
    fill_high(bufs, NC)


def fill_links_prev(xprev, bufs):
    fill_column(xprev, (0, 1, 2, 3), xprev, 408, bufs, 0, (0, 10), (YP, 0, 3))
    fill_low(bufs, NC)


def fill_lambda_local(lam, bufs):
    zero = jnp.zeros((2, 128), jnp.float32)
    for c in range(32):
        for x in range(2):
            to = place(c, x + 1)
            bufs[O][pl.ds(to + 2, 8), :] = lam[pl.ds((c * 2 + x) * 8, 8), :]
            bufs[O][pl.ds(to, 2), :] = zero
            bufs[O][pl.ds(to + 10, 2), :] = zero
    fill_y(bufs, NA, (0, 2, 3), (0, 1, 2, 3))
    fill_z(bufs, NA)


def fill_lambda_y(ynext, yprev, bufs):
    zero = jnp.zeros((1, 128), jnp.float32)
    for d in range(4):
        for k in range(NA):
            for x in range(2):
                to = place(d * NA + k, x + 1)
                if d != 1:
                    source = pl.ds((DOWN_Y.index(d) * NA + k) * 8 + x * 4, 4)
                    bufs[YP][pl.ds(to + 3, 4, stride=2), :] = ynext[source, :]
                bufs[YM][pl.ds(to + 2, 4, stride=2), :] = yprev[pl.ds((d * NA + k) * 8 + x * 4, 4), :]
                if d == 3:
                    bufs[YP][pl.ds(to + 1, 1), :] = zero
                if d == 1:
                    bufs[YM][pl.ds(to + 10, 1), :] = zero
    fill_mixed(bufs, NA)


def fill_lambda_x(xnext, xprev, bufs):
    zero = jnp.zeros((2, 128), jnp.float32)
    for d in range(4):
        for k in range(NA):
            high, low = place(d * NA + k, 3), place(d * NA + k, 0)
            if d != 0:
                bufs[O][pl.ds(high + 2, 8), :] = xnext[pl.ds(((d - 1) * NA + k) * 8, 8), :]
            bufs[O][pl.ds(low + 2, 8), :] = xprev[pl.ds((d * NA + k) * 8, 8), :]
            if d == 3:
                bufs[O][pl.ds(high, 2), :] = zero
            if d == 0:
                bufs[O][pl.ds(low + 10, 2), :] = zero
    for k in range(NA):
        bufs[YM][pl.ds(place(NA + k, 3) + 2, 4, stride=2), :] = xnext[pl.ds(192 + k * 4, 4), :]
        bufs[YP][pl.ds(place(k, 0) + 3, 4, stride=2), :] = xprev[pl.ds(256 + k * 4, 4), :]
    fill_high(bufs, NA)
    fill_low(bufs, NA)


def step(*signed):
    vector = [0, 0, 0, 0]
    for which, sign in signed:
        vector[which] += sign
    return vector


def where(bufs, n, d, offset, x):
    key = buffer_of[(offset[1], offset[2])]
    row = 2 + 2 * offset[3]
    dd = d - base_dir.get(key, 0)
    shift = (x + 1 + offset[0]) * ROWS

    def read(k):
        return bufs[key][pl.ds(place(dd * n + k, 0) + row + shift, 8), :]

    return read


def link(bufs, d, offset, x):
    read = where(bufs, NC, d, offset, x)
    return load_matrix(lambda i, j, ri: read((i * 3 + j) * 2 + ri))


def lam_at(bufs, d, offset, x):
    read = where(bufs, NA, d, offset, x)
    return unpack8([read(k) for k in range(NA)])


def exponent_force(v, u, target, clow):
    a = v[:3]
    off = [(v[3 + 2 * k], v[4 + 2 * k]) for k in range(3)]
    norm = [r * r + s * s for r, s in off]
    sd = [
        -(a[0] * a[0] + norm[0] + norm[1]),
        -(a[1] * a[1] + norm[0] + norm[2]),
        -(a[2] * a[2] + norm[1] + norm[2]),
    ]
    (r0, s0), (r1, s1), (r2, s2) = off
    so = [
        (a[2] * s0 - (r1 * r2 + s1 * s2), -a[2] * r0 - (s1 * r2 - r1 * s2)),
        (a[1] * s1 + (r0 * r2 - s0 * s2), -a[1] * r1 + (r0 * s2 + s0 * r2)),
        (a[0] * s2 - (r0 * r1 + s0 * s1), -a[0] * r2 - (r0 * s1 - s0 * r1)),
    ]
    c = 0.5 * (sd[0] + sd[1] + sd[2])
    cross = [off[k][1] * so[k][0] - off[k][0] * so[k][1] for k in range(3)]
    dd = (a[0] * sd[0] + a[1] * sd[1] + a[2] * sd[2] + 2.0 * (cross[0] + cross[1] + cross[2])) * (1.0 / 3.0)
    p0r = 1.0 - dd * dd * (1.0 / 720.0)
    p0i = dd * (1.0 / 6.0 + c * (1.0 / 120.0))
    p1r = 1.0 + c * (1.0 / 6.0 + c * (1.0 / 120.0))
    p1i = dd * (1.0 / 24.0 + c * (1.0 / 360.0))
    p2r = 0.5 + c * (1.0 / 24.0 + c * (1.0 / 720.0))
    p2i = dd * (1.0 / 120.0)
    m = mm(target, u, False, True)
    hd = [m[i][i][0] for i in range(3)]
    kd = [m[i][i][1] for i in range(3)]
    ho = [(0.5 * (m[i][j][0] + m[j][i][0]), 0.5 * (m[i][j][1] - m[j][i][1])) for i, j in UPPER]
    ko = [(0.5 * (m[i][j][0] - m[j][i][0]), 0.5 * (m[i][j][1] + m[j][i][1])) for i, j in UPPER]
    t0r = hd[0] + hd[1] + hd[2]
    t0i = -(kd[0] + kd[1] + kd[2])

    def dots(x, y, xo, yo):
        diag = x[0] * y[0] + x[1] * y[1] + x[2] * y[2]
        rest = [xo[k][0] * yo[k][0] + xo[k][1] * yo[k][1] for k in range(3)]
        return diag + 2.0 * (rest[0] + rest[1] + rest[2])

    def crossed(x, y, xo, yo):
        diag = x[0] * y[0] + x[1] * y[1] + x[2] * y[2]
        rest = [yo[k][1] * xo[k][0] - yo[k][0] * xo[k][1] for k in range(3)]
        return diag + 2.0 * (rest[0] + rest[1] + rest[2])

    t1r = dots(kd, a, ko, off)
    t1i = crossed(hd, a, ho, off)
    t2r = dots(hd, sd, ho, so)
    t2i = -crossed(sd, kd, so, ko)
    by_c = (
        t1r * (1.0 / 6.0 + c * (1.0 / 60.0))
        + t2r * (1.0 / 24.0 + c * (1.0 / 360.0))
        - dd * (t0i * (1.0 / 120.0) + t1i * (1.0 / 360.0))
    )
    by_d = -(
        dd * t0r * (1.0 / 360.0)
        + t0i * (1.0 / 6.0 + c * (1.0 / 120.0))
        + t1i * (1.0 / 24.0 + c * (1.0 / 360.0))
        + t2i * (1.0 / 120.0)
    )
    herm = [[None] * 3 for _ in range(3)]
    for i in range(3):
        herm[i][i] = (-(p2r * hd[i] + p2i * kd[i]), None)
    for k, (i, j) in enumerate(UPPER):
        re = -(p2r * ho[k][0] + p2i * ko[k][1])
        im = p2i * ko[k][0] - p2r * ho[k][1]
        herm[i][j] = (re, im)
        herm[j][i] = (re, -im)
    amat = anti(v)
    g = skew(mm(amat, herm))
    lam = [p1r * kd[i] - p1i * hd[i] + g[i] - by_c * a[i] + by_d * sd[i] for i in range(3)]
    for k in range(3):
        lam.append(p1r * ko[k][0] + p1i * ho[k][1] + g[3 + 2 * k] - by_c * off[k][0] - by_d * so[k][1])
        lam.append(p1r * ko[k][1] - p1i * ho[k][0] + g[4 + 2 * k] - by_c * off[k][1] + by_d * so[k][0])
    mean = (lam[0] + lam[1] + lam[2]) * (1.0 / 3.0)
    lam = [smear_weight * (lam[i] - mean) for i in range(3)] + [smear_weight * lam[k] for k in range(3, 9)]
    edag = [[None] * 3 for _ in range(3)]
    for i in range(3):
        edag[i][i] = (p0r - p1i * a[i] + p2r * sd[i], -(p0i + p1r * a[i] + p2i * sd[i]))
    for k, (i, j) in enumerate(UPPER):
        r, s = off[k]
        sr, si = so[k]
        edag[i][j] = (
            (p2r * sr - p1i * s) + (p2i * si - p1r * r),
            (p1i * r - p2i * sr) + (p2r * si - p1r * s),
        )
        edag[j][i] = (
            (p2r * sr - p1i * s) - (p2i * si - p1r * r),
            -(p1i * r + p2i * sr) - (p2r * si + p1r * s),
        )
    direct = msub(mm(edag, target), mm(anti(lam), clow))
    return lam, direct


def plane_fields(m, n):
    here = step()
    return [(m, here), (n, here), (n, step((m, 1))), (m, step((n, 1)))]


def lower_fields(m, n):
    back = step((n, -1))
    return [(n, back), (m, back), (n, step((n, -1), (m, 1)))]


def level(fields, x):
    found = 0
    for _, offset in fields:
        if x + offset[0] == -1:
            found = 3
        elif x + offset[0] == 2:
            found = max(found, 2)
        elif offset[1]:
            found = max(found, 1)
    return found


LOWERS = [(m, n) for m in range(4) for n in range(4) if n != m]


def items(wanted):
    planes = [(p, m, n, x) for x in range(2) for p, (m, n) in enumerate(PAIRS) if level(plane_fields(m, n), x) == wanted]
    lowers = [(m, n, x) for x in range(2) for m, n in LOWERS if level(lower_fields(m, n), x) == wanted]
    return planes, lowers


def cells(n, k, x):
    return pl.ds((n + k) * 16 + x * 8, 8)


def load_cells(ref, n, x):
    return load_matrix(lambda i, j, ri: ref[cells(n, (i * 3 + j) * 2 + ri, x), :])


def store_cells(ref, n, x, m):
    for i in range(3):
        for j in range(3):
            for ri in range(2):
                ref[cells(n, (i * 3 + j) * 2 + ri, x), :] = m[i][j][ri]


def take_incoming(incoming, inner):
    for c in range(144):
        inner[pl.ds(c * 8, 4, stride=2), :] = incoming[pl.ds(c * 8, 4), :]
        inner[pl.ds(c * 8 + 1, 4, stride=2), :] = incoming[pl.ds(c * 8 + 4, 4), :]


def forward_items(wanted, bufs, omega, loops, low):
    planes, lowers = items(wanted)
    begun = {(m, x) for w in range(wanted) for m, _, x in items(w)[1]}
    for p, m, n, x in planes:
        a, d, b, c = [link(bufs, which, offset, x) for which, offset in plane_fields(m, n)]
        loop = mm(mm(a, b), mm(d, c), False, True)
        store_cells(omega, p * 18, x, loop)
        for k, v in enumerate(skew(loop)):
            loops[cells(p * 9, k, x), :] = v
    for m in range(4):
        for x in range(2):
            value = load_cells(low, m * 18, x) if (m, x) in begun else None
            mine = [n for mm_, n, xx in lowers if (mm_, xx) == (m, x)]
            if not mine:
                continue
            for n in mine:
                e, g, h = [link(bufs, which, offset, x) for which, offset in lower_fields(m, n)]
                term = mm(mm(e, g, True, False), h)
                value = term if value is None else madd(value, term)
            store_cells(low, m * 18, x, value)


def finish_forward(xs, bufs, inner, loops, low, lam_out, direct):
    for x in xs:
        for m in range(4):
            u = link(bufs, m, step(), x)
            below = load_cells(low, m * 18, x)
            v = skew_product(below, u, True)
            for p, (f, s) in enumerate(PAIRS):
                if m == f:
                    v = [v[k] - loops[cells(p * 9, k, x), :] for k in range(9)]
                if m == s:
                    v = [v[k] + loops[cells(p * 9, k, x), :] for k in range(9)]
            mean = (v[0] + v[1] + v[2]) * (1.0 / 3.0)
            v = [(0.5 * smear_weight) * (v[k] - mean) for k in range(3)] + [
                (0.5 * smear_weight) * v[k] for k in range(3, 9)
            ]
            lam, force = exponent_force(v, u, load_cells(inner, m * 18, x), below)
            for k, v in enumerate(lam[:2] + lam[3:]):
                lam_out[cells(m * NA, k, x), :] = v
            store_cells(direct, m * 18, x, force)


def backward_items(wanted, bufs, lams, omega, sums, acc):
    planes, lowers = items(wanted)
    begun = {(d, x) for w in range(wanted) for _, m, n, x in items(w)[0] for d in (m, n)}

    def gather(d, x, m):
        store_cells(sums, d * 18, x, madd(load_cells(sums, d * 18, x), m) if (d, x) in begun else m)
        begun.add((d, x))

    for p, m, n, x in planes:
        fields = plane_fields(m, n)
        a, d = [link(bufs, which, offset, x) for which, offset in fields[:2]]
        la, ld, lb, lc = [lam_at(lams, which, offset, x) for which, offset in fields]
        lb, lc = carried(a, lb), carried(d, lc)
        loop = load_cells(omega, p * 18, x)
        z = [ld[k] - la[k] for k in range(9)]
        first = anti([z[k] + lc[k] for k in range(9)])
        second = anti([lb[k] - z[k] for k in range(9)])
        gather(m, x, msub(mm(first, loop, False, True), mm(loop, anti(lb), True, False)))
        gather(n, x, msub(mm(second, loop), mm(loop, anti(lc))))
    for m in range(4):
        for x in range(2):
            mine = [n for mm_, n, xx in lowers if (mm_, xx) == (m, x)]
            if not mine:
                continue
            force = load_cells(acc, m * 18, x)
            for n in mine:
                fields = lower_fields(m, n)
                e, g, h = [link(bufs, which, offset, x) for which, offset in fields]
                le, lg, lh = [lam_at(lams, which, offset, x) for which, offset in fields]
                inside = madd(mm(anti([lg[k] - le[k] for k in range(9)]), g), mm(g, anti(lh)))
                force = madd(force, mm(mm(e, inside, True, False), h))
            store_cells(acc, m * 18, x, force)


def finish_backward(bufs, sums, acc, out):
    for x in range(2):
        for m in range(4):
            f = load_cells(sums, m * 18, x)
            force = madd(mm(f, link(bufs, m, step(), x)), load_cells(acc, m * 18, x))
            store_cells(acc, m * 18, x, force)
            for k in range(18):
                at = ((m * 18 + k) * 2 + x) * 8
                out[pl.ds(at, 4), :] = acc[pl.ds(at, 4, stride=2), :]
                out[pl.ds(at + 4, 4), :] = acc[pl.ds(at + 1, 4, stride=2), :]


def links_local_body(*refs):
    links, incoming = refs[:2]
    bufs, (inner, omega, loops, low) = refs[2:9], refs[9:]
    fill_links_local(links, bufs)
    take_incoming(incoming, inner)
    forward_items(0, bufs, omega, loops, low)


def links_y_body(*refs):
    ynext, yprev, xnext, corner, inner = refs[:5]
    bufs, (omega, loops, low, lam, direct) = refs[15:22], refs[22:]
    fill_links_y(ynext, yprev, bufs)
    forward_items(1, bufs, omega, loops, low)
    fill_links_next(xnext, corner, bufs)
    forward_items(2, bufs, omega, loops, low)
    finish_forward((1,), bufs, inner, loops, low, lam, direct)


def links_x_body(*refs):
    xprev, inner = refs[:2]
    bufs, (omega, loops, low, lam, direct, up, down) = refs[14:21], refs[21:]
    fill_links_prev(xprev, bufs)
    forward_items(3, bufs, omega, loops, low)
    finish_forward((0,), bufs, inner, loops, low, lam, direct)

    def reader(row):
        return lambda d, q, x: lam[pl.ds(((d * NA + q) * 2 + x) * 8 + row, 4, stride=2), :]

    pack_y(up, down, NA, reader(1), reader(0))


def lambda_local_body(*refs):
    bufs, (omega, lam) = refs[:7], refs[7:9]
    acc, lams, sums = refs[10], refs[11:18], refs[18]
    fill_lambda_local(lam, lams)
    backward_items(0, bufs, lams, omega, sums, acc)


def lambda_y_body(*refs):
    bufs, (omega, ynext, yprev) = refs[:7], refs[7:10]
    acc, lams, sums = refs[19], refs[20:27], refs[27]
    fill_lambda_y(ynext, yprev, lams)
    backward_items(1, bufs, lams, omega, sums, acc)


def lambda_x_body(*refs):
    bufs, (omega, xnext, xprev) = refs[:7], refs[7:10]
    out, acc, lams, sums = refs[19], refs[20], refs[21:28], refs[28]
    fill_lambda_x(xnext, xprev, lams)
    backward_items(2, bufs, lams, omega, sums, acc)
    backward_items(3, bufs, lams, omega, sums, acc)
    finish_backward(bufs, sums, acc, out)


def rows(n):
    return jax.ShapeDtypeStruct((n, 128), jnp.float32)


def buffer_rows(n):
    return [(n if key in base_dir else 4 * n) * 4 * ROWS for key in range(7)]


def call(body, args, outs, kept=(), cost=0, first=0):
    shapes = [rows(n) for n in outs]
    shapes[first:first] = [rows(a.shape[0]) for a in kept]
    return pl.pallas_call(
        body,
        out_shape=tuple(shapes),
        in_specs=[pl.BlockSpec(memory_space=pltpu.VMEM)] * (len(args) + len(kept)),
        out_specs=(pl.BlockSpec(memory_space=pltpu.VMEM),) * len(shapes),
        input_output_aliases={len(args) + k: first + k for k in range(len(kept))},
        cost_estimate=pl.CostEstimate(flops=cost, bytes_accessed=0, transcendentals=0) if cost else None,
        compiler_params=pltpu.CompilerParams(vmem_limit_bytes=VM),
    )(*args, *kept)


def shifted(shard, axis, by):
    length = lax.axis_size(axis)
    return lax.ppermute(shard, axis, [(i, (i + by) % length) for i in range(length)])


def diagonal(shard, by_x, by_y):
    nx, ny = lax.axis_size("gx"), lax.axis_size("gy")
    pairs = [(i * ny + j, (i + by_x) % nx * ny + (j + by_y) % ny) for i in range(nx) for j in range(ny)]
    return lax.ppermute(shard, ("gx", "gy"), pairs)


def body(links, incoming):
    links = jnp.transpose(links, (0, 1, 2, 3, 4, 6, 5, 7)).reshape(144 * ROWS, 128)
    shape = incoming.shape
    incoming = incoming.reshape(1152, 128)
    yup, ydown, xdown, corner = call(pack_first_body, (links,), (408, 312, 312, 48))
    yprev, ynext = shifted(yup, "gy", 1), shifted(ydown, "gy", -1)
    xnext, corner = shifted(xdown, "gx", -1), diagonal(corner, -1, 1)
    inner, *kept = (lambda r: (r[7], *r[:7], *r[8:]))(
        call(links_local_body, (links, incoming), buffer_rows(NC) + [1152, 1728, 864, 1152])
    )
    (xup,) = call(pack_x_body, (links, ynext, yprev, xnext, corner, kept[-1]), (456,))
    xprev = shifted(xup, "gx", 1)
    kept = call(links_y_body, (ynext, yprev, xnext, corner, inner), (512, 1152), kept)
    r = call(links_x_body, (xprev, inner), (256, 192), kept)
    bufs, omega, (lam, acc, yup, ydown) = r[:7], r[7], r[10:]
    yprev, ynext = shifted(yup, "gy", 1), shifted(ydown, "gy", -1)
    kept = call(lambda_local_body, (*bufs, omega, lam), buffer_rows(NA) + [1152], (acc,))
    xup, xdown = call(pack_lambda_x_body, (lam, ynext, yprev, kept[-1]), (288, 224))
    xprev, xnext = shifted(xup, "gx", 1), shifted(xdown, "gx", -1)
    kept = call(lambda_y_body, (*bufs, omega, ynext, yprev), (), kept)
    out = call(lambda_x_body, (*bufs, omega, xnext, xprev), (1152,), kept, first=1)[0]
    return out.reshape(shape)


def solution(mesh):
    placed = P(None, None, None, None, "gx", "gy", None, None)
    return jax.shard_map(body, mesh=mesh, in_specs=(placed, placed), out_specs=placed, check_vma=False)
```

```python
import jax
import jax.numpy as jnp
from jax import lax
from jax.experimental import pallas as pl
from jax.experimental.pallas import tpu as pltpu
from jax.sharding import PartitionSpec as P

smear_weight = 0.2
NC, NA = 18, 8
ROWS = 12
VM = 8 * 2**20
O, YP, YM, ZP, ZM, ZPYM, ZMYP = range(7)
buffer_of = {(0, 0): O, (1, 0): YP, (-1, 0): YM, (0, 1): ZP, (0, -1): ZM, (-1, 1): ZPYM, (1, -1): ZMYP}
base_dir = {ZPYM: 1, ZMYP: 2}
PAIRS = [(m, n) for m in range(4) for n in range(m + 1, 4)]
DOWN_Y = [0, 2, 3]
UPPER = [(0, 1), (0, 2), (1, 2)]


def total(terms):
    plus = [a * b for s, a, b in terms if s > 0]
    minus = [a * b for s, a, b in terms if s < 0]
    if not plus:
        value = -minus[0]
        minus = minus[1:]
    else:
        value = plus[0]
        for other in plus[1:]:
            value = value + other
    for other in minus:
        value = value - other
    return value


def entry(left, right, i, k, dag_left=False, dag_right=False, want=(True, True)):
    real, imag = [], []
    for j in range(3):
        ar, ai = left[j][i] if dag_left else left[i][j]
        br, bi = right[k][j] if dag_right else right[j][k]
        sa = -1 if dag_left else 1
        sb = -1 if dag_right else 1
        if ar is not None and br is not None:
            real.append((1, ar, br))
        if ai is not None and bi is not None:
            real.append((-sa * sb, ai, bi))
        if ar is not None and bi is not None:
            imag.append((sb, ar, bi))
        if ai is not None and br is not None:
            imag.append((sa, ai, br))
    return (total(real) if want[0] else None, total(imag) if want[1] else None)


def mm(left, right, dag_left=False, dag_right=False):
    return [[entry(left, right, i, k, dag_left, dag_right) for k in range(3)] for i in range(3)]


def madd(a, b):
    return [[(a[i][j][0] + b[i][j][0], a[i][j][1] + b[i][j][1]) for j in range(3)] for i in range(3)]


def msub(a, b):
    return [[(a[i][j][0] - b[i][j][0], a[i][j][1] - b[i][j][1]) for j in range(3)] for i in range(3)]


def skew(m):
    out = [m[i][i][1] + m[i][i][1] for i in range(3)]
    for i, j in UPPER:
        out += [m[i][j][0] - m[j][i][0], m[i][j][1] + m[j][i][1]]
    return out


def skew_product(left, right, dag_right=False):
    return skew(mm(left, right, False, dag_right))


def unpack8(v):
    return [v[0], v[1], -v[0] - v[1]] + list(v[2:])


def anti(v):
    out = [[None] * 3 for _ in range(3)]
    for i in range(3):
        out[i][i] = (None, v[i])
    for k, (i, j) in enumerate(UPPER):
        r, s = v[3 + 2 * k], v[4 + 2 * k]
        out[i][j] = (r, s)
        out[j][i] = (-r, s)
    return out


def carried(u, v):
    half = mm(u, anti(v))
    diag = [entry(half, u, i, i, False, True, (False, True))[1] for i in range(2)]
    out = [diag[0], diag[1], -diag[0] - diag[1]]
    for i, j in UPPER:
        out += list(entry(half, u, i, j, False, True))
    return out


def third_row(m):
    row = []
    for j in range(3):
        p, q = (j + 1) % 3, (j + 2) % 3
        ar, ai = m[0][p]
        br, bi = m[1][q]
        cr, ci = m[0][q]
        dr, di = m[1][p]
        row.append(
            (ar * br - ai * bi - cr * dr + ci * di, cr * di + ci * dr - ar * bi - ai * br)
        )
    return row


def comp(d, i, j, ri):
    return ((d * 3 + i) * 3 + j) * 2 + ri


def place(c, xe):
    return (c * 4 + xe) * ROWS


def load_matrix(read):
    return [[(read(i, j, 0), read(i, j, 1)) for j in range(3)] for i in range(3)]


def pack_y(up, down, n, read_up, read_down):
    for d in range(4):
        for q in range(n):
            for x in range(2):
                up[pl.ds(((d * n + q) * 2 + x) * 4, 4), :] = read_up(d, q, x)
                if d != 1:
                    down[pl.ds(((DOWN_Y.index(d) * n + q) * 2 + x) * 4, 4), :] = read_down(d, q, x)


def pack_first_body(links, xdown, xup, yup, ydown, cdown, cup):
    def reader(row):
        return lambda d, q, x: links[pl.ds(((d * 18 + q) * 2 + x) * ROWS + row, 4, stride=2), :]

    pack_y(yup, ydown, 12, reader(3), reader(2))
    for q in range(12):
        for x in range(2):
            yup[pl.ds(384 + q * 2 + x, 1), :] = links[pl.ds(((18 + q) * 2 + x) * ROWS + 11, 1), :]
            ydown[pl.ds(288 + q * 2 + x, 1), :] = links[pl.ds(((54 + q) * 2 + x) * ROWS, 1), :]
        for d in range(1, 4):
            xdown[pl.ds(((d - 1) * 12 + q) * 8, 8), :] = links[pl.ds((d * 18 + q) * 2 * ROWS + 2, 8), :]
        xdown[pl.ds(288 + q * 2, 2), :] = links[pl.ds((54 + q) * 2 * ROWS, 2), :]
        for d in range(4):
            xup[pl.ds((d * 12 + q) * 8, 8), :] = links[pl.ds(((d * 18 + q) * 2 + 1) * ROWS + 2, 8), :]
        xup[pl.ds(384 + q * 2, 2), :] = links[pl.ds((q * 2 + 1) * ROWS + 10, 2), :]
        cdown[pl.ds(q * 4, 4), :] = links[pl.ds((18 + q) * 2 * ROWS + 3, 4, stride=2), :]
        cup[pl.ds(q * 4, 4), :] = links[pl.ds((q * 2 + 1) * ROWS + 2, 4, stride=2), :]


def pack_lambda(lam, xdown, xup, yup, ydown, cdown, cup):
    def reader(row):
        return lambda d, q, x: lam[pl.ds(((d * NA + q) * 2 + x) * 8 + row, 4, stride=2), :]

    pack_y(yup, ydown, NA, reader(1), reader(0))
    for c in range(32):
        xup[pl.ds(c * 8, 8), :] = lam[pl.ds((c * 2 + 1) * 8, 8), :]
        if c >= NA:
            xdown[pl.ds((c - NA) * 8, 8), :] = lam[pl.ds(c * 16, 8), :]
    for k in range(NA):
        cdown[pl.ds(k * 4, 4), :] = lam[pl.ds((NA + k) * 16 + 1, 4, stride=2), :]
        cup[pl.ds(k * 4, 4), :] = lam[pl.ds((k * 2 + 1) * 8, 4, stride=2), :]


def two_rows(read):
    m = [[(read((i * 3 + j) * 2), read((i * 3 + j) * 2 + 1)) for j in range(3)] for i in range(2)]
    return m + [third_row(m)]


def put(write, m):
    for i in range(3):
        for j in range(3):
            for ri in range(2):
                write((i * 3 + j) * 2 + ri, m[i][j][ri])


def roll_z(v, by):
    return pltpu.roll(v, (128 - by) % 128, 1)


def fill_y(bufs, n, dirs_p, dirs_m):
    for x in (1, 2):
        for d in range(4):
            for k in range(n):
                at = place(d * n + k, x)
                if d in dirs_p:
                    bufs[YP][pl.ds(at, 6, stride=2), :] = bufs[O][pl.ds(at + 1, 6, stride=2), :]
                if d in dirs_m:
                    bufs[YM][pl.ds(at + 1, 6, stride=2), :] = bufs[O][pl.ds(at, 6, stride=2), :]


def fill_z(bufs, n):
    for d in range(4):
        for k in range(n):
            c = d * n + k
            for x in (1, 2):
                at = place(c, x)
                zp, zm = bufs[ZP], bufs[ZM]
                if d != 2:
                    zp[pl.ds(at + 2, 8), :] = roll_z(bufs[O][pl.ds(at + 2, 8), :], 1)
                if d == 3:
                    zp[pl.ds(at, 2), :] = roll_z(bufs[O][pl.ds(at, 2), :], 1)
                zm[pl.ds(at + 2, 8), :] = roll_z(bufs[O][pl.ds(at + 2, 8), :], -1)
                if d == 2:
                    zm[pl.ds(at + 10, 2), :] = roll_z(bufs[O][pl.ds(at + 10, 2), :], -1)


def fill_mixed(bufs, n):
    for k in range(n):
        for x in (1, 2):
            bufs[ZPYM][pl.ds(place(k, x) + 2, 8), :] = roll_z(bufs[YM][pl.ds(place(n + k, x) + 2, 8), :], 1)
            bufs[ZMYP][pl.ds(place(k, x) + 2, 8), :] = roll_z(bufs[YP][pl.ds(place(2 * n + k, x) + 2, 8), :], -1)


def fill_high(bufs, n):
    for k in range(n):
        high, side = place(2 * n + k, 3), place(n + k, 3)
        bufs[ZM][pl.ds(high + 2, 8), :] = roll_z(bufs[O][pl.ds(high + 2, 8), :], -1)
        bufs[YM][pl.ds(side + 3, 4, stride=2), :] = bufs[O][pl.ds(side + 2, 4, stride=2), :]


def fill_low(bufs, n):
    for k in range(n):
        low = place(k, 0)
        bufs[ZP][pl.ds(low + 2, 8), :] = roll_z(bufs[O][pl.ds(low + 2, 8), :], 1)
        bufs[YP][pl.ds(low + 2, 4, stride=2), :] = bufs[O][pl.ds(low + 3, 4, stride=2), :]


def fill_links_local(links, bufs):
    for c in range(72):
        for x in range(2):
            source, to = (c * 2 + x) * ROWS, place(c, x + 1)
            bufs[O][pl.ds(to, 8), :] = links[pl.ds(source, 8), :]
            bufs[O][pl.ds(to + 8, 4), :] = links[pl.ds(source + 8, 4), :]
    fill_y(bufs, NC, (0, 2, 3), (0, 1, 2, 3))
    fill_z(bufs, NC)


def fill_links_y(ynext, yprev, bufs):
    for d in range(4):
        for source, buf, off in ((ynext, YP, 3), (yprev, YM, 2)):
            if buf == YP and d == 1:
                continue
            slot = DOWN_Y.index(d) if buf == YP else d
            m = two_rows(lambda q: source[pl.ds((slot * 12 + q) * 8, 8), :])

            def write(q, v):
                for x in range(2):
                    bufs[buf][pl.ds(place(d * NC + q, x + 1) + off, 4, stride=2), :] = v[4 * x : 4 * x + 4]

            put(write, m)
    for source, buf, d, row, at in ((ynext, YP, 3, 1, 288), (yprev, YM, 1, 10, 384)):
        m = two_rows(lambda q: source[pl.ds(at + q * 2, 2), :])

        def write_row(q, v):
            for x in range(2):
                bufs[buf][pl.ds(place(d * NC + q, x + 1) + row, 1), :] = v[x : x + 1]

        put(write_row, m)
    fill_mixed(bufs, NC)


def fill_column(source, slots, corner, bufs, xe, edge, corner_to):
    for slot, d in enumerate(slots):
        m = two_rows(lambda q: source[pl.ds((slot * 12 + q) * 8, 8), :])

        def write(q, v):
            bufs[O][pl.ds(place(d * NC + q, xe) + 2, 8), :] = v

        put(write, m)
    d, row = edge
    m = two_rows(lambda q: source[pl.ds(len(slots) * 96 + q * 2, 2), :])

    def write_edge(q, v):
        bufs[O][pl.ds(place(d * NC + q, xe) + row, 2), :] = v

    put(write_edge, m)
    buf, corner_dir, off = corner_to
    m = two_rows(lambda q: corner[pl.ds(q * 4, 4), :])

    def write_corner(q, v):
        bufs[buf][pl.ds(place(corner_dir * NC + q, xe) + off, 4, stride=2), :] = v

    put(write_corner, m)


def fill_links_next(xnext, corner, bufs):
    fill_column(xnext, (1, 2, 3), corner, bufs, 3, (3, 0), (YM, 1, 2))
    fill_high(bufs, NC)


def fill_links_prev(xprev, corner, bufs):
    fill_column(xprev, (0, 1, 2, 3), corner, bufs, 0, (0, 10), (YP, 0, 3))
    fill_low(bufs, NC)


def fill_lambda_local(lam, bufs):
    zero = jnp.zeros((2, 128), jnp.float32)
    for c in range(32):
        for x in range(2):
            to = place(c, x + 1)
            bufs[O][pl.ds(to + 2, 8), :] = lam[pl.ds((c * 2 + x) * 8, 8), :]
            bufs[O][pl.ds(to, 2), :] = zero
            bufs[O][pl.ds(to + 10, 2), :] = zero
    fill_y(bufs, NA, (0, 2, 3), (0, 1, 2, 3))
    fill_z(bufs, NA)


def fill_lambda_y(ynext, yprev, bufs):
    zero = jnp.zeros((1, 128), jnp.float32)
    for d in range(4):
        for k in range(NA):
            for x in range(2):
                to = place(d * NA + k, x + 1)
                if d != 1:
                    source = pl.ds((DOWN_Y.index(d) * NA + k) * 8 + x * 4, 4)
                    bufs[YP][pl.ds(to + 3, 4, stride=2), :] = ynext[source, :]
                bufs[YM][pl.ds(to + 2, 4, stride=2), :] = yprev[pl.ds((d * NA + k) * 8 + x * 4, 4), :]
                if d == 3:
                    bufs[YP][pl.ds(to + 1, 1), :] = zero
                if d == 1:
                    bufs[YM][pl.ds(to + 10, 1), :] = zero
    fill_mixed(bufs, NA)


def fill_lambda_x(xnext, cnext, xprev, cprev, bufs):
    zero = jnp.zeros((2, 128), jnp.float32)
    for d in range(4):
        for k in range(NA):
            high, low = place(d * NA + k, 3), place(d * NA + k, 0)
            if d != 0:
                bufs[O][pl.ds(high + 2, 8), :] = xnext[pl.ds(((d - 1) * NA + k) * 8, 8), :]
            bufs[O][pl.ds(low + 2, 8), :] = xprev[pl.ds((d * NA + k) * 8, 8), :]
            if d == 3:
                bufs[O][pl.ds(high, 2), :] = zero
            if d == 0:
                bufs[O][pl.ds(low + 10, 2), :] = zero
    for k in range(NA):
        bufs[YM][pl.ds(place(NA + k, 3) + 2, 4, stride=2), :] = cnext[pl.ds(k * 4, 4), :]
        bufs[YP][pl.ds(place(k, 0) + 3, 4, stride=2), :] = cprev[pl.ds(k * 4, 4), :]
    fill_high(bufs, NA)
    fill_low(bufs, NA)


def step(*signed):
    vector = [0, 0, 0, 0]
    for which, sign in signed:
        vector[which] += sign
    return vector


def where(bufs, n, d, offset, x):
    key = buffer_of[(offset[1], offset[2])]
    row = 2 + 2 * offset[3]
    dd = d - base_dir.get(key, 0)
    shift = (x + 1 + offset[0]) * ROWS

    def read(k):
        return bufs[key][pl.ds(place(dd * n + k, 0) + row + shift, 8), :]

    return read


def link(bufs, d, offset, x):
    read = where(bufs, NC, d, offset, x)
    return load_matrix(lambda i, j, ri: read((i * 3 + j) * 2 + ri))


def lam_at(bufs, d, offset, x):
    read = where(bufs, NA, d, offset, x)
    return unpack8([read(k) for k in range(NA)])


def exponent_force(v, u, target, clow):
    a = v[:3]
    off = [(v[3 + 2 * k], v[4 + 2 * k]) for k in range(3)]
    norm = [r * r + s * s for r, s in off]
    sd = [
        -(a[0] * a[0] + norm[0] + norm[1]),
        -(a[1] * a[1] + norm[0] + norm[2]),
        -(a[2] * a[2] + norm[1] + norm[2]),
    ]
    (r0, s0), (r1, s1), (r2, s2) = off
    so = [
        (a[2] * s0 - (r1 * r2 + s1 * s2), -a[2] * r0 - (s1 * r2 - r1 * s2)),
        (a[1] * s1 + (r0 * r2 - s0 * s2), -a[1] * r1 + (r0 * s2 + s0 * r2)),
        (a[0] * s2 - (r0 * r1 + s0 * s1), -a[0] * r2 - (r0 * s1 - s0 * r1)),
    ]
    c = 0.5 * (sd[0] + sd[1] + sd[2])
    cross = [off[k][1] * so[k][0] - off[k][0] * so[k][1] for k in range(3)]
    dd = (a[0] * sd[0] + a[1] * sd[1] + a[2] * sd[2] + 2.0 * (cross[0] + cross[1] + cross[2])) * (1.0 / 3.0)
    p0r = 1.0 - dd * dd * (1.0 / 720.0)
    p0i = dd * (1.0 / 6.0 + c * (1.0 / 120.0))
    p1r = 1.0 + c * (1.0 / 6.0 + c * (1.0 / 120.0))
    p1i = dd * (1.0 / 24.0 + c * (1.0 / 360.0))
    p2r = 0.5 + c * (1.0 / 24.0 + c * (1.0 / 720.0))
    p2i = dd * (1.0 / 120.0)
    m = mm(target, u, False, True)
    hd = [m[i][i][0] for i in range(3)]
    kd = [m[i][i][1] for i in range(3)]
    ho = [(0.5 * (m[i][j][0] + m[j][i][0]), 0.5 * (m[i][j][1] - m[j][i][1])) for i, j in UPPER]
    ko = [(0.5 * (m[i][j][0] - m[j][i][0]), 0.5 * (m[i][j][1] + m[j][i][1])) for i, j in UPPER]
    t0r = hd[0] + hd[1] + hd[2]
    t0i = -(kd[0] + kd[1] + kd[2])

    def dots(x, y, xo, yo):
        diag = x[0] * y[0] + x[1] * y[1] + x[2] * y[2]
        rest = [xo[k][0] * yo[k][0] + xo[k][1] * yo[k][1] for k in range(3)]
        return diag + 2.0 * (rest[0] + rest[1] + rest[2])

    def crossed(x, y, xo, yo):
        diag = x[0] * y[0] + x[1] * y[1] + x[2] * y[2]
        rest = [yo[k][1] * xo[k][0] - yo[k][0] * xo[k][1] for k in range(3)]
        return diag + 2.0 * (rest[0] + rest[1] + rest[2])

    t1r = dots(kd, a, ko, off)
    t1i = crossed(hd, a, ho, off)
    t2r = dots(hd, sd, ho, so)
    t2i = -crossed(sd, kd, so, ko)
    by_c = (
        t1r * (1.0 / 6.0 + c * (1.0 / 60.0))
        + t2r * (1.0 / 24.0 + c * (1.0 / 360.0))
        - dd * (t0i * (1.0 / 120.0) + t1i * (1.0 / 360.0))
    )
    by_d = -(
        dd * t0r * (1.0 / 360.0)
        + t0i * (1.0 / 6.0 + c * (1.0 / 120.0))
        + t1i * (1.0 / 24.0 + c * (1.0 / 360.0))
        + t2i * (1.0 / 120.0)
    )
    herm = [[None] * 3 for _ in range(3)]
    for i in range(3):
        herm[i][i] = (-(p2r * hd[i] + p2i * kd[i]), None)
    for k, (i, j) in enumerate(UPPER):
        re = -(p2r * ho[k][0] + p2i * ko[k][1])
        im = p2i * ko[k][0] - p2r * ho[k][1]
        herm[i][j] = (re, im)
        herm[j][i] = (re, -im)
    amat = anti(v)
    g = skew(mm(amat, herm))
    lam = [p1r * kd[i] - p1i * hd[i] + g[i] - by_c * a[i] + by_d * sd[i] for i in range(3)]
    for k in range(3):
        lam.append(p1r * ko[k][0] + p1i * ho[k][1] + g[3 + 2 * k] - by_c * off[k][0] - by_d * so[k][1])
        lam.append(p1r * ko[k][1] - p1i * ho[k][0] + g[4 + 2 * k] - by_c * off[k][1] + by_d * so[k][0])
    mean = (lam[0] + lam[1] + lam[2]) * (1.0 / 3.0)
    lam = [smear_weight * (lam[i] - mean) for i in range(3)] + [smear_weight * lam[k] for k in range(3, 9)]
    edag = [[None] * 3 for _ in range(3)]
    for i in range(3):
        edag[i][i] = (p0r - p1i * a[i] + p2r * sd[i], -(p0i + p1r * a[i] + p2i * sd[i]))
    for k, (i, j) in enumerate(UPPER):
        r, s = off[k]
        sr, si = so[k]
        edag[i][j] = (
            (p2r * sr - p1i * s) + (p2i * si - p1r * r),
            (p1i * r - p2i * sr) + (p2r * si - p1r * s),
        )
        edag[j][i] = (
            (p2r * sr - p1i * s) - (p2i * si - p1r * r),
            -(p1i * r + p2i * sr) - (p2r * si + p1r * s),
        )
    direct = msub(mm(edag, target), mm(anti(lam), clow))
    return lam, direct


def plane_fields(m, n):
    here = step()
    return [(m, here), (n, here), (n, step((m, 1))), (m, step((n, 1)))]


def lower_fields(m, n):
    back = step((n, -1))
    return [(n, back), (m, back), (n, step((n, -1), (m, 1)))]


def level(fields, x):
    found = 0
    for _, offset in fields:
        if x + offset[0] == -1:
            found = 3
        elif x + offset[0] == 2:
            found = max(found, 2)
        elif offset[1]:
            found = max(found, 1)
    return found


LOWERS = [(m, n) for m in range(4) for n in range(4) if n != m]


def items(wanted):
    planes = [(p, m, n, x) for x in range(2) for p, (m, n) in enumerate(PAIRS) if level(plane_fields(m, n), x) == wanted]
    lowers = [(m, n, x) for x in range(2) for m, n in LOWERS if level(lower_fields(m, n), x) == wanted]
    return planes, lowers


def cells(n, k, x):
    return pl.ds((n + k) * 16 + x * 8, 8)


def load_cells(ref, n, x):
    return load_matrix(lambda i, j, ri: ref[cells(n, (i * 3 + j) * 2 + ri, x), :])


def store_cells(ref, n, x, m):
    for i in range(3):
        for j in range(3):
            for ri in range(2):
                ref[cells(n, (i * 3 + j) * 2 + ri, x), :] = m[i][j][ri]


def take_incoming(incoming, inner):
    for c in range(144):
        inner[pl.ds(c * 8, 4, stride=2), :] = incoming[pl.ds(c * 8, 4), :]
        inner[pl.ds(c * 8 + 1, 4, stride=2), :] = incoming[pl.ds(c * 8 + 4, 4), :]


def forward_items(wanted, bufs, omega, loops, low):
    planes, lowers = items(wanted)
    begun = {(m, x) for w in range(wanted) for m, _, x in items(w)[1]}
    for p, m, n, x in planes:
        a, d, b, c = [link(bufs, which, offset, x) for which, offset in plane_fields(m, n)]
        loop = mm(mm(a, b), mm(d, c), False, True)
        store_cells(omega, p * 18, x, loop)
        for k, v in enumerate(skew(loop)):
            loops[cells(p * 9, k, x), :] = v
    for m in range(4):
        for x in range(2):
            value = load_cells(low, m * 18, x) if (m, x) in begun else None
            mine = [n for mm_, n, xx in lowers if (mm_, xx) == (m, x)]
            if not mine:
                continue
            for n in mine:
                e, g, h = [link(bufs, which, offset, x) for which, offset in lower_fields(m, n)]
                term = mm(mm(e, g, True, False), h)
                value = term if value is None else madd(value, term)
            store_cells(low, m * 18, x, value)


def finish_forward(xs, bufs, inner, loops, low, lam_out, direct):
    for x in xs:
        for m in range(4):
            u = link(bufs, m, step(), x)
            below = load_cells(low, m * 18, x)
            v = skew_product(below, u, True)
            for p, (f, s) in enumerate(PAIRS):
                if m == f:
                    v = [v[k] - loops[cells(p * 9, k, x), :] for k in range(9)]
                if m == s:
                    v = [v[k] + loops[cells(p * 9, k, x), :] for k in range(9)]
            mean = (v[0] + v[1] + v[2]) * (1.0 / 3.0)
            v = [(0.5 * smear_weight) * (v[k] - mean) for k in range(3)] + [
                (0.5 * smear_weight) * v[k] for k in range(3, 9)
            ]
            lam, force = exponent_force(v, u, load_cells(inner, m * 18, x), below)
            for k, v in enumerate(lam[:2] + lam[3:]):
                lam_out[cells(m * NA, k, x), :] = v
            store_cells(direct, m * 18, x, force)


def backward_items(wanted, bufs, lams, omega, sums, acc):
    planes, lowers = items(wanted)
    begun = {(d, x) for w in range(wanted) for _, m, n, x in items(w)[0] for d in (m, n)}

    def gather(d, x, m):
        store_cells(sums, d * 18, x, madd(load_cells(sums, d * 18, x), m) if (d, x) in begun else m)
        begun.add((d, x))

    for p, m, n, x in planes:
        fields = plane_fields(m, n)
        a, d = [link(bufs, which, offset, x) for which, offset in fields[:2]]
        la, ld, lb, lc = [lam_at(lams, which, offset, x) for which, offset in fields]
        lb, lc = carried(a, lb), carried(d, lc)
        loop = load_cells(omega, p * 18, x)
        z = [ld[k] - la[k] for k in range(9)]
        first = anti([z[k] + lc[k] for k in range(9)])
        second = anti([lb[k] - z[k] for k in range(9)])
        gather(m, x, msub(mm(first, loop, False, True), mm(loop, anti(lb), True, False)))
        gather(n, x, msub(mm(second, loop), mm(loop, anti(lc))))
    for m in range(4):
        for x in range(2):
            mine = [n for mm_, n, xx in lowers if (mm_, xx) == (m, x)]
            if not mine:
                continue
            force = load_cells(acc, m * 18, x)
            for n in mine:
                fields = lower_fields(m, n)
                e, g, h = [link(bufs, which, offset, x) for which, offset in fields]
                le, lg, lh = [lam_at(lams, which, offset, x) for which, offset in fields]
                inside = madd(mm(anti([lg[k] - le[k] for k in range(9)]), g), mm(g, anti(lh)))
                force = madd(force, mm(mm(e, inside, True, False), h))
            store_cells(acc, m * 18, x, force)


def finish_backward(bufs, sums, acc, out):
    for x in range(2):
        for m in range(4):
            f = load_cells(sums, m * 18, x)
            force = madd(mm(f, link(bufs, m, step(), x)), load_cells(acc, m * 18, x))
            store_cells(acc, m * 18, x, force)
            for k in range(18):
                at = ((m * 18 + k) * 2 + x) * 8
                out[pl.ds(at, 4), :] = acc[pl.ds(at, 4, stride=2), :]
                out[pl.ds(at + 4, 4), :] = acc[pl.ds(at + 1, 4, stride=2), :]


def links_local_body(*refs):
    links = refs[0]
    bufs, (omega, loops, low) = refs[1:8], refs[8:]
    fill_links_local(links, bufs)
    forward_items(0, bufs, omega, loops, low)


def links_y_body(*refs):
    ynext, yprev, incoming = refs[:3]
    bufs, (omega, loops, low, inner) = refs[13:20], refs[20:]
    fill_links_y(ynext, yprev, bufs)
    take_incoming(incoming, inner)
    forward_items(1, bufs, omega, loops, low)


def links_x_body(*refs):
    xnext, cnext, xprev, cprev, inner = refs[:5]
    bufs, (omega, loops, low, lam, direct), messages = refs[15:22], refs[22:27], refs[27:]
    fill_links_next(xnext, cnext, bufs)
    forward_items(2, bufs, omega, loops, low)
    finish_forward((1,), bufs, inner, loops, low, lam, direct)
    fill_links_prev(xprev, cprev, bufs)
    forward_items(3, bufs, omega, loops, low)
    finish_forward((0,), bufs, inner, loops, low, lam, direct)
    pack_lambda(lam, *messages)


def lambda_local_body(*refs):
    bufs, (omega, lam) = refs[:7], refs[7:9]
    acc, lams, sums = refs[10], refs[11:18], refs[18]
    fill_lambda_local(lam, lams)
    backward_items(0, bufs, lams, omega, sums, acc)


def lambda_y_body(*refs):
    bufs, (omega, ynext, yprev) = refs[:7], refs[7:10]
    acc, lams, sums = refs[19], refs[20:27], refs[27]
    fill_lambda_y(ynext, yprev, lams)
    backward_items(1, bufs, lams, omega, sums, acc)


def lambda_x_body(*refs):
    bufs, (omega, xnext, cnext, xprev, cprev) = refs[:7], refs[7:12]
    out, acc, lams, sums = refs[21], refs[22], refs[23:30], refs[30]
    fill_lambda_x(xnext, cnext, xprev, cprev, lams)
    backward_items(2, bufs, lams, omega, sums, acc)
    backward_items(3, bufs, lams, omega, sums, acc)
    finish_backward(bufs, sums, acc, out)


def rows(n):
    return jax.ShapeDtypeStruct((n, 128), jnp.float32)


def buffer_rows(n):
    return [(n if key in base_dir else 4 * n) * 4 * ROWS for key in range(7)]


def call(body, args, outs, kept=(), cost=0, first=0):
    shapes = [rows(n) for n in outs]
    shapes[first:first] = [rows(a.shape[0]) for a in kept]
    return pl.pallas_call(
        body,
        out_shape=tuple(shapes),
        in_specs=[pl.BlockSpec(memory_space=pltpu.VMEM)] * (len(args) + len(kept)),
        out_specs=(pl.BlockSpec(memory_space=pltpu.VMEM),) * len(shapes),
        input_output_aliases={len(args) + k: first + k for k in range(len(kept))},
        cost_estimate=pl.CostEstimate(flops=cost, bytes_accessed=0, transcendentals=0) if cost else None,
        compiler_params=pltpu.CompilerParams(vmem_limit_bytes=VM),
    )(*args, *kept)


def shifted(shard, axis, by):
    length = lax.axis_size(axis)
    return lax.ppermute(shard, axis, [(i, (i + by) % length) for i in range(length)])


def diagonal(shard, by_x, by_y):
    nx, ny = lax.axis_size("gx"), lax.axis_size("gy")
    pairs = [(i * ny + j, (i + by_x) % nx * ny + (j + by_y) % ny) for i in range(nx) for j in range(ny)]
    return lax.ppermute(shard, ("gx", "gy"), pairs)


def exchanged(messages):
    xdown, xup, yup, ydown, cdown, cup = messages
    return (
        shifted(xdown, "gx", -1),
        shifted(xup, "gx", 1),
        shifted(yup, "gy", 1),
        shifted(ydown, "gy", -1),
        diagonal(cdown, -1, 1),
        diagonal(cup, 1, -1),
    )


def body(links, incoming):
    links = jnp.transpose(links, (0, 1, 2, 3, 4, 6, 5, 7)).reshape(144 * ROWS, 128)
    shape = incoming.shape
    incoming = incoming.reshape(1152, 128)
    xnext, xprev, yprev, ynext, cnext, cprev = exchanged(call(pack_first_body, (links,), (312, 408, 408, 312, 48, 48)))
    kept = call(links_local_body, (links,), buffer_rows(NC) + [1728, 864, 1152])
    *kept, inner = call(links_y_body, (ynext, yprev, incoming), (1152,), kept)
    r = call(links_x_body, (xnext, cnext, xprev, cprev, inner), (512, 1152, 192, 256, 256, 192, 32, 32), kept)
    bufs, omega, (lam, acc) = r[:7], r[7], r[10:12]
    xnext, xprev, yprev, ynext, cnext, cprev = exchanged(r[12:])
    kept = call(lambda_local_body, (*bufs, omega, lam), buffer_rows(NA) + [1152], (acc,))
    kept = call(lambda_y_body, (*bufs, omega, ynext, yprev), (), kept)
    out = call(lambda_x_body, (*bufs, omega, xnext, cnext, xprev, cprev), (1152,), kept, first=1)[0]
    return out.reshape(shape)


def solution(mesh):
    placed = P(None, None, None, None, "gx", "gy", None, None)
    return jax.shard_map(body, mesh=mesh, in_specs=(placed, placed), out_specs=placed, check_vma=False)
```

```python
import jax
import jax.numpy as jnp
from jax import lax
from jax.experimental import pallas as pl
from jax.experimental.pallas import tpu as pltpu
from jax.sharding import PartitionSpec as P

smear_weight = 0.2
NC, NA = 18, 8
ROWS = 12
VM = 8 * 2**20
O, YP, YM, ZP, ZM, ZPYM, ZMYP = range(7)
buffer_of = {(0, 0): O, (1, 0): YP, (-1, 0): YM, (0, 1): ZP, (0, -1): ZM, (-1, 1): ZPYM, (1, -1): ZMYP}
base_dir = {ZPYM: 1, ZMYP: 2}
PAIRS = [(m, n) for m in range(4) for n in range(m + 1, 4)]
DOWN_Y = [0, 2, 3]
UPPER = [(0, 1), (0, 2), (1, 2)]


def total(terms):
    plus = [a * b for s, a, b in terms if s > 0]
    minus = [a * b for s, a, b in terms if s < 0]
    if not plus:
        value = -minus[0]
        minus = minus[1:]
    else:
        value = plus[0]
        for other in plus[1:]:
            value = value + other
    for other in minus:
        value = value - other
    return value


def entry(left, right, i, k, dag_left=False, dag_right=False, want=(True, True)):
    real, imag = [], []
    for j in range(3):
        ar, ai = left[j][i] if dag_left else left[i][j]
        br, bi = right[k][j] if dag_right else right[j][k]
        sa = -1 if dag_left else 1
        sb = -1 if dag_right else 1
        if ar is not None and br is not None:
            real.append((1, ar, br))
        if ai is not None and bi is not None:
            real.append((-sa * sb, ai, bi))
        if ar is not None and bi is not None:
            imag.append((sb, ar, bi))
        if ai is not None and br is not None:
            imag.append((sa, ai, br))
    return (total(real) if want[0] else None, total(imag) if want[1] else None)


def mm(left, right, dag_left=False, dag_right=False):
    return [[entry(left, right, i, k, dag_left, dag_right) for k in range(3)] for i in range(3)]


def madd(a, b):
    return [[(a[i][j][0] + b[i][j][0], a[i][j][1] + b[i][j][1]) for j in range(3)] for i in range(3)]


def msub(a, b):
    return [[(a[i][j][0] - b[i][j][0], a[i][j][1] - b[i][j][1]) for j in range(3)] for i in range(3)]


def skew(m):
    out = [m[i][i][1] + m[i][i][1] for i in range(3)]
    for i, j in UPPER:
        out += [m[i][j][0] - m[j][i][0], m[i][j][1] + m[j][i][1]]
    return out


def skew_product(left, right, dag_right=False):
    return skew(mm(left, right, False, dag_right))


def unpack8(v):
    return [v[0], v[1], -v[0] - v[1]] + list(v[2:])


def anti(v):
    out = [[None] * 3 for _ in range(3)]
    for i in range(3):
        out[i][i] = (None, v[i])
    for k, (i, j) in enumerate(UPPER):
        r, s = v[3 + 2 * k], v[4 + 2 * k]
        out[i][j] = (r, s)
        out[j][i] = (-r, s)
    return out


def carried(u, v):
    half = mm(u, anti(v))
    diag = [entry(half, u, i, i, False, True, (False, True))[1] for i in range(2)]
    out = [diag[0], diag[1], -diag[0] - diag[1]]
    for i, j in UPPER:
        out += list(entry(half, u, i, j, False, True))
    return out


def third_row(m):
    row = []
    for j in range(3):
        p, q = (j + 1) % 3, (j + 2) % 3
        ar, ai = m[0][p]
        br, bi = m[1][q]
        cr, ci = m[0][q]
        dr, di = m[1][p]
        row.append(
            (ar * br - ai * bi - cr * dr + ci * di, cr * di + ci * dr - ar * bi - ai * br)
        )
    return row


def comp(d, i, j, ri):
    return ((d * 3 + i) * 3 + j) * 2 + ri


def place(c, xe):
    return (c * 4 + xe) * ROWS


def load_matrix(read):
    return [[(read(i, j, 0), read(i, j, 1)) for j in range(3)] for i in range(3)]


def pack_y(up, down, n, read_up, read_down):
    for d in range(4):
        for q in range(n):
            for x in range(2):
                up[pl.ds(((d * n + q) * 2 + x) * 4, 4), :] = read_up(d, q, x)
                if d != 1:
                    down[pl.ds(((DOWN_Y.index(d) * n + q) * 2 + x) * 4, 4), :] = read_down(d, q, x)


def pack_first_body(links, xdown, xup, yup, ydown):
    def reader(row):
        return lambda d, q, x: links[pl.ds(((d * 18 + q) * 2 + x) * ROWS + row, 4, stride=2), :]

    pack_y(yup, ydown, 12, reader(3), reader(2))
    for q in range(12):
        for x in range(2):
            yup[pl.ds(384 + q * 2 + x, 1), :] = links[pl.ds(((18 + q) * 2 + x) * ROWS + 11, 1), :]
            ydown[pl.ds(288 + q * 2 + x, 1), :] = links[pl.ds(((54 + q) * 2 + x) * ROWS, 1), :]
        for d in range(1, 4):
            xdown[pl.ds(((d - 1) * 12 + q) * 8, 8), :] = links[pl.ds((d * 18 + q) * 2 * ROWS + 2, 8), :]
        xdown[pl.ds(288 + q * 2, 2), :] = links[pl.ds((54 + q) * 2 * ROWS, 2), :]
        for d in range(4):
            xup[pl.ds((d * 12 + q) * 8, 8), :] = links[pl.ds(((d * 18 + q) * 2 + 1) * ROWS + 2, 8), :]
        xup[pl.ds(384 + q * 2, 2), :] = links[pl.ds((q * 2 + 1) * ROWS + 10, 2), :]


def pack_corners_body(ynext, yprev, up, down):
    for q in range(12):
        up[pl.ds(q * 4, 4), :] = ynext[pl.ds(q * 8 + 4, 4), :]
        down[pl.ds(q * 4, 4), :] = yprev[pl.ds((12 + q) * 8, 4), :]


def pack_lambda_x_body(lam, ynext, yprev, after, up, down):
    for c in range(32):
        up[pl.ds(c * 8, 8), :] = lam[pl.ds((c * 2 + 1) * 8, 8), :]
        if c >= NA:
            down[pl.ds((c - NA) * 8, 8), :] = lam[pl.ds(c * 16, 8), :]
    for k in range(NA):
        up[pl.ds(256 + k * 4, 4), :] = ynext[pl.ds(k * 8 + 4, 4), :]
        down[pl.ds(192 + k * 4, 4), :] = yprev[pl.ds((NA + k) * 8, 4), :]


def two_rows(read):
    m = [[(read((i * 3 + j) * 2), read((i * 3 + j) * 2 + 1)) for j in range(3)] for i in range(2)]
    return m + [third_row(m)]


def put(write, m):
    for i in range(3):
        for j in range(3):
            for ri in range(2):
                write((i * 3 + j) * 2 + ri, m[i][j][ri])


def roll_z(v, by):
    return pltpu.roll(v, (128 - by) % 128, 1)


def fill_y(bufs, n, dirs_p, dirs_m):
    for x in (1, 2):
        for d in range(4):
            for k in range(n):
                at = place(d * n + k, x)
                if d in dirs_p:
                    bufs[YP][pl.ds(at, 6, stride=2), :] = bufs[O][pl.ds(at + 1, 6, stride=2), :]
                if d in dirs_m:
                    bufs[YM][pl.ds(at + 1, 6, stride=2), :] = bufs[O][pl.ds(at, 6, stride=2), :]


def fill_z(bufs, n):
    for d in range(4):
        for k in range(n):
            c = d * n + k
            for x in (1, 2):
                at = place(c, x)
                zp, zm = bufs[ZP], bufs[ZM]
                if d != 2:
                    zp[pl.ds(at + 2, 8), :] = roll_z(bufs[O][pl.ds(at + 2, 8), :], 1)
                if d == 3:
                    zp[pl.ds(at, 2), :] = roll_z(bufs[O][pl.ds(at, 2), :], 1)
                zm[pl.ds(at + 2, 8), :] = roll_z(bufs[O][pl.ds(at + 2, 8), :], -1)
                if d == 2:
                    zm[pl.ds(at + 10, 2), :] = roll_z(bufs[O][pl.ds(at + 10, 2), :], -1)


def fill_mixed(bufs, n):
    for k in range(n):
        for x in (1, 2):
            bufs[ZPYM][pl.ds(place(k, x) + 2, 8), :] = roll_z(bufs[YM][pl.ds(place(n + k, x) + 2, 8), :], 1)
            bufs[ZMYP][pl.ds(place(k, x) + 2, 8), :] = roll_z(bufs[YP][pl.ds(place(2 * n + k, x) + 2, 8), :], -1)


def fill_high(bufs, n):
    for k in range(n):
        high, side = place(2 * n + k, 3), place(n + k, 3)
        bufs[ZM][pl.ds(high + 2, 8), :] = roll_z(bufs[O][pl.ds(high + 2, 8), :], -1)
        bufs[YM][pl.ds(side + 3, 4, stride=2), :] = bufs[O][pl.ds(side + 2, 4, stride=2), :]


def fill_low(bufs, n):
    for k in range(n):
        low = place(k, 0)
        bufs[ZP][pl.ds(low + 2, 8), :] = roll_z(bufs[O][pl.ds(low + 2, 8), :], 1)
        bufs[YP][pl.ds(low + 2, 4, stride=2), :] = bufs[O][pl.ds(low + 3, 4, stride=2), :]


def fill_links_local(links, bufs):
    for c in range(72):
        for x in range(2):
            source, to = (c * 2 + x) * ROWS, place(c, x + 1)
            bufs[O][pl.ds(to, 8), :] = links[pl.ds(source, 8), :]
            bufs[O][pl.ds(to + 8, 4), :] = links[pl.ds(source + 8, 4), :]
    fill_y(bufs, NC, (0, 2, 3), (0, 1, 2, 3))
    fill_z(bufs, NC)


def fill_links_y(ynext, yprev, bufs):
    for d in range(4):
        for source, buf, off in ((ynext, YP, 3), (yprev, YM, 2)):
            if buf == YP and d == 1:
                continue
            slot = DOWN_Y.index(d) if buf == YP else d
            m = two_rows(lambda q: source[pl.ds((slot * 12 + q) * 8, 8), :])

            def write(q, v):
                for x in range(2):
                    bufs[buf][pl.ds(place(d * NC + q, x + 1) + off, 4, stride=2), :] = v[4 * x : 4 * x + 4]

            put(write, m)
    for source, buf, d, row, at in ((ynext, YP, 3, 1, 288), (yprev, YM, 1, 10, 384)):
        m = two_rows(lambda q: source[pl.ds(at + q * 2, 2), :])

        def write_row(q, v):
            for x in range(2):
                bufs[buf][pl.ds(place(d * NC + q, x + 1) + row, 1), :] = v[x : x + 1]

        put(write_row, m)
    fill_mixed(bufs, NC)


def fill_column(source, slots, corner, bufs, xe, edge, corner_to):
    for slot, d in enumerate(slots):
        m = two_rows(lambda q: source[pl.ds((slot * 12 + q) * 8, 8), :])

        def write(q, v):
            bufs[O][pl.ds(place(d * NC + q, xe) + 2, 8), :] = v

        put(write, m)
    d, row = edge
    m = two_rows(lambda q: source[pl.ds(len(slots) * 96 + q * 2, 2), :])

    def write_edge(q, v):
        bufs[O][pl.ds(place(d * NC + q, xe) + row, 2), :] = v

    put(write_edge, m)
    buf, corner_dir, off = corner_to
    m = two_rows(lambda q: corner[pl.ds(q * 4, 4), :])

    def write_corner(q, v):
        bufs[buf][pl.ds(place(corner_dir * NC + q, xe) + off, 4, stride=2), :] = v

    put(write_corner, m)


def fill_links_next(xnext, corner, bufs):
    fill_column(xnext, (1, 2, 3), corner, bufs, 3, (3, 0), (YM, 1, 2))
    fill_high(bufs, NC)


def fill_links_prev(xprev, corner, bufs):
    fill_column(xprev, (0, 1, 2, 3), corner, bufs, 0, (0, 10), (YP, 0, 3))
    fill_low(bufs, NC)


def fill_lambda_local(lam, bufs):
    zero = jnp.zeros((2, 128), jnp.float32)
    for c in range(32):
        for x in range(2):
            to = place(c, x + 1)
            bufs[O][pl.ds(to + 2, 8), :] = lam[pl.ds((c * 2 + x) * 8, 8), :]
            bufs[O][pl.ds(to, 2), :] = zero
            bufs[O][pl.ds(to + 10, 2), :] = zero
    fill_y(bufs, NA, (0, 2, 3), (0, 1, 2, 3))
    fill_z(bufs, NA)


def fill_lambda_y(ynext, yprev, bufs):
    zero = jnp.zeros((1, 128), jnp.float32)
    for d in range(4):
        for k in range(NA):
            for x in range(2):
                to = place(d * NA + k, x + 1)
                if d != 1:
                    source = pl.ds((DOWN_Y.index(d) * NA + k) * 8 + x * 4, 4)
                    bufs[YP][pl.ds(to + 3, 4, stride=2), :] = ynext[source, :]
                bufs[YM][pl.ds(to + 2, 4, stride=2), :] = yprev[pl.ds((d * NA + k) * 8 + x * 4, 4), :]
                if d == 3:
                    bufs[YP][pl.ds(to + 1, 1), :] = zero
                if d == 1:
                    bufs[YM][pl.ds(to + 10, 1), :] = zero
    fill_mixed(bufs, NA)


def fill_lambda_x(xnext, xprev, bufs):
    zero = jnp.zeros((2, 128), jnp.float32)
    for d in range(4):
        for k in range(NA):
            high, low = place(d * NA + k, 3), place(d * NA + k, 0)
            if d != 0:
                bufs[O][pl.ds(high + 2, 8), :] = xnext[pl.ds(((d - 1) * NA + k) * 8, 8), :]
            bufs[O][pl.ds(low + 2, 8), :] = xprev[pl.ds((d * NA + k) * 8, 8), :]
            if d == 3:
                bufs[O][pl.ds(high, 2), :] = zero
            if d == 0:
                bufs[O][pl.ds(low + 10, 2), :] = zero
    for k in range(NA):
        bufs[YM][pl.ds(place(NA + k, 3) + 2, 4, stride=2), :] = xnext[pl.ds(192 + k * 4, 4), :]
        bufs[YP][pl.ds(place(k, 0) + 3, 4, stride=2), :] = xprev[pl.ds(256 + k * 4, 4), :]
    fill_high(bufs, NA)
    fill_low(bufs, NA)


def step(*signed):
    vector = [0, 0, 0, 0]
    for which, sign in signed:
        vector[which] += sign
    return vector


def where(bufs, n, d, offset, x):
    key = buffer_of[(offset[1], offset[2])]
    row = 2 + 2 * offset[3]
    dd = d - base_dir.get(key, 0)
    shift = (x + 1 + offset[0]) * ROWS

    def read(k):
        return bufs[key][pl.ds(place(dd * n + k, 0) + row + shift, 8), :]

    return read


def link(bufs, d, offset, x):
    read = where(bufs, NC, d, offset, x)
    return load_matrix(lambda i, j, ri: read((i * 3 + j) * 2 + ri))


def lam_at(bufs, d, offset, x):
    read = where(bufs, NA, d, offset, x)
    return unpack8([read(k) for k in range(NA)])


def exponent_force(v, u, target, clow):
    a = v[:3]
    off = [(v[3 + 2 * k], v[4 + 2 * k]) for k in range(3)]
    norm = [r * r + s * s for r, s in off]
    sd = [
        -(a[0] * a[0] + norm[0] + norm[1]),
        -(a[1] * a[1] + norm[0] + norm[2]),
        -(a[2] * a[2] + norm[1] + norm[2]),
    ]
    (r0, s0), (r1, s1), (r2, s2) = off
    so = [
        (a[2] * s0 - (r1 * r2 + s1 * s2), -a[2] * r0 - (s1 * r2 - r1 * s2)),
        (a[1] * s1 + (r0 * r2 - s0 * s2), -a[1] * r1 + (r0 * s2 + s0 * r2)),
        (a[0] * s2 - (r0 * r1 + s0 * s1), -a[0] * r2 - (r0 * s1 - s0 * r1)),
    ]
    c = 0.5 * (sd[0] + sd[1] + sd[2])
    cross = [off[k][1] * so[k][0] - off[k][0] * so[k][1] for k in range(3)]
    dd = (a[0] * sd[0] + a[1] * sd[1] + a[2] * sd[2] + 2.0 * (cross[0] + cross[1] + cross[2])) * (1.0 / 3.0)
    p0r = 1.0 - dd * dd * (1.0 / 720.0)
    p0i = dd * (1.0 / 6.0 + c * (1.0 / 120.0))
    p1r = 1.0 + c * (1.0 / 6.0 + c * (1.0 / 120.0))
    p1i = dd * (1.0 / 24.0 + c * (1.0 / 360.0))
    p2r = 0.5 + c * (1.0 / 24.0 + c * (1.0 / 720.0))
    p2i = dd * (1.0 / 120.0)
    m = mm(target, u, False, True)
    hd = [m[i][i][0] for i in range(3)]
    kd = [m[i][i][1] for i in range(3)]
    ho = [(0.5 * (m[i][j][0] + m[j][i][0]), 0.5 * (m[i][j][1] - m[j][i][1])) for i, j in UPPER]
    ko = [(0.5 * (m[i][j][0] - m[j][i][0]), 0.5 * (m[i][j][1] + m[j][i][1])) for i, j in UPPER]
    t0r = hd[0] + hd[1] + hd[2]
    t0i = -(kd[0] + kd[1] + kd[2])

    def dots(x, y, xo, yo):
        diag = x[0] * y[0] + x[1] * y[1] + x[2] * y[2]
        rest = [xo[k][0] * yo[k][0] + xo[k][1] * yo[k][1] for k in range(3)]
        return diag + 2.0 * (rest[0] + rest[1] + rest[2])

    def crossed(x, y, xo, yo):
        diag = x[0] * y[0] + x[1] * y[1] + x[2] * y[2]
        rest = [yo[k][1] * xo[k][0] - yo[k][0] * xo[k][1] for k in range(3)]
        return diag + 2.0 * (rest[0] + rest[1] + rest[2])

    t1r = dots(kd, a, ko, off)
    t1i = crossed(hd, a, ho, off)
    t2r = dots(hd, sd, ho, so)
    t2i = -crossed(sd, kd, so, ko)
    by_c = (
        t1r * (1.0 / 6.0 + c * (1.0 / 60.0))
        + t2r * (1.0 / 24.0 + c * (1.0 / 360.0))
        - dd * (t0i * (1.0 / 120.0) + t1i * (1.0 / 360.0))
    )
    by_d = -(
        dd * t0r * (1.0 / 360.0)
        + t0i * (1.0 / 6.0 + c * (1.0 / 120.0))
        + t1i * (1.0 / 24.0 + c * (1.0 / 360.0))
        + t2i * (1.0 / 120.0)
    )
    herm = [[None] * 3 for _ in range(3)]
    for i in range(3):
        herm[i][i] = (-(p2r * hd[i] + p2i * kd[i]), None)
    for k, (i, j) in enumerate(UPPER):
        re = -(p2r * ho[k][0] + p2i * ko[k][1])
        im = p2i * ko[k][0] - p2r * ho[k][1]
        herm[i][j] = (re, im)
        herm[j][i] = (re, -im)
    amat = anti(v)
    g = skew(mm(amat, herm))
    lam = [p1r * kd[i] - p1i * hd[i] + g[i] - by_c * a[i] + by_d * sd[i] for i in range(3)]
    for k in range(3):
        lam.append(p1r * ko[k][0] + p1i * ho[k][1] + g[3 + 2 * k] - by_c * off[k][0] - by_d * so[k][1])
        lam.append(p1r * ko[k][1] - p1i * ho[k][0] + g[4 + 2 * k] - by_c * off[k][1] + by_d * so[k][0])
    mean = (lam[0] + lam[1] + lam[2]) * (1.0 / 3.0)
    lam = [smear_weight * (lam[i] - mean) for i in range(3)] + [smear_weight * lam[k] for k in range(3, 9)]
    edag = [[None] * 3 for _ in range(3)]
    for i in range(3):
        edag[i][i] = (p0r - p1i * a[i] + p2r * sd[i], -(p0i + p1r * a[i] + p2i * sd[i]))
    for k, (i, j) in enumerate(UPPER):
        r, s = off[k]
        sr, si = so[k]
        edag[i][j] = (
            (p2r * sr - p1i * s) + (p2i * si - p1r * r),
            (p1i * r - p2i * sr) + (p2r * si - p1r * s),
        )
        edag[j][i] = (
            (p2r * sr - p1i * s) - (p2i * si - p1r * r),
            -(p1i * r + p2i * sr) - (p2r * si + p1r * s),
        )
    direct = msub(mm(edag, target), mm(anti(lam), clow))
    return lam, direct


def plane_fields(m, n):
    here = step()
    return [(m, here), (n, here), (n, step((m, 1))), (m, step((n, 1)))]


def lower_fields(m, n):
    back = step((n, -1))
    return [(n, back), (m, back), (n, step((n, -1), (m, 1)))]


def level(fields, x):
    found = 0
    for _, offset in fields:
        if x + offset[0] == -1:
            found = 3
        elif x + offset[0] == 2:
            found = max(found, 2)
        elif offset[1]:
            found = max(found, 1)
    return found


LOWERS = [(m, n) for m in range(4) for n in range(4) if n != m]


def items(wanted):
    planes = [(p, m, n, x) for x in range(2) for p, (m, n) in enumerate(PAIRS) if level(plane_fields(m, n), x) == wanted]
    lowers = [(m, n, x) for x in range(2) for m, n in LOWERS if level(lower_fields(m, n), x) == wanted]
    return planes, lowers


def cells(n, k, x):
    return pl.ds((n + k) * 16 + x * 8, 8)


def load_cells(ref, n, x):
    return load_matrix(lambda i, j, ri: ref[cells(n, (i * 3 + j) * 2 + ri, x), :])


def store_cells(ref, n, x, m):
    for i in range(3):
        for j in range(3):
            for ri in range(2):
                ref[cells(n, (i * 3 + j) * 2 + ri, x), :] = m[i][j][ri]


def take_incoming(incoming, inner):
    for c in range(144):
        inner[pl.ds(c * 8, 4, stride=2), :] = incoming[pl.ds(c * 8, 4), :]
        inner[pl.ds(c * 8 + 1, 4, stride=2), :] = incoming[pl.ds(c * 8 + 4, 4), :]


def forward_items(wanted, bufs, omega, loops, low):
    planes, lowers = items(wanted)
    begun = {(m, x) for w in range(wanted) for m, _, x in items(w)[1]}
    for p, m, n, x in planes:
        a, d, b, c = [link(bufs, which, offset, x) for which, offset in plane_fields(m, n)]
        loop = mm(mm(a, b), mm(d, c), False, True)
        store_cells(omega, p * 18, x, loop)
        for k, v in enumerate(skew(loop)):
            loops[cells(p * 9, k, x), :] = v
    for m in range(4):
        for x in range(2):
            value = load_cells(low, m * 18, x) if (m, x) in begun else None
            mine = [n for mm_, n, xx in lowers if (mm_, xx) == (m, x)]
            if not mine:
                continue
            for n in mine:
                e, g, h = [link(bufs, which, offset, x) for which, offset in lower_fields(m, n)]
                term = mm(mm(e, g, True, False), h)
                value = term if value is None else madd(value, term)
            store_cells(low, m * 18, x, value)


def finish_forward(xs, bufs, inner, loops, low, lam_out, direct):
    for x in xs:
        for m in range(4):
            u = link(bufs, m, step(), x)
            below = load_cells(low, m * 18, x)
            v = skew_product(below, u, True)
            for p, (f, s) in enumerate(PAIRS):
                if m == f:
                    v = [v[k] - loops[cells(p * 9, k, x), :] for k in range(9)]
                if m == s:
                    v = [v[k] + loops[cells(p * 9, k, x), :] for k in range(9)]
            mean = (v[0] + v[1] + v[2]) * (1.0 / 3.0)
            v = [(0.5 * smear_weight) * (v[k] - mean) for k in range(3)] + [
                (0.5 * smear_weight) * v[k] for k in range(3, 9)
            ]
            lam, force = exponent_force(v, u, load_cells(inner, m * 18, x), below)
            for k, v in enumerate(lam[:2] + lam[3:]):
                lam_out[cells(m * NA, k, x), :] = v
            store_cells(direct, m * 18, x, force)


def backward_items(wanted, bufs, lams, omega, sums, acc):
    planes, lowers = items(wanted)
    begun = {(d, x) for w in range(wanted) for _, m, n, x in items(w)[0] for d in (m, n)}

    def gather(d, x, m):
        store_cells(sums, d * 18, x, madd(load_cells(sums, d * 18, x), m) if (d, x) in begun else m)
        begun.add((d, x))

    for p, m, n, x in planes:
        fields = plane_fields(m, n)
        a, d = [link(bufs, which, offset, x) for which, offset in fields[:2]]
        la, ld, lb, lc = [lam_at(lams, which, offset, x) for which, offset in fields]
        lb, lc = carried(a, lb), carried(d, lc)
        loop = load_cells(omega, p * 18, x)
        z = [ld[k] - la[k] for k in range(9)]
        first = anti([z[k] + lc[k] for k in range(9)])
        second = anti([lb[k] - z[k] for k in range(9)])
        gather(m, x, msub(mm(first, loop, False, True), mm(loop, anti(lb), True, False)))
        gather(n, x, msub(mm(second, loop), mm(loop, anti(lc))))
    for m in range(4):
        for x in range(2):
            mine = [n for mm_, n, xx in lowers if (mm_, xx) == (m, x)]
            if not mine:
                continue
            force = load_cells(acc, m * 18, x)
            for n in mine:
                fields = lower_fields(m, n)
                e, g, h = [link(bufs, which, offset, x) for which, offset in fields]
                le, lg, lh = [lam_at(lams, which, offset, x) for which, offset in fields]
                inside = madd(mm(anti([lg[k] - le[k] for k in range(9)]), g), mm(g, anti(lh)))
                force = madd(force, mm(mm(e, inside, True, False), h))
            store_cells(acc, m * 18, x, force)


def finish_backward(bufs, sums, acc, out):
    for x in range(2):
        for m in range(4):
            f = load_cells(sums, m * 18, x)
            force = madd(mm(f, link(bufs, m, step(), x)), load_cells(acc, m * 18, x))
            store_cells(acc, m * 18, x, force)
            for k in range(18):
                at = ((m * 18 + k) * 2 + x) * 8
                out[pl.ds(at, 4), :] = acc[pl.ds(at, 4, stride=2), :]
                out[pl.ds(at + 4, 4), :] = acc[pl.ds(at + 1, 4, stride=2), :]


def links_local_body(*refs):
    links = refs[0]
    bufs, (omega, loops, low) = refs[1:8], refs[8:]
    fill_links_local(links, bufs)
    forward_items(0, bufs, omega, loops, low)


def links_y_body(*refs):
    ynext, yprev, incoming = refs[:3]
    bufs, (omega, loops, low, inner) = refs[13:20], refs[20:]
    fill_links_y(ynext, yprev, bufs)
    take_incoming(incoming, inner)
    forward_items(1, bufs, omega, loops, low)


def links_x_body(*refs):
    xnext, cnext, xprev, cprev, inner = refs[:5]
    bufs, (omega, loops, low, lam, direct, up, down) = refs[15:22], refs[22:]
    fill_links_next(xnext, cnext, bufs)
    forward_items(2, bufs, omega, loops, low)
    finish_forward((1,), bufs, inner, loops, low, lam, direct)
    fill_links_prev(xprev, cprev, bufs)
    forward_items(3, bufs, omega, loops, low)
    finish_forward((0,), bufs, inner, loops, low, lam, direct)

    def reader(row):
        return lambda d, q, x: lam[pl.ds(((d * NA + q) * 2 + x) * 8 + row, 4, stride=2), :]

    pack_y(up, down, NA, reader(1), reader(0))


def lambda_local_body(*refs):
    bufs, (omega, lam) = refs[:7], refs[7:9]
    acc, lams, sums = refs[10], refs[11:18], refs[18]
    fill_lambda_local(lam, lams)
    backward_items(0, bufs, lams, omega, sums, acc)


def lambda_y_body(*refs):
    bufs, (omega, ynext, yprev) = refs[:7], refs[7:10]
    acc, lams, sums = refs[19], refs[20:27], refs[27]
    fill_lambda_y(ynext, yprev, lams)
    backward_items(1, bufs, lams, omega, sums, acc)


def lambda_x_body(*refs):
    bufs, (omega, xnext, xprev) = refs[:7], refs[7:10]
    out, acc, lams, sums = refs[19], refs[20], refs[21:28], refs[28]
    fill_lambda_x(xnext, xprev, lams)
    backward_items(2, bufs, lams, omega, sums, acc)
    backward_items(3, bufs, lams, omega, sums, acc)
    finish_backward(bufs, sums, acc, out)


def rows(n):
    return jax.ShapeDtypeStruct((n, 128), jnp.float32)


def buffer_rows(n):
    return [(n if key in base_dir else 4 * n) * 4 * ROWS for key in range(7)]


def call(body, args, outs, kept=(), cost=0, first=0):
    shapes = [rows(n) for n in outs]
    shapes[first:first] = [rows(a.shape[0]) for a in kept]
    return pl.pallas_call(
        body,
        out_shape=tuple(shapes),
        in_specs=[pl.BlockSpec(memory_space=pltpu.VMEM)] * (len(args) + len(kept)),
        out_specs=(pl.BlockSpec(memory_space=pltpu.VMEM),) * len(shapes),
        input_output_aliases={len(args) + k: first + k for k in range(len(kept))},
        cost_estimate=pl.CostEstimate(flops=cost, bytes_accessed=0, transcendentals=0) if cost else None,
        compiler_params=pltpu.CompilerParams(vmem_limit_bytes=VM),
    )(*args, *kept)


def shifted(shard, axis, by):
    length = lax.axis_size(axis)
    return lax.ppermute(shard, axis, [(i, (i + by) % length) for i in range(length)])


def body(links, incoming):
    links = jnp.transpose(links, (0, 1, 2, 3, 4, 6, 5, 7)).reshape(144 * ROWS, 128)
    shape = incoming.shape
    incoming = incoming.reshape(1152, 128)
    xdown, xup, yup, ydown = call(pack_first_body, (links,), (312, 408, 408, 312))
    xnext, xprev = shifted(xdown, "gx", -1), shifted(xup, "gx", 1)
    yprev, ynext = shifted(yup, "gy", 1), shifted(ydown, "gy", -1)
    cup, cdown = call(pack_corners_body, (ynext, yprev), (48, 48))
    cprev, cnext = shifted(cup, "gx", 1), shifted(cdown, "gx", -1)
    kept = call(links_local_body, (links,), buffer_rows(NC) + [1728, 864, 1152])
    *kept, inner = call(links_y_body, (ynext, yprev, incoming), (1152,), kept)
    r = call(links_x_body, (xnext, cnext, xprev, cprev, inner), (512, 1152, 256, 192), kept)
    bufs, omega, (lam, acc, yup, ydown) = r[:7], r[7], r[10:]
    yprev, ynext = shifted(yup, "gy", 1), shifted(ydown, "gy", -1)
    kept = call(lambda_local_body, (*bufs, omega, lam), buffer_rows(NA) + [1152], (acc,))
    xup, xdown = call(pack_lambda_x_body, (lam, ynext, yprev, kept[-1]), (288, 224))
    xprev, xnext = shifted(xup, "gx", 1), shifted(xdown, "gx", -1)
    kept = call(lambda_y_body, (*bufs, omega, ynext, yprev), (), kept)
    out = call(lambda_x_body, (*bufs, omega, xnext, xprev), (1152,), kept, first=1)[0]
    return out.reshape(shape)


def solution(mesh):
    placed = P(None, None, None, None, "gx", "gy", None, None)
    return jax.shard_map(body, mesh=mesh, in_specs=(placed, placed), out_specs=placed, check_vma=False)
```

```python
import jax
import jax.numpy as jnp
from jax import lax
from jax.experimental import pallas as pl
from jax.experimental.pallas import tpu as pltpu
from jax.sharding import PartitionSpec as P

smear_weight = 0.2
NC, NA = 18, 8
ROWS = 12
VM = 8 * 2**20
O, YP, YM, ZP, ZM, ZPYM, ZMYP = range(7)
buffer_of = {(0, 0): O, (1, 0): YP, (-1, 0): YM, (0, 1): ZP, (0, -1): ZM, (-1, 1): ZPYM, (1, -1): ZMYP}
base_dir = {ZPYM: 1, ZMYP: 2}
PAIRS = [(m, n) for m in range(4) for n in range(m + 1, 4)]
DOWN_Y = [0, 2, 3]
UPPER = [(0, 1), (0, 2), (1, 2)]


def total(terms):
    plus = [a * b for s, a, b in terms if s > 0]
    minus = [a * b for s, a, b in terms if s < 0]
    if not plus:
        value = -minus[0]
        minus = minus[1:]
    else:
        value = plus[0]
        for other in plus[1:]:
            value = value + other
    for other in minus:
        value = value - other
    return value


def entry(left, right, i, k, dag_left=False, dag_right=False, want=(True, True)):
    real, imag = [], []
    for j in range(3):
        ar, ai = left[j][i] if dag_left else left[i][j]
        br, bi = right[k][j] if dag_right else right[j][k]
        sa = -1 if dag_left else 1
        sb = -1 if dag_right else 1
        if ar is not None and br is not None:
            real.append((1, ar, br))
        if ai is not None and bi is not None:
            real.append((-sa * sb, ai, bi))
        if ar is not None and bi is not None:
            imag.append((sb, ar, bi))
        if ai is not None and br is not None:
            imag.append((sa, ai, br))
    return (total(real) if want[0] else None, total(imag) if want[1] else None)


def mm(left, right, dag_left=False, dag_right=False):
    return [[entry(left, right, i, k, dag_left, dag_right) for k in range(3)] for i in range(3)]


def madd(a, b):
    return [[(a[i][j][0] + b[i][j][0], a[i][j][1] + b[i][j][1]) for j in range(3)] for i in range(3)]


def msub(a, b):
    return [[(a[i][j][0] - b[i][j][0], a[i][j][1] - b[i][j][1]) for j in range(3)] for i in range(3)]


def skew(m):
    out = [m[i][i][1] + m[i][i][1] for i in range(3)]
    for i, j in UPPER:
        out += [m[i][j][0] - m[j][i][0], m[i][j][1] + m[j][i][1]]
    return out


def skew_product(left, right, dag_right=False):
    return skew(mm(left, right, False, dag_right))


def unpack8(v):
    return [v[0], v[1], -v[0] - v[1]] + list(v[2:])


def anti(v):
    out = [[None] * 3 for _ in range(3)]
    for i in range(3):
        out[i][i] = (None, v[i])
    for k, (i, j) in enumerate(UPPER):
        r, s = v[3 + 2 * k], v[4 + 2 * k]
        out[i][j] = (r, s)
        out[j][i] = (-r, s)
    return out


def carried(u, v):
    half = mm(u, anti(v))
    diag = [entry(half, u, i, i, False, True, (False, True))[1] for i in range(2)]
    out = [diag[0], diag[1], -diag[0] - diag[1]]
    for i, j in UPPER:
        out += list(entry(half, u, i, j, False, True))
    return out


def carried_back(u, v):
    half = mm(u, anti(v), True, False)
    diag = [entry(half, u, i, i, False, False, (False, True))[1] for i in range(2)]
    out = [diag[0], diag[1], -diag[0] - diag[1]]
    for i, j in UPPER:
        out += list(entry(half, u, i, j))
    return out


def first_rows():
    return lax.broadcasted_iota(jnp.int32, (8, 128), 0) % 2 == 0


def third_row(m):
    row = []
    for j in range(3):
        p, q = (j + 1) % 3, (j + 2) % 3
        ar, ai = m[0][p]
        br, bi = m[1][q]
        cr, ci = m[0][q]
        dr, di = m[1][p]
        row.append(
            (ar * br - ai * bi - cr * dr + ci * di, cr * di + ci * dr - ar * bi - ai * br)
        )
    return row


def comp(d, i, j, ri):
    return ((d * 3 + i) * 3 + j) * 2 + ri


def place(c, xe):
    return (c * 4 + xe) * ROWS


def load_matrix(read):
    return [[(read(i, j, 0), read(i, j, 1)) for j in range(3)] for i in range(3)]


def pack_y(up, down, n, read_up, read_down):
    for d in range(4):
        for q in range(n):
            for x in range(2):
                up[pl.ds(((d * n + q) * 2 + x) * 4, 4), :] = read_up(d, q, x)
                if d != 1:
                    down[pl.ds(((DOWN_Y.index(d) * n + q) * 2 + x) * 4, 4), :] = read_down(d, q, x)


def pack_first_body(links, xdown, yup, ydown):
    def reader(row):
        return lambda d, q, x: links[pl.ds(((d * 18 + q) * 2 + x) * ROWS + row, 4, stride=2), :]

    pack_y(yup, ydown, 12, reader(3), reader(2))
    for q in range(12):
        for x in range(2):
            yup[pl.ds(384 + q * 2 + x, 1), :] = links[pl.ds(((18 + q) * 2 + x) * ROWS + 11, 1), :]
            ydown[pl.ds(288 + q * 2 + x, 1), :] = links[pl.ds(((54 + q) * 2 + x) * ROWS, 1), :]
        for d in range(1, 4):
            xdown[pl.ds(((d - 1) * 12 + q) * 8, 8), :] = links[pl.ds((d * 18 + q) * 2 * ROWS + 2, 8), :]
        xdown[pl.ds(288 + q * 2, 2), :] = links[pl.ds((54 + q) * 2 * ROWS, 2), :]


def pack_up_body(links, up):
    def read(d, row):
        return load_matrix(lambda i, j, ri: links[pl.ds((comp(d, i, j, ri) * 2 + 1) * ROWS + row, 8), :])

    across = read(0, 2)
    for m in (1, 2, 3):
        side = read(m, 2)
        half = [[entry(across, side, i, k, True, False) for k in range(3)] for i in range(2)]
        if m == 2:
            last = [[(roll_z(v[0], 1), roll_z(v[1], 1)) for v in row] for row in across]
        else:
            last = read(0, 3 if m == 1 else 4)
        for i in range(2):
            for j in range(3):
                value = entry(half, last, i, j)
                for ri in range(2):
                    out = jnp.where(first_rows(), value[ri], half[i][j][ri]) if m == 1 else value[ri]
                    up[pl.ds(((m - 1) * 12 + (i * 3 + j) * 2 + ri) * 8, 8), :] = out


def pack_corners_body(ynext, yprev, up, down):
    for q in range(12):
        up[pl.ds(q * 4, 4), :] = ynext[pl.ds(q * 8 + 4, 4), :]
        down[pl.ds(q * 4, 4), :] = yprev[pl.ds((12 + q) * 8, 4), :]


def pack_lambda_down_body(lam, yprev, after, down):
    for c in range(24):
        down[pl.ds(c * 8, 8), :] = lam[pl.ds((c + NA) * 16, 8), :]
    for k in range(NA):
        down[pl.ds(192 + k * 4, 4), :] = yprev[pl.ds((NA + k) * 8, 4), :]


def two_rows(read):
    m = [[(read((i * 3 + j) * 2), read((i * 3 + j) * 2 + 1)) for j in range(3)] for i in range(2)]
    return m + [third_row(m)]


def put(write, m):
    for i in range(3):
        for j in range(3):
            for ri in range(2):
                write((i * 3 + j) * 2 + ri, m[i][j][ri])


def roll_z(v, by):
    return pltpu.roll(v, (128 - by) % 128, 1)


def fill_y(bufs, n, dirs_p, dirs_m):
    for x in (1, 2):
        for d in range(4):
            for k in range(n):
                at = place(d * n + k, x)
                if d in dirs_p:
                    bufs[YP][pl.ds(at, 6, stride=2), :] = bufs[O][pl.ds(at + 1, 6, stride=2), :]
                if d in dirs_m:
                    bufs[YM][pl.ds(at + 1, 6, stride=2), :] = bufs[O][pl.ds(at, 6, stride=2), :]


def fill_z(bufs, n):
    for d in range(4):
        for k in range(n):
            c = d * n + k
            for x in (1, 2):
                at = place(c, x)
                zp, zm = bufs[ZP], bufs[ZM]
                if d != 2:
                    zp[pl.ds(at + 2, 8), :] = roll_z(bufs[O][pl.ds(at + 2, 8), :], 1)
                if d == 3:
                    zp[pl.ds(at, 2), :] = roll_z(bufs[O][pl.ds(at, 2), :], 1)
                zm[pl.ds(at + 2, 8), :] = roll_z(bufs[O][pl.ds(at + 2, 8), :], -1)
                if d == 2:
                    zm[pl.ds(at + 10, 2), :] = roll_z(bufs[O][pl.ds(at + 10, 2), :], -1)


def fill_mixed(bufs, n):
    for k in range(n):
        for x in (1, 2):
            bufs[ZPYM][pl.ds(place(k, x) + 2, 8), :] = roll_z(bufs[YM][pl.ds(place(n + k, x) + 2, 8), :], 1)
            bufs[ZMYP][pl.ds(place(k, x) + 2, 8), :] = roll_z(bufs[YP][pl.ds(place(2 * n + k, x) + 2, 8), :], -1)


def fill_high(bufs, n):
    for k in range(n):
        high, side = place(2 * n + k, 3), place(n + k, 3)
        bufs[ZM][pl.ds(high + 2, 8), :] = roll_z(bufs[O][pl.ds(high + 2, 8), :], -1)
        bufs[YM][pl.ds(side + 3, 4, stride=2), :] = bufs[O][pl.ds(side + 2, 4, stride=2), :]


def fill_links_local(links, bufs):
    for c in range(72):
        for x in range(2):
            source, to = (c * 2 + x) * ROWS, place(c, x + 1)
            bufs[O][pl.ds(to, 8), :] = links[pl.ds(source, 8), :]
            bufs[O][pl.ds(to + 8, 4), :] = links[pl.ds(source + 8, 4), :]
    fill_y(bufs, NC, (0, 2, 3), (0, 1, 2, 3))
    fill_z(bufs, NC)


def fill_links_y(ynext, yprev, bufs):
    for d in range(4):
        for source, buf, off in ((ynext, YP, 3), (yprev, YM, 2)):
            if buf == YP and d == 1:
                continue
            slot = DOWN_Y.index(d) if buf == YP else d
            m = two_rows(lambda q: source[pl.ds((slot * 12 + q) * 8, 8), :])

            def write(q, v):
                for x in range(2):
                    bufs[buf][pl.ds(place(d * NC + q, x + 1) + off, 4, stride=2), :] = v[4 * x : 4 * x + 4]

            put(write, m)
    for source, buf, d, row, at in ((ynext, YP, 3, 1, 288), (yprev, YM, 1, 10, 384)):
        m = two_rows(lambda q: source[pl.ds(at + q * 2, 2), :])

        def write_row(q, v):
            for x in range(2):
                bufs[buf][pl.ds(place(d * NC + q, x + 1) + row, 1), :] = v[x : x + 1]

        put(write_row, m)
    fill_mixed(bufs, NC)


def fill_links_next(xnext, bufs):
    for d in (1, 2, 3):
        m = two_rows(lambda q: xnext[pl.ds(((d - 1) * 12 + q) * 8, 8), :])

        def write(q, v):
            bufs[O][pl.ds(place(d * NC + q, 3) + 2, 8), :] = v

        put(write, m)
    m = two_rows(lambda q: xnext[pl.ds(288 + q * 2, 2), :])

    def write_edge(q, v):
        bufs[O][pl.ds(place(3 * NC + q, 3), 2), :] = v

    put(write_edge, m)
    fill_high(bufs, NC)


def fill_corner(corner, buf, d, xe, off, bufs):
    m = two_rows(lambda q: corner[pl.ds(q * 4, 4), :])

    def write_corner(q, v):
        bufs[buf][pl.ds(place(d * NC + q, xe) + off, 4, stride=2), :] = v

    put(write_corner, m)


def take_staples(xprev, bufs, ready):
    for m in (1, 2, 3):
        staple = two_rows(lambda q: xprev[pl.ds(((m - 1) * 12 + q) * 8, 8), :])
        if m == 1:
            whole = mm(staple, link(bufs, 0, step((0, -1), (1, 1)), 0))
            staple = [
                [tuple(jnp.where(first_rows(), staple[i][j][ri], whole[i][j][ri]) for ri in range(2)) for j in range(3)]
                for i in range(3)
            ]
        for i in range(3):
            for j in range(3):
                for ri in range(2):
                    ready[pl.ds(comp(m - 1, i, j, ri) * 8, 8), :] = staple[i][j][ri]


def ready_staple(ready, m):
    return load_matrix(lambda i, j, ri: ready[pl.ds(comp(m - 1, i, j, ri) * 8, 8), :])


def fill_lambda_local(lam, bufs):
    zero = jnp.zeros((2, 128), jnp.float32)
    for c in range(32):
        for x in range(2):
            to = place(c, x + 1)
            bufs[O][pl.ds(to + 2, 8), :] = lam[pl.ds((c * 2 + x) * 8, 8), :]
            bufs[O][pl.ds(to, 2), :] = zero
            bufs[O][pl.ds(to + 10, 2), :] = zero
    fill_y(bufs, NA, (0, 2, 3), (0, 1, 2, 3))
    fill_z(bufs, NA)


def fill_lambda_y(ynext, yprev, bufs):
    zero = jnp.zeros((1, 128), jnp.float32)
    for d in range(4):
        for k in range(NA):
            for x in range(2):
                to = place(d * NA + k, x + 1)
                if d != 1:
                    source = pl.ds((DOWN_Y.index(d) * NA + k) * 8 + x * 4, 4)
                    bufs[YP][pl.ds(to + 3, 4, stride=2), :] = ynext[source, :]
                bufs[YM][pl.ds(to + 2, 4, stride=2), :] = yprev[pl.ds((d * NA + k) * 8 + x * 4, 4), :]
                if d == 3:
                    bufs[YP][pl.ds(to + 1, 1), :] = zero
                if d == 1:
                    bufs[YM][pl.ds(to + 10, 1), :] = zero
    fill_mixed(bufs, NA)


def fill_lambda_next(xnext, bufs):
    zero = jnp.zeros((2, 128), jnp.float32)
    for c in range(24):
        bufs[O][pl.ds(place(NA + c, 3) + 2, 8), :] = xnext[pl.ds(c * 8, 8), :]
    for k in range(NA):
        bufs[O][pl.ds(place(3 * NA + k, 3), 2), :] = zero
        bufs[YM][pl.ds(place(NA + k, 3) + 2, 4, stride=2), :] = xnext[pl.ds(192 + k * 4, 4), :]
    fill_high(bufs, NA)


def step(*signed):
    vector = [0, 0, 0, 0]
    for which, sign in signed:
        vector[which] += sign
    return vector


def where(bufs, n, d, offset, x):
    key = buffer_of[(offset[1], offset[2])]
    row = 2 + 2 * offset[3]
    dd = d - base_dir.get(key, 0)
    shift = (x + 1 + offset[0]) * ROWS

    def read(k):
        return bufs[key][pl.ds(place(dd * n + k, 0) + row + shift, 8), :]

    return read


def link(bufs, d, offset, x):
    read = where(bufs, NC, d, offset, x)
    return load_matrix(lambda i, j, ri: read((i * 3 + j) * 2 + ri))


def lam_at(bufs, d, offset, x):
    read = where(bufs, NA, d, offset, x)
    return unpack8([read(k) for k in range(NA)])


def exponent_force(v, m, target, clow):
    a = v[:3]
    off = [(v[3 + 2 * k], v[4 + 2 * k]) for k in range(3)]
    norm = [r * r + s * s for r, s in off]
    sd = [
        -(a[0] * a[0] + norm[0] + norm[1]),
        -(a[1] * a[1] + norm[0] + norm[2]),
        -(a[2] * a[2] + norm[1] + norm[2]),
    ]
    (r0, s0), (r1, s1), (r2, s2) = off
    so = [
        (a[2] * s0 - (r1 * r2 + s1 * s2), -a[2] * r0 - (s1 * r2 - r1 * s2)),
        (a[1] * s1 + (r0 * r2 - s0 * s2), -a[1] * r1 + (r0 * s2 + s0 * r2)),
        (a[0] * s2 - (r0 * r1 + s0 * s1), -a[0] * r2 - (r0 * s1 - s0 * r1)),
    ]
    c = 0.5 * (sd[0] + sd[1] + sd[2])
    cross = [off[k][1] * so[k][0] - off[k][0] * so[k][1] for k in range(3)]
    dd = (a[0] * sd[0] + a[1] * sd[1] + a[2] * sd[2] + 2.0 * (cross[0] + cross[1] + cross[2])) * (1.0 / 3.0)
    p0r = 1.0 - dd * dd * (1.0 / 720.0)
    p0i = dd * (1.0 / 6.0 + c * (1.0 / 120.0))
    p1r = 1.0 + c * (1.0 / 6.0 + c * (1.0 / 120.0))
    p1i = dd * (1.0 / 24.0 + c * (1.0 / 360.0))
    p2r = 0.5 + c * (1.0 / 24.0 + c * (1.0 / 720.0))
    p2i = dd * (1.0 / 120.0)
    hd = [m[i][i][0] for i in range(3)]
    kd = [m[i][i][1] for i in range(3)]
    ho = [(0.5 * (m[i][j][0] + m[j][i][0]), 0.5 * (m[i][j][1] - m[j][i][1])) for i, j in UPPER]
    ko = [(0.5 * (m[i][j][0] - m[j][i][0]), 0.5 * (m[i][j][1] + m[j][i][1])) for i, j in UPPER]
    t0r = hd[0] + hd[1] + hd[2]
    t0i = -(kd[0] + kd[1] + kd[2])

    def dots(x, y, xo, yo):
        diag = x[0] * y[0] + x[1] * y[1] + x[2] * y[2]
        rest = [xo[k][0] * yo[k][0] + xo[k][1] * yo[k][1] for k in range(3)]
        return diag + 2.0 * (rest[0] + rest[1] + rest[2])

    def crossed(x, y, xo, yo):
        diag = x[0] * y[0] + x[1] * y[1] + x[2] * y[2]
        rest = [yo[k][1] * xo[k][0] - yo[k][0] * xo[k][1] for k in range(3)]
        return diag + 2.0 * (rest[0] + rest[1] + rest[2])

    t1r = dots(kd, a, ko, off)
    t1i = crossed(hd, a, ho, off)
    t2r = dots(hd, sd, ho, so)
    t2i = -crossed(sd, kd, so, ko)
    by_c = (
        t1r * (1.0 / 6.0 + c * (1.0 / 60.0))
        + t2r * (1.0 / 24.0 + c * (1.0 / 360.0))
        - dd * (t0i * (1.0 / 120.0) + t1i * (1.0 / 360.0))
    )
    by_d = -(
        dd * t0r * (1.0 / 360.0)
        + t0i * (1.0 / 6.0 + c * (1.0 / 120.0))
        + t1i * (1.0 / 24.0 + c * (1.0 / 360.0))
        + t2i * (1.0 / 120.0)
    )
    herm = [[None] * 3 for _ in range(3)]
    for i in range(3):
        herm[i][i] = (-(p2r * hd[i] + p2i * kd[i]), None)
    for k, (i, j) in enumerate(UPPER):
        re = -(p2r * ho[k][0] + p2i * ko[k][1])
        im = p2i * ko[k][0] - p2r * ho[k][1]
        herm[i][j] = (re, im)
        herm[j][i] = (re, -im)
    amat = anti(v)
    g = skew(mm(amat, herm))
    lam = [p1r * kd[i] - p1i * hd[i] + g[i] - by_c * a[i] + by_d * sd[i] for i in range(3)]
    for k in range(3):
        lam.append(p1r * ko[k][0] + p1i * ho[k][1] + g[3 + 2 * k] - by_c * off[k][0] - by_d * so[k][1])
        lam.append(p1r * ko[k][1] - p1i * ho[k][0] + g[4 + 2 * k] - by_c * off[k][1] + by_d * so[k][0])
    mean = (lam[0] + lam[1] + lam[2]) * (1.0 / 3.0)
    lam = [smear_weight * (lam[i] - mean) for i in range(3)] + [smear_weight * lam[k] for k in range(3, 9)]
    edag = [[None] * 3 for _ in range(3)]
    for i in range(3):
        edag[i][i] = (p0r - p1i * a[i] + p2r * sd[i], -(p0i + p1r * a[i] + p2i * sd[i]))
    for k, (i, j) in enumerate(UPPER):
        r, s = off[k]
        sr, si = so[k]
        edag[i][j] = (
            (p2r * sr - p1i * s) + (p2i * si - p1r * r),
            (p1i * r - p2i * sr) + (p2r * si - p1r * s),
        )
        edag[j][i] = (
            (p2r * sr - p1i * s) - (p2i * si - p1r * r),
            -(p1i * r + p2i * sr) - (p2r * si + p1r * s),
        )
    direct = msub(mm(edag, target), mm(anti(lam), clow))
    return lam, direct


def plane_fields(m, n):
    here = step()
    return [(m, here), (n, here), (n, step((m, 1))), (m, step((n, 1)))]


def lower_fields(m, n):
    back = step((n, -1))
    return [(n, back), (m, back), (n, step((n, -1), (m, 1)))]


def level(fields, x):
    found = 0
    for _, offset in fields:
        if x + offset[0] == -1:
            found = 3
        elif x + offset[0] == 2:
            found = max(found, 3 if offset[1] else 2)
        elif offset[1]:
            found = max(found, 1)
    return found


LOWERS = [(m, n) for m in range(4) for n in range(4) if n != m]


def items(wanted):
    planes = [(p, m, n, x) for x in range(2) for p, (m, n) in enumerate(PAIRS) if level(plane_fields(m, n), x) == wanted]
    lowers = [(m, n, x) for x in range(2) for m, n in LOWERS if level(lower_fields(m, n), x) == wanted]
    return planes, lowers


def cells(n, k, x):
    return pl.ds((n + k) * 16 + x * 8, 8)


def load_cells(ref, n, x):
    return load_matrix(lambda i, j, ri: ref[cells(n, (i * 3 + j) * 2 + ri, x), :])


def store_cells(ref, n, x, m):
    for i in range(3):
        for j in range(3):
            for ri in range(2):
                ref[cells(n, (i * 3 + j) * 2 + ri, x), :] = m[i][j][ri]


def take_incoming(incoming, inner):
    for c in range(144):
        inner[pl.ds(c * 8, 4, stride=2), :] = incoming[pl.ds(c * 8, 4), :]
        inner[pl.ds(c * 8 + 1, 4, stride=2), :] = incoming[pl.ds(c * 8 + 4, 4), :]


def forward_items(wanted, bufs, omega, loops, low, ready=None):
    planes, lowers = items(wanted)
    begun = {(m, x) for w in range(wanted) for m, _, x in items(w)[1]}
    for p, m, n, x in planes:
        a, d, b, c = [link(bufs, which, offset, x) for which, offset in plane_fields(m, n)]
        loop = mm(mm(a, b), mm(d, c), False, True)
        store_cells(omega, p * 18, x, loop)
        for k, v in enumerate(skew(loop)):
            loops[cells(p * 9, k, x), :] = v
    for m in range(4):
        for x in range(2):
            value = load_cells(low, m * 18, x) if (m, x) in begun else None
            mine = [n for mm_, n, xx in lowers if (mm_, xx) == (m, x)]
            if not mine:
                continue
            for n in mine:
                if n == 0 and x == 0:
                    term = ready_staple(ready, m)
                else:
                    e, g, h = [link(bufs, which, offset, x) for which, offset in lower_fields(m, n)]
                    term = mm(mm(e, g, True, False), h)
                value = term if value is None else madd(value, term)
            store_cells(low, m * 18, x, value)


def target_products(bufs, inner, moved):
    for x in range(2):
        for m in range(4):
            target = load_cells(inner, m * 18, x)
            store_cells(moved, m * 18, x, mm(target, link(bufs, m, step(), x), False, True))


def finish_forward(bufs, inner, moved, loops, low, lam_out, direct):
    for x in range(2):
        for m in range(4):
            u = link(bufs, m, step(), x)
            below = load_cells(low, m * 18, x)
            v = skew_product(below, u, True)
            for p, (f, s) in enumerate(PAIRS):
                if m == f:
                    v = [v[k] - loops[cells(p * 9, k, x), :] for k in range(9)]
                if m == s:
                    v = [v[k] + loops[cells(p * 9, k, x), :] for k in range(9)]
            mean = (v[0] + v[1] + v[2]) * (1.0 / 3.0)
            v = [(0.5 * smear_weight) * (v[k] - mean) for k in range(3)] + [
                (0.5 * smear_weight) * v[k] for k in range(3, 9)
            ]
            lam, force = exponent_force(v, load_cells(moved, m * 18, x), load_cells(inner, m * 18, x), below)
            for k, v in enumerate(lam[:2] + lam[3:]):
                lam_out[cells(m * NA, k, x), :] = v
            store_cells(direct, m * 18, x, force)


def backward_items(wanted, bufs, lams, omega, sums, acc, ready=None, xprev=None):
    planes, lowers = items(wanted)
    begun = {(d, x) for w in range(wanted) for _, m, n, x in items(w)[0] for d in (m, n)}

    def gather(d, x, m):
        store_cells(sums, d * 18, x, madd(load_cells(sums, d * 18, x), m) if (d, x) in begun else m)
        begun.add((d, x))

    for p, m, n, x in planes:
        fields = plane_fields(m, n)
        a, d = [link(bufs, which, offset, x) for which, offset in fields[:2]]
        la, ld, lb, lc = [lam_at(lams, which, offset, x) for which, offset in fields]
        lb, lc = carried(a, lb), carried(d, lc)
        loop = load_cells(omega, p * 18, x)
        z = [ld[k] - la[k] for k in range(9)]
        first = anti([z[k] + lc[k] for k in range(9)])
        second = anti([lb[k] - z[k] for k in range(9)])
        gather(m, x, msub(mm(first, loop, False, True), mm(loop, anti(lb), True, False)))
        gather(n, x, msub(mm(second, loop), mm(loop, anti(lc))))
    for m in range(4):
        for x in range(2):
            mine = [n for mm_, n, xx in lowers if (mm_, xx) == (m, x)]
            if not mine:
                continue
            force = load_cells(acc, m * 18, x)
            for n in mine:
                if n == 0 and x == 0:
                    y = unpack8([xprev[pl.ds(((m - 1) * NA + k) * 8, 8), :] for k in range(NA)])
                    force = madd(force, mm(anti(y), ready_staple(ready, m)))
                    continue
                fields = lower_fields(m, n)
                e, g, h = [link(bufs, which, offset, x) for which, offset in fields]
                le, lg, lh = [lam_at(lams, which, offset, x) for which, offset in fields]
                inside = madd(mm(anti([lg[k] - le[k] for k in range(9)]), g), mm(g, anti(lh)))
                force = madd(force, mm(mm(e, inside, True, False), h))
            store_cells(acc, m * 18, x, force)


def finish_backward(bufs, sums, acc, out):
    for x in range(2):
        for m in range(4):
            f = load_cells(sums, m * 18, x)
            force = madd(mm(f, link(bufs, m, step(), x)), load_cells(acc, m * 18, x))
            store_cells(acc, m * 18, x, force)
            for k in range(18):
                at = ((m * 18 + k) * 2 + x) * 8
                out[pl.ds(at, 4), :] = acc[pl.ds(at, 4, stride=2), :]
                out[pl.ds(at + 4, 4), :] = acc[pl.ds(at + 1, 4, stride=2), :]


def links_local_body(*refs):
    links = refs[0]
    bufs, (omega, loops, low) = refs[1:8], refs[8:]
    fill_links_local(links, bufs)
    forward_items(0, bufs, omega, loops, low)


def links_y_body(*refs):
    ynext, yprev, incoming = refs[:3]
    bufs, (omega, loops, low, inner, moved) = refs[13:20], refs[20:]
    fill_links_y(ynext, yprev, bufs)
    take_incoming(incoming, inner)
    forward_items(1, bufs, omega, loops, low)
    target_products(bufs, inner, moved)


def links_next_body(*refs):
    xnext = refs[0]
    bufs, (omega, loops, low) = refs[11:18], refs[18:]
    fill_links_next(xnext, bufs)
    forward_items(2, bufs, omega, loops, low)


def links_x_body(*refs):
    cnext, xprev, cprev, inner, moved = refs[:5]
    bufs, (omega, loops, low, lam, direct, up, down, ready) = refs[15:22], refs[22:]
    fill_corner(cnext, YM, 1, 3, 2, bufs)
    fill_corner(cprev, YP, 0, 0, 3, bufs)
    take_staples(xprev, bufs, ready)
    forward_items(3, bufs, omega, loops, low, ready)
    finish_forward(bufs, inner, moved, loops, low, lam, direct)

    def reader(row):
        return lambda d, q, x: lam[pl.ds(((d * NA + q) * 2 + x) * 8 + row, 4, stride=2), :]

    pack_y(up, down, NA, reader(1), reader(0))


def lambda_local_body(*refs):
    bufs, (omega, lam) = refs[:7], refs[7:9]
    acc, lams, sums = refs[10], refs[11:18], refs[18]
    fill_lambda_local(lam, lams)
    backward_items(0, bufs, lams, omega, sums, acc)


def lambda_up_body(*refs):
    ynext, yprev, links = refs[:3]
    lams, up = refs[10:17], refs[17]
    fill_lambda_y(ynext, yprev, lams)
    here = step()
    for m in (1, 2, 3):
        a, d = link([links], 0, here, 1), link([links], m, here, 1)
        la, ld, lc = lam_at(lams, 0, here, 1), lam_at(lams, m, here, 1), lam_at(lams, 0, step((m, 1)), 1)
        lc = carried(d, lc)
        y = carried_back(a, [ld[k] - la[k] + lc[k] for k in range(9)])
        for k, v in enumerate(y[:2] + y[3:]):
            up[pl.ds(((m - 1) * NA + k) * 8, 8), :] = v


def lambda_y_body(*refs):
    bufs, omega, lams = refs[:7], refs[7], refs[8:15]
    acc, sums = refs[17:]
    backward_items(1, bufs, lams, omega, sums, acc)


def lambda_x_body(*refs):
    bufs, (omega, ready, xnext, xprev) = refs[:7], refs[7:11]
    out, acc, lams, sums = refs[20], refs[21], refs[22:29], refs[29]
    fill_lambda_next(xnext, lams)
    backward_items(2, bufs, lams, omega, sums, acc)
    backward_items(3, bufs, lams, omega, sums, acc, ready, xprev)
    finish_backward(bufs, sums, acc, out)


def rows(n):
    return jax.ShapeDtypeStruct((n, 128), jnp.float32)


def buffer_rows(n):
    return [(n if key in base_dir else 4 * n) * 4 * ROWS for key in range(7)]


def call(body, args, outs, kept=(), cost=0, first=0):
    shapes = [rows(n) for n in outs]
    shapes[first:first] = [rows(a.shape[0]) for a in kept]
    return pl.pallas_call(
        body,
        out_shape=tuple(shapes),
        in_specs=[pl.BlockSpec(memory_space=pltpu.VMEM)] * (len(args) + len(kept)),
        out_specs=(pl.BlockSpec(memory_space=pltpu.VMEM),) * len(shapes),
        input_output_aliases={len(args) + k: first + k for k in range(len(kept))},
        cost_estimate=pl.CostEstimate(flops=cost, bytes_accessed=0, transcendentals=0) if cost else None,
        compiler_params=pltpu.CompilerParams(vmem_limit_bytes=VM),
    )(*args, *kept)


def shifted(shard, axis, by):
    length = lax.axis_size(axis)
    return lax.ppermute(shard, axis, [(i, (i + by) % length) for i in range(length)])


def body(links, incoming):
    links = jnp.transpose(links, (0, 1, 2, 3, 4, 6, 5, 7)).reshape(144 * ROWS, 128)
    shape = incoming.shape
    incoming = incoming.reshape(1152, 128)
    xdown, yup, ydown = call(pack_first_body, (links,), (312, 408, 312))
    xnext = shifted(xdown, "gx", -1)
    yprev, ynext = shifted(yup, "gy", 1), shifted(ydown, "gy", -1)
    (xup,) = call(pack_up_body, (links,), (288,))
    xprev = shifted(xup, "gx", 1)
    cup, cdown = call(pack_corners_body, (ynext, yprev), (48, 48))
    cprev, cnext = shifted(cup, "gx", 1), shifted(cdown, "gx", -1)
    kept = call(links_local_body, (links,), buffer_rows(NC) + [1728, 864, 1152])
    *kept, inner, moved = call(links_y_body, (ynext, yprev, incoming), (1152, 1152), kept)
    kept = call(links_next_body, (xnext,), (), kept)
    r = call(links_x_body, (cnext, xprev, cprev, inner, moved), (512, 1152, 256, 192, 432), kept)
    bufs, omega, (lam, acc, yup, ydown, ready) = r[:7], r[7], r[10:]
    yprev, ynext = shifted(yup, "gy", 1), shifted(ydown, "gy", -1)
    acc, *lams, sums = call(lambda_local_body, (*bufs, omega, lam), buffer_rows(NA) + [1152], (acc,))
    (xdown,) = call(pack_lambda_down_body, (lam, yprev, sums), (224,))
    xnext = shifted(xdown, "gx", -1)
    *lams, xup = call(lambda_up_body, (ynext, yprev, bufs[O]), (192,), lams)
    xprev = shifted(xup, "gx", 1)
    acc, sums = call(lambda_y_body, (*bufs, omega, *lams), (), (acc, sums))
    out = call(lambda_x_body, (*bufs, omega, ready, xnext, xprev), (1152,), (acc, *lams, sums), first=1)[0]
    return out.reshape(shape)


def solution(mesh):
    placed = P(None, None, None, None, "gx", "gy", None, None)
    return jax.shard_map(body, mesh=mesh, in_specs=(placed, placed), out_specs=placed, check_vma=False)
```

```python
import jax
import jax.numpy as jnp
from jax import lax
from jax.experimental import pallas as pl
from jax.experimental.pallas import tpu as pltpu
from jax.sharding import PartitionSpec as P

smear_weight = 0.2
NC, NA = 18, 8
ROWS = 12
VM = 8 * 2**20
O, YP, YM, ZP, ZM, ZPYM, ZMYP = range(7)
buffer_of = {(0, 0): O, (1, 0): YP, (-1, 0): YM, (0, 1): ZP, (0, -1): ZM, (-1, 1): ZPYM, (1, -1): ZMYP}
base_dir = {ZPYM: 1, ZMYP: 2}
PAIRS = [(m, n) for m in range(4) for n in range(m + 1, 4)]
DOWN_Y = [0, 2, 3]
UPPER = [(0, 1), (0, 2), (1, 2)]


def total(terms):
    plus = [a * b for s, a, b in terms if s > 0]
    minus = [a * b for s, a, b in terms if s < 0]
    if not plus:
        value = -minus[0]
        minus = minus[1:]
    else:
        value = plus[0]
        for other in plus[1:]:
            value = value + other
    for other in minus:
        value = value - other
    return value


def entry(left, right, i, k, dag_left=False, dag_right=False, want=(True, True)):
    real, imag = [], []
    for j in range(3):
        ar, ai = left[j][i] if dag_left else left[i][j]
        br, bi = right[k][j] if dag_right else right[j][k]
        sa = -1 if dag_left else 1
        sb = -1 if dag_right else 1
        if ar is not None and br is not None:
            real.append((1, ar, br))
        if ai is not None and bi is not None:
            real.append((-sa * sb, ai, bi))
        if ar is not None and bi is not None:
            imag.append((sb, ar, bi))
        if ai is not None and br is not None:
            imag.append((sa, ai, br))
    return (total(real) if want[0] else None, total(imag) if want[1] else None)


def mm(left, right, dag_left=False, dag_right=False):
    return [[entry(left, right, i, k, dag_left, dag_right) for k in range(3)] for i in range(3)]


def madd(a, b):
    return [[(a[i][j][0] + b[i][j][0], a[i][j][1] + b[i][j][1]) for j in range(3)] for i in range(3)]


def msub(a, b):
    return [[(a[i][j][0] - b[i][j][0], a[i][j][1] - b[i][j][1]) for j in range(3)] for i in range(3)]


def skew(m):
    out = [m[i][i][1] + m[i][i][1] for i in range(3)]
    for i, j in UPPER:
        out += [m[i][j][0] - m[j][i][0], m[i][j][1] + m[j][i][1]]
    return out


def skew_product(left, right, dag_right=False):
    return skew(mm(left, right, False, dag_right))


def unpack8(v):
    return [v[0], v[1], -v[0] - v[1]] + list(v[2:])


def anti(v):
    out = [[None] * 3 for _ in range(3)]
    for i in range(3):
        out[i][i] = (None, v[i])
    for k, (i, j) in enumerate(UPPER):
        r, s = v[3 + 2 * k], v[4 + 2 * k]
        out[i][j] = (r, s)
        out[j][i] = (-r, s)
    return out


def carried(u, v):
    half = mm(u, anti(v))
    diag = [entry(half, u, i, i, False, True, (False, True))[1] for i in range(2)]
    out = [diag[0], diag[1], -diag[0] - diag[1]]
    for i, j in UPPER:
        out += list(entry(half, u, i, j, False, True))
    return out


def carried_back(u, v):
    half = mm(u, anti(v), True, False)
    diag = [entry(half, u, i, i, False, False, (False, True))[1] for i in range(2)]
    out = [diag[0], diag[1], -diag[0] - diag[1]]
    for i, j in UPPER:
        out += list(entry(half, u, i, j))
    return out


def first_rows():
    return lax.broadcasted_iota(jnp.int32, (8, 128), 0) % 2 == 0


def third_row(m):
    row = []
    for j in range(3):
        p, q = (j + 1) % 3, (j + 2) % 3
        ar, ai = m[0][p]
        br, bi = m[1][q]
        cr, ci = m[0][q]
        dr, di = m[1][p]
        row.append(
            (ar * br - ai * bi - cr * dr + ci * di, cr * di + ci * dr - ar * bi - ai * br)
        )
    return row


def comp(d, i, j, ri):
    return ((d * 3 + i) * 3 + j) * 2 + ri


def place(c, xe):
    return (c * 4 + xe) * ROWS


def load_matrix(read):
    return [[(read(i, j, 0), read(i, j, 1)) for j in range(3)] for i in range(3)]


def pack_y(up, down, n, read_up, read_down):
    for d in range(4):
        for q in range(n):
            for x in range(2):
                up[pl.ds(((d * n + q) * 2 + x) * 4, 4), :] = read_up(d, q, x)
                if d != 1:
                    down[pl.ds(((DOWN_Y.index(d) * n + q) * 2 + x) * 4, 4), :] = read_down(d, q, x)


def pack_first_body(links, xdown, yup, ydown, cdown, cup):
    def reader(row):
        return lambda d, q, x: links[pl.ds(((d * 18 + q) * 2 + x) * ROWS + row, 4, stride=2), :]

    pack_y(yup, ydown, 12, reader(3), reader(2))
    for q in range(12):
        for x in range(2):
            yup[pl.ds(384 + q * 2 + x, 1), :] = links[pl.ds(((18 + q) * 2 + x) * ROWS + 11, 1), :]
            ydown[pl.ds(288 + q * 2 + x, 1), :] = links[pl.ds(((54 + q) * 2 + x) * ROWS, 1), :]
        for d in range(1, 4):
            xdown[pl.ds(((d - 1) * 12 + q) * 8, 8), :] = links[pl.ds((d * 18 + q) * 2 * ROWS + 2, 8), :]
        xdown[pl.ds(288 + q * 2, 2), :] = links[pl.ds((54 + q) * 2 * ROWS, 2), :]
        cdown[pl.ds(q * 4, 4), :] = links[pl.ds((18 + q) * 2 * ROWS + 3, 4, stride=2), :]
        cup[pl.ds(q * 4, 4), :] = links[pl.ds((q * 2 + 1) * ROWS + 2, 4, stride=2), :]


def pack_up_body(links, up):
    def read(d, row):
        return load_matrix(lambda i, j, ri: links[pl.ds((comp(d, i, j, ri) * 2 + 1) * ROWS + row, 8), :])

    across = read(0, 2)
    for m in (1, 2, 3):
        side = read(m, 2)
        half = [[entry(across, side, i, k, True, False) for k in range(3)] for i in range(2)]
        if m == 2:
            last = [[(roll_z(v[0], 1), roll_z(v[1], 1)) for v in row] for row in across]
        else:
            last = read(0, 3 if m == 1 else 4)
        for i in range(2):
            for j in range(3):
                value = entry(half, last, i, j)
                for ri in range(2):
                    out = jnp.where(first_rows(), value[ri], half[i][j][ri]) if m == 1 else value[ri]
                    up[pl.ds(((m - 1) * 12 + (i * 3 + j) * 2 + ri) * 8, 8), :] = out


def pack_lambda_down_body(lam, yprev, after, down):
    for c in range(24):
        down[pl.ds(c * 8, 8), :] = lam[pl.ds((c + NA) * 16, 8), :]
    for k in range(NA):
        down[pl.ds(192 + k * 4, 4), :] = yprev[pl.ds((NA + k) * 8, 4), :]


def two_rows(read):
    m = [[(read((i * 3 + j) * 2), read((i * 3 + j) * 2 + 1)) for j in range(3)] for i in range(2)]
    return m + [third_row(m)]


def put(write, m):
    for i in range(3):
        for j in range(3):
            for ri in range(2):
                write((i * 3 + j) * 2 + ri, m[i][j][ri])


def roll_z(v, by):
    return pltpu.roll(v, (128 - by) % 128, 1)


def fill_y(bufs, n, dirs_p, dirs_m):
    for x in (1, 2):
        for d in range(4):
            for k in range(n):
                at = place(d * n + k, x)
                if d in dirs_p:
                    bufs[YP][pl.ds(at, 6, stride=2), :] = bufs[O][pl.ds(at + 1, 6, stride=2), :]
                if d in dirs_m:
                    bufs[YM][pl.ds(at + 1, 6, stride=2), :] = bufs[O][pl.ds(at, 6, stride=2), :]


def fill_z(bufs, n):
    for d in range(4):
        for k in range(n):
            c = d * n + k
            for x in (1, 2):
                at = place(c, x)
                zp, zm = bufs[ZP], bufs[ZM]
                if d != 2:
                    zp[pl.ds(at + 2, 8), :] = roll_z(bufs[O][pl.ds(at + 2, 8), :], 1)
                if d == 3:
                    zp[pl.ds(at, 2), :] = roll_z(bufs[O][pl.ds(at, 2), :], 1)
                zm[pl.ds(at + 2, 8), :] = roll_z(bufs[O][pl.ds(at + 2, 8), :], -1)
                if d == 2:
                    zm[pl.ds(at + 10, 2), :] = roll_z(bufs[O][pl.ds(at + 10, 2), :], -1)


def fill_mixed(bufs, n):
    for k in range(n):
        for x in (1, 2):
            bufs[ZPYM][pl.ds(place(k, x) + 2, 8), :] = roll_z(bufs[YM][pl.ds(place(n + k, x) + 2, 8), :], 1)
            bufs[ZMYP][pl.ds(place(k, x) + 2, 8), :] = roll_z(bufs[YP][pl.ds(place(2 * n + k, x) + 2, 8), :], -1)


def fill_high(bufs, n):
    for k in range(n):
        high, side = place(2 * n + k, 3), place(n + k, 3)
        bufs[ZM][pl.ds(high + 2, 8), :] = roll_z(bufs[O][pl.ds(high + 2, 8), :], -1)
        bufs[YM][pl.ds(side + 3, 4, stride=2), :] = bufs[O][pl.ds(side + 2, 4, stride=2), :]


def fill_links_local(links, bufs):
    for c in range(72):
        for x in range(2):
            source, to = (c * 2 + x) * ROWS, place(c, x + 1)
            bufs[O][pl.ds(to, 8), :] = links[pl.ds(source, 8), :]
            bufs[O][pl.ds(to + 8, 4), :] = links[pl.ds(source + 8, 4), :]
    fill_y(bufs, NC, (0, 2, 3), (0, 1, 2, 3))
    fill_z(bufs, NC)


def fill_links_y(ynext, yprev, bufs):
    for d in range(4):
        for source, buf, off in ((ynext, YP, 3), (yprev, YM, 2)):
            if buf == YP and d == 1:
                continue
            slot = DOWN_Y.index(d) if buf == YP else d
            m = two_rows(lambda q: source[pl.ds((slot * 12 + q) * 8, 8), :])

            def write(q, v):
                for x in range(2):
                    bufs[buf][pl.ds(place(d * NC + q, x + 1) + off, 4, stride=2), :] = v[4 * x : 4 * x + 4]

            put(write, m)
    for source, buf, d, row, at in ((ynext, YP, 3, 1, 288), (yprev, YM, 1, 10, 384)):
        m = two_rows(lambda q: source[pl.ds(at + q * 2, 2), :])

        def write_row(q, v):
            for x in range(2):
                bufs[buf][pl.ds(place(d * NC + q, x + 1) + row, 1), :] = v[x : x + 1]

        put(write_row, m)
    fill_mixed(bufs, NC)


def fill_links_next(xnext, bufs):
    for d in (1, 2, 3):
        m = two_rows(lambda q: xnext[pl.ds(((d - 1) * 12 + q) * 8, 8), :])

        def write(q, v):
            bufs[O][pl.ds(place(d * NC + q, 3) + 2, 8), :] = v

        put(write, m)
    m = two_rows(lambda q: xnext[pl.ds(288 + q * 2, 2), :])

    def write_edge(q, v):
        bufs[O][pl.ds(place(3 * NC + q, 3), 2), :] = v

    put(write_edge, m)
    fill_high(bufs, NC)


def fill_corner(corner, buf, d, xe, off, bufs):
    m = two_rows(lambda q: corner[pl.ds(q * 4, 4), :])

    def write_corner(q, v):
        bufs[buf][pl.ds(place(d * NC + q, xe) + off, 4, stride=2), :] = v

    put(write_corner, m)


def take_staples(xprev, bufs, ready):
    for m in (1, 2, 3):
        staple = two_rows(lambda q: xprev[pl.ds(((m - 1) * 12 + q) * 8, 8), :])
        if m == 1:
            whole = mm(staple, link(bufs, 0, step((0, -1), (1, 1)), 0))
            staple = [
                [tuple(jnp.where(first_rows(), staple[i][j][ri], whole[i][j][ri]) for ri in range(2)) for j in range(3)]
                for i in range(3)
            ]
        for i in range(3):
            for j in range(3):
                for ri in range(2):
                    ready[pl.ds(comp(m - 1, i, j, ri) * 8, 8), :] = staple[i][j][ri]


def ready_staple(ready, m):
    return load_matrix(lambda i, j, ri: ready[pl.ds(comp(m - 1, i, j, ri) * 8, 8), :])


def fill_lambda_local(lam, bufs):
    zero = jnp.zeros((2, 128), jnp.float32)
    for c in range(32):
        for x in range(2):
            to = place(c, x + 1)
            bufs[O][pl.ds(to + 2, 8), :] = lam[pl.ds((c * 2 + x) * 8, 8), :]
            bufs[O][pl.ds(to, 2), :] = zero
            bufs[O][pl.ds(to + 10, 2), :] = zero
    fill_y(bufs, NA, (0, 2, 3), (0, 1, 2, 3))
    fill_z(bufs, NA)


def fill_lambda_y(ynext, yprev, bufs):
    zero = jnp.zeros((1, 128), jnp.float32)
    for d in range(4):
        for k in range(NA):
            for x in range(2):
                to = place(d * NA + k, x + 1)
                if d != 1:
                    source = pl.ds((DOWN_Y.index(d) * NA + k) * 8 + x * 4, 4)
                    bufs[YP][pl.ds(to + 3, 4, stride=2), :] = ynext[source, :]
                bufs[YM][pl.ds(to + 2, 4, stride=2), :] = yprev[pl.ds((d * NA + k) * 8 + x * 4, 4), :]
                if d == 3:
                    bufs[YP][pl.ds(to + 1, 1), :] = zero
                if d == 1:
                    bufs[YM][pl.ds(to + 10, 1), :] = zero
    fill_mixed(bufs, NA)


def fill_lambda_next(xnext, bufs):
    zero = jnp.zeros((2, 128), jnp.float32)
    for c in range(24):
        bufs[O][pl.ds(place(NA + c, 3) + 2, 8), :] = xnext[pl.ds(c * 8, 8), :]
    for k in range(NA):
        bufs[O][pl.ds(place(3 * NA + k, 3), 2), :] = zero
        bufs[YM][pl.ds(place(NA + k, 3) + 2, 4, stride=2), :] = xnext[pl.ds(192 + k * 4, 4), :]
    fill_high(bufs, NA)


def step(*signed):
    vector = [0, 0, 0, 0]
    for which, sign in signed:
        vector[which] += sign
    return vector


def where(bufs, n, d, offset, x):
    key = buffer_of[(offset[1], offset[2])]
    row = 2 + 2 * offset[3]
    dd = d - base_dir.get(key, 0)
    shift = (x + 1 + offset[0]) * ROWS

    def read(k):
        return bufs[key][pl.ds(place(dd * n + k, 0) + row + shift, 8), :]

    return read


def link(bufs, d, offset, x):
    read = where(bufs, NC, d, offset, x)
    return load_matrix(lambda i, j, ri: read((i * 3 + j) * 2 + ri))


def lam_at(bufs, d, offset, x):
    read = where(bufs, NA, d, offset, x)
    return unpack8([read(k) for k in range(NA)])


def exponent_force(v, m, target, clow):
    a = v[:3]
    off = [(v[3 + 2 * k], v[4 + 2 * k]) for k in range(3)]
    norm = [r * r + s * s for r, s in off]
    sd = [
        -(a[0] * a[0] + norm[0] + norm[1]),
        -(a[1] * a[1] + norm[0] + norm[2]),
        -(a[2] * a[2] + norm[1] + norm[2]),
    ]
    (r0, s0), (r1, s1), (r2, s2) = off
    so = [
        (a[2] * s0 - (r1 * r2 + s1 * s2), -a[2] * r0 - (s1 * r2 - r1 * s2)),
        (a[1] * s1 + (r0 * r2 - s0 * s2), -a[1] * r1 + (r0 * s2 + s0 * r2)),
        (a[0] * s2 - (r0 * r1 + s0 * s1), -a[0] * r2 - (r0 * s1 - s0 * r1)),
    ]
    c = 0.5 * (sd[0] + sd[1] + sd[2])
    cross = [off[k][1] * so[k][0] - off[k][0] * so[k][1] for k in range(3)]
    dd = (a[0] * sd[0] + a[1] * sd[1] + a[2] * sd[2] + 2.0 * (cross[0] + cross[1] + cross[2])) * (1.0 / 3.0)
    p0r = 1.0 - dd * dd * (1.0 / 720.0)
    p0i = dd * (1.0 / 6.0 + c * (1.0 / 120.0))
    p1r = 1.0 + c * (1.0 / 6.0 + c * (1.0 / 120.0))
    p1i = dd * (1.0 / 24.0 + c * (1.0 / 360.0))
    p2r = 0.5 + c * (1.0 / 24.0 + c * (1.0 / 720.0))
    p2i = dd * (1.0 / 120.0)
    hd = [m[i][i][0] for i in range(3)]
    kd = [m[i][i][1] for i in range(3)]
    ho = [(0.5 * (m[i][j][0] + m[j][i][0]), 0.5 * (m[i][j][1] - m[j][i][1])) for i, j in UPPER]
    ko = [(0.5 * (m[i][j][0] - m[j][i][0]), 0.5 * (m[i][j][1] + m[j][i][1])) for i, j in UPPER]
    t0r = hd[0] + hd[1] + hd[2]
    t0i = -(kd[0] + kd[1] + kd[2])

    def dots(x, y, xo, yo):
        diag = x[0] * y[0] + x[1] * y[1] + x[2] * y[2]
        rest = [xo[k][0] * yo[k][0] + xo[k][1] * yo[k][1] for k in range(3)]
        return diag + 2.0 * (rest[0] + rest[1] + rest[2])

    def crossed(x, y, xo, yo):
        diag = x[0] * y[0] + x[1] * y[1] + x[2] * y[2]
        rest = [yo[k][1] * xo[k][0] - yo[k][0] * xo[k][1] for k in range(3)]
        return diag + 2.0 * (rest[0] + rest[1] + rest[2])

    t1r = dots(kd, a, ko, off)
    t1i = crossed(hd, a, ho, off)
    t2r = dots(hd, sd, ho, so)
    t2i = -crossed(sd, kd, so, ko)
    by_c = (
        t1r * (1.0 / 6.0 + c * (1.0 / 60.0))
        + t2r * (1.0 / 24.0 + c * (1.0 / 360.0))
        - dd * (t0i * (1.0 / 120.0) + t1i * (1.0 / 360.0))
    )
    by_d = -(
        dd * t0r * (1.0 / 360.0)
        + t0i * (1.0 / 6.0 + c * (1.0 / 120.0))
        + t1i * (1.0 / 24.0 + c * (1.0 / 360.0))
        + t2i * (1.0 / 120.0)
    )
    herm = [[None] * 3 for _ in range(3)]
    for i in range(3):
        herm[i][i] = (-(p2r * hd[i] + p2i * kd[i]), None)
    for k, (i, j) in enumerate(UPPER):
        re = -(p2r * ho[k][0] + p2i * ko[k][1])
        im = p2i * ko[k][0] - p2r * ho[k][1]
        herm[i][j] = (re, im)
        herm[j][i] = (re, -im)
    amat = anti(v)
    g = skew(mm(amat, herm))
    lam = [p1r * kd[i] - p1i * hd[i] + g[i] - by_c * a[i] + by_d * sd[i] for i in range(3)]
    for k in range(3):
        lam.append(p1r * ko[k][0] + p1i * ho[k][1] + g[3 + 2 * k] - by_c * off[k][0] - by_d * so[k][1])
        lam.append(p1r * ko[k][1] - p1i * ho[k][0] + g[4 + 2 * k] - by_c * off[k][1] + by_d * so[k][0])
    mean = (lam[0] + lam[1] + lam[2]) * (1.0 / 3.0)
    lam = [smear_weight * (lam[i] - mean) for i in range(3)] + [smear_weight * lam[k] for k in range(3, 9)]
    edag = [[None] * 3 for _ in range(3)]
    for i in range(3):
        edag[i][i] = (p0r - p1i * a[i] + p2r * sd[i], -(p0i + p1r * a[i] + p2i * sd[i]))
    for k, (i, j) in enumerate(UPPER):
        r, s = off[k]
        sr, si = so[k]
        edag[i][j] = (
            (p2r * sr - p1i * s) + (p2i * si - p1r * r),
            (p1i * r - p2i * sr) + (p2r * si - p1r * s),
        )
        edag[j][i] = (
            (p2r * sr - p1i * s) - (p2i * si - p1r * r),
            -(p1i * r + p2i * sr) - (p2r * si + p1r * s),
        )
    direct = msub(mm(edag, target), mm(anti(lam), clow))
    return lam, direct


def plane_fields(m, n):
    here = step()
    return [(m, here), (n, here), (n, step((m, 1))), (m, step((n, 1)))]


def lower_fields(m, n):
    back = step((n, -1))
    return [(n, back), (m, back), (n, step((n, -1), (m, 1)))]


def level(fields, x):
    found = 0
    for _, offset in fields:
        if x + offset[0] == -1:
            found = 3
        elif x + offset[0] == 2:
            found = max(found, 3 if offset[1] else 2)
        elif offset[1]:
            found = max(found, 1)
    return found


LOWERS = [(m, n) for m in range(4) for n in range(4) if n != m]


def items(wanted):
    planes = [(p, m, n, x) for x in range(2) for p, (m, n) in enumerate(PAIRS) if level(plane_fields(m, n), x) == wanted]
    lowers = [(m, n, x) for x in range(2) for m, n in LOWERS if level(lower_fields(m, n), x) == wanted]
    return planes, lowers


def cells(n, k, x):
    return pl.ds((n + k) * 16 + x * 8, 8)


def load_cells(ref, n, x):
    return load_matrix(lambda i, j, ri: ref[cells(n, (i * 3 + j) * 2 + ri, x), :])


def store_cells(ref, n, x, m):
    for i in range(3):
        for j in range(3):
            for ri in range(2):
                ref[cells(n, (i * 3 + j) * 2 + ri, x), :] = m[i][j][ri]


def take_incoming(incoming, inner):
    for c in range(144):
        inner[pl.ds(c * 8, 4, stride=2), :] = incoming[pl.ds(c * 8, 4), :]
        inner[pl.ds(c * 8 + 1, 4, stride=2), :] = incoming[pl.ds(c * 8 + 4, 4), :]


def forward_items(wanted, bufs, omega, loops, low, ready=None):
    planes, lowers = items(wanted)
    begun = {(m, x) for w in range(wanted) for m, _, x in items(w)[1]}
    for p, m, n, x in planes:
        a, d, b, c = [link(bufs, which, offset, x) for which, offset in plane_fields(m, n)]
        loop = mm(mm(a, b), mm(d, c), False, True)
        store_cells(omega, p * 18, x, loop)
        for k, v in enumerate(skew(loop)):
            loops[cells(p * 9, k, x), :] = v
    for m in range(4):
        for x in range(2):
            value = load_cells(low, m * 18, x) if (m, x) in begun else None
            mine = [n for mm_, n, xx in lowers if (mm_, xx) == (m, x)]
            if not mine:
                continue
            for n in mine:
                if n == 0 and x == 0:
                    term = ready_staple(ready, m)
                else:
                    e, g, h = [link(bufs, which, offset, x) for which, offset in lower_fields(m, n)]
                    term = mm(mm(e, g, True, False), h)
                value = term if value is None else madd(value, term)
            store_cells(low, m * 18, x, value)


def target_products(bufs, inner, moved):
    for x in range(2):
        for m in range(4):
            target = load_cells(inner, m * 18, x)
            store_cells(moved, m * 18, x, mm(target, link(bufs, m, step(), x), False, True))


def finish_forward(bufs, inner, moved, loops, low, lam_out, direct):
    for x in range(2):
        for m in range(4):
            u = link(bufs, m, step(), x)
            below = load_cells(low, m * 18, x)
            v = skew_product(below, u, True)
            for p, (f, s) in enumerate(PAIRS):
                if m == f:
                    v = [v[k] - loops[cells(p * 9, k, x), :] for k in range(9)]
                if m == s:
                    v = [v[k] + loops[cells(p * 9, k, x), :] for k in range(9)]
            mean = (v[0] + v[1] + v[2]) * (1.0 / 3.0)
            v = [(0.5 * smear_weight) * (v[k] - mean) for k in range(3)] + [
                (0.5 * smear_weight) * v[k] for k in range(3, 9)
            ]
            lam, force = exponent_force(v, load_cells(moved, m * 18, x), load_cells(inner, m * 18, x), below)
            for k, v in enumerate(lam[:2] + lam[3:]):
                lam_out[cells(m * NA, k, x), :] = v
            store_cells(direct, m * 18, x, force)


def backward_items(wanted, bufs, lams, omega, sums, acc, ready=None, xprev=None):
    planes, lowers = items(wanted)
    begun = {(d, x) for w in range(wanted) for _, m, n, x in items(w)[0] for d in (m, n)}

    def gather(d, x, m):
        store_cells(sums, d * 18, x, madd(load_cells(sums, d * 18, x), m) if (d, x) in begun else m)
        begun.add((d, x))

    for p, m, n, x in planes:
        fields = plane_fields(m, n)
        a, d = [link(bufs, which, offset, x) for which, offset in fields[:2]]
        la, ld, lb, lc = [lam_at(lams, which, offset, x) for which, offset in fields]
        lb, lc = carried(a, lb), carried(d, lc)
        loop = load_cells(omega, p * 18, x)
        z = [ld[k] - la[k] for k in range(9)]
        first = anti([z[k] + lc[k] for k in range(9)])
        second = anti([lb[k] - z[k] for k in range(9)])
        gather(m, x, msub(mm(first, loop, False, True), mm(loop, anti(lb), True, False)))
        gather(n, x, msub(mm(second, loop), mm(loop, anti(lc))))
    for m in range(4):
        for x in range(2):
            mine = [n for mm_, n, xx in lowers if (mm_, xx) == (m, x)]
            if not mine:
                continue
            force = load_cells(acc, m * 18, x)
            for n in mine:
                if n == 0 and x == 0:
                    y = unpack8([xprev[pl.ds(((m - 1) * NA + k) * 8, 8), :] for k in range(NA)])
                    force = madd(force, mm(anti(y), ready_staple(ready, m)))
                    continue
                fields = lower_fields(m, n)
                e, g, h = [link(bufs, which, offset, x) for which, offset in fields]
                le, lg, lh = [lam_at(lams, which, offset, x) for which, offset in fields]
                inside = madd(mm(anti([lg[k] - le[k] for k in range(9)]), g), mm(g, anti(lh)))
                force = madd(force, mm(mm(e, inside, True, False), h))
            store_cells(acc, m * 18, x, force)


def finish_backward(bufs, sums, acc, out):
    for x in range(2):
        for m in range(4):
            f = load_cells(sums, m * 18, x)
            force = madd(mm(f, link(bufs, m, step(), x)), load_cells(acc, m * 18, x))
            store_cells(acc, m * 18, x, force)
            for k in range(18):
                at = ((m * 18 + k) * 2 + x) * 8
                out[pl.ds(at, 4), :] = acc[pl.ds(at, 4, stride=2), :]
                out[pl.ds(at + 4, 4), :] = acc[pl.ds(at + 1, 4, stride=2), :]


def links_local_body(*refs):
    links = refs[0]
    bufs, (omega, loops, low) = refs[1:8], refs[8:]
    fill_links_local(links, bufs)
    forward_items(0, bufs, omega, loops, low)


def links_y_body(*refs):
    ynext, yprev, incoming = refs[:3]
    bufs, (omega, loops, low, inner, moved) = refs[13:20], refs[20:]
    fill_links_y(ynext, yprev, bufs)
    take_incoming(incoming, inner)
    forward_items(1, bufs, omega, loops, low)
    target_products(bufs, inner, moved)


def links_next_body(*refs):
    xnext = refs[0]
    bufs, (omega, loops, low) = refs[11:18], refs[18:]
    fill_links_next(xnext, bufs)
    forward_items(2, bufs, omega, loops, low)


def links_x_body(*refs):
    cnext, xprev, cprev, inner, moved = refs[:5]
    bufs, (omega, loops, low, lam, direct, up, down, ready) = refs[15:22], refs[22:]
    fill_corner(cnext, YM, 1, 3, 2, bufs)
    fill_corner(cprev, YP, 0, 0, 3, bufs)
    take_staples(xprev, bufs, ready)
    forward_items(3, bufs, omega, loops, low, ready)
    finish_forward(bufs, inner, moved, loops, low, lam, direct)

    def reader(row):
        return lambda d, q, x: lam[pl.ds(((d * NA + q) * 2 + x) * 8 + row, 4, stride=2), :]

    pack_y(up, down, NA, reader(1), reader(0))


def lambda_local_body(*refs):
    bufs, (omega, lam) = refs[:7], refs[7:9]
    acc, lams, sums = refs[10], refs[11:18], refs[18]
    fill_lambda_local(lam, lams)
    backward_items(0, bufs, lams, omega, sums, acc)


def lambda_up_body(*refs):
    ynext, yprev, links = refs[:3]
    lams, up = refs[10:17], refs[17]
    fill_lambda_y(ynext, yprev, lams)
    here = step()
    for m in (1, 2, 3):
        a, d = link([links], 0, here, 1), link([links], m, here, 1)
        la, ld, lc = lam_at(lams, 0, here, 1), lam_at(lams, m, here, 1), lam_at(lams, 0, step((m, 1)), 1)
        lc = carried(d, lc)
        y = carried_back(a, [ld[k] - la[k] + lc[k] for k in range(9)])
        for k, v in enumerate(y[:2] + y[3:]):
            up[pl.ds(((m - 1) * NA + k) * 8, 8), :] = v


def lambda_y_body(*refs):
    bufs, omega, lams = refs[:7], refs[7], refs[8:15]
    acc, sums = refs[17:]
    backward_items(1, bufs, lams, omega, sums, acc)


def lambda_x_body(*refs):
    bufs, (omega, ready, xnext, xprev) = refs[:7], refs[7:11]
    out, acc, lams, sums = refs[20], refs[21], refs[22:29], refs[29]
    fill_lambda_next(xnext, lams)
    backward_items(2, bufs, lams, omega, sums, acc)
    backward_items(3, bufs, lams, omega, sums, acc, ready, xprev)
    finish_backward(bufs, sums, acc, out)


def rows(n):
    return jax.ShapeDtypeStruct((n, 128), jnp.float32)


def buffer_rows(n):
    return [(n if key in base_dir else 4 * n) * 4 * ROWS for key in range(7)]


def call(body, args, outs, kept=(), cost=0, first=0):
    shapes = [rows(n) for n in outs]
    shapes[first:first] = [rows(a.shape[0]) for a in kept]
    return pl.pallas_call(
        body,
        out_shape=tuple(shapes),
        in_specs=[pl.BlockSpec(memory_space=pltpu.VMEM)] * (len(args) + len(kept)),
        out_specs=(pl.BlockSpec(memory_space=pltpu.VMEM),) * len(shapes),
        input_output_aliases={len(args) + k: first + k for k in range(len(kept))},
        cost_estimate=pl.CostEstimate(flops=cost, bytes_accessed=0, transcendentals=0) if cost else None,
        compiler_params=pltpu.CompilerParams(vmem_limit_bytes=VM),
    )(*args, *kept)


def shifted(shard, axis, by):
    length = lax.axis_size(axis)
    return lax.ppermute(shard, axis, [(i, (i + by) % length) for i in range(length)])


def diagonal(shard, by_x, by_y):
    nx, ny = lax.axis_size("gx"), lax.axis_size("gy")
    pairs = [(i * ny + j, (i + by_x) % nx * ny + (j + by_y) % ny) for i in range(nx) for j in range(ny)]
    return lax.ppermute(shard, ("gx", "gy"), pairs)


def body(links, incoming):
    links = jnp.transpose(links, (0, 1, 2, 3, 4, 6, 5, 7)).reshape(144 * ROWS, 128)
    shape = incoming.shape
    incoming = incoming.reshape(1152, 128)
    xdown, yup, ydown, cdown, cup = call(pack_first_body, (links,), (312, 408, 312, 48, 48))
    xnext = shifted(xdown, "gx", -1)
    yprev, ynext = shifted(yup, "gy", 1), shifted(ydown, "gy", -1)
    (xup,) = call(pack_up_body, (links,), (288,))
    xprev = shifted(xup, "gx", 1)
    cprev, cnext = diagonal(cup, 1, -1), diagonal(cdown, -1, 1)
    kept = call(links_local_body, (links,), buffer_rows(NC) + [1728, 864, 1152])
    *kept, inner, moved = call(links_y_body, (ynext, yprev, incoming), (1152, 1152), kept)
    kept = call(links_next_body, (xnext,), (), kept)
    r = call(links_x_body, (cnext, xprev, cprev, inner, moved), (512, 1152, 256, 192, 432), kept)
    bufs, omega, (lam, acc, yup, ydown, ready) = r[:7], r[7], r[10:]
    yprev, ynext = shifted(yup, "gy", 1), shifted(ydown, "gy", -1)
    acc, *lams, sums = call(lambda_local_body, (*bufs, omega, lam), buffer_rows(NA) + [1152], (acc,))
    (xdown,) = call(pack_lambda_down_body, (lam, yprev, sums), (224,))
    xnext = shifted(xdown, "gx", -1)
    *lams, xup = call(lambda_up_body, (ynext, yprev, bufs[O]), (192,), lams)
    xprev = shifted(xup, "gx", 1)
    acc, sums = call(lambda_y_body, (*bufs, omega, *lams), (), (acc, sums))
    out = call(lambda_x_body, (*bufs, omega, ready, xnext, xprev), (1152,), (acc, *lams, sums), first=1)[0]
    return out.reshape(shape)


def solution(mesh):
    placed = P(None, None, None, None, "gx", "gy", None, None)
    return jax.shard_map(body, mesh=mesh, in_specs=(placed, placed), out_specs=placed, check_vma=False)
```

```python
import jax
import jax.numpy as jnp
from jax import lax
from jax.experimental import pallas as pl
from jax.experimental.pallas import tpu as pltpu
from jax.sharding import PartitionSpec as P

smear_weight = 0.2
NC, NA = 18, 8
ROWS = 12
VM = 8 * 2**20
O, YP, YM, ZP, ZM, ZPYM, ZMYP = range(7)
buffer_of = {(0, 0): O, (1, 0): YP, (-1, 0): YM, (0, 1): ZP, (0, -1): ZM, (-1, 1): ZPYM, (1, -1): ZMYP}
base_dir = {ZPYM: 1, ZMYP: 2}
PAIRS = [(m, n) for m in range(4) for n in range(m + 1, 4)]
DOWN_Y = [0, 2, 3]
UPPER = [(0, 1), (0, 2), (1, 2)]


def total(terms):
    plus = [a * b for s, a, b in terms if s > 0]
    minus = [a * b for s, a, b in terms if s < 0]
    if not plus:
        value = -minus[0]
        minus = minus[1:]
    else:
        value = plus[0]
        for other in plus[1:]:
            value = value + other
    for other in minus:
        value = value - other
    return value


def entry(left, right, i, k, dag_left=False, dag_right=False, want=(True, True)):
    real, imag = [], []
    for j in range(3):
        ar, ai = left[j][i] if dag_left else left[i][j]
        br, bi = right[k][j] if dag_right else right[j][k]
        sa = -1 if dag_left else 1
        sb = -1 if dag_right else 1
        if ar is not None and br is not None:
            real.append((1, ar, br))
        if ai is not None and bi is not None:
            real.append((-sa * sb, ai, bi))
        if ar is not None and bi is not None:
            imag.append((sb, ar, bi))
        if ai is not None and br is not None:
            imag.append((sa, ai, br))
    return (total(real) if want[0] else None, total(imag) if want[1] else None)


def mm(left, right, dag_left=False, dag_right=False):
    return [[entry(left, right, i, k, dag_left, dag_right) for k in range(3)] for i in range(3)]


def madd(a, b):
    return [[(a[i][j][0] + b[i][j][0], a[i][j][1] + b[i][j][1]) for j in range(3)] for i in range(3)]


def msub(a, b):
    return [[(a[i][j][0] - b[i][j][0], a[i][j][1] - b[i][j][1]) for j in range(3)] for i in range(3)]


def skew(m):
    out = [m[i][i][1] + m[i][i][1] for i in range(3)]
    for i, j in UPPER:
        out += [m[i][j][0] - m[j][i][0], m[i][j][1] + m[j][i][1]]
    return out


def skew_product(left, right, dag_right=False):
    return skew(mm(left, right, False, dag_right))


def unpack8(v):
    return [v[0], v[1], -v[0] - v[1]] + list(v[2:])


def anti(v):
    out = [[None] * 3 for _ in range(3)]
    for i in range(3):
        out[i][i] = (None, v[i])
    for k, (i, j) in enumerate(UPPER):
        r, s = v[3 + 2 * k], v[4 + 2 * k]
        out[i][j] = (r, s)
        out[j][i] = (-r, s)
    return out


def carried(u, v):
    half = mm(u, anti(v))
    diag = [entry(half, u, i, i, False, True, (False, True))[1] for i in range(2)]
    out = [diag[0], diag[1], -diag[0] - diag[1]]
    for i, j in UPPER:
        out += list(entry(half, u, i, j, False, True))
    return out


def third_row(m):
    row = []
    for j in range(3):
        p, q = (j + 1) % 3, (j + 2) % 3
        ar, ai = m[0][p]
        br, bi = m[1][q]
        cr, ci = m[0][q]
        dr, di = m[1][p]
        row.append(
            (ar * br - ai * bi - cr * dr + ci * di, cr * di + ci * dr - ar * bi - ai * br)
        )
    return row


def comp(d, i, j, ri):
    return ((d * 3 + i) * 3 + j) * 2 + ri


def place(c, xe):
    return (c * 4 + xe) * ROWS


def load_matrix(read):
    return [[(read(i, j, 0), read(i, j, 1)) for j in range(3)] for i in range(3)]


def pack_y(up, down, n, read_up, read_down):
    for d in range(4):
        for q in range(n):
            for x in range(2):
                up[pl.ds(((d * n + q) * 2 + x) * 4, 4), :] = read_up(d, q, x)
                if d != 1:
                    down[pl.ds(((DOWN_Y.index(d) * n + q) * 2 + x) * 4, 4), :] = read_down(d, q, x)


def pack_first_body(links, xdown, xup, yup, ydown):
    def reader(row):
        return lambda d, q, x: links[pl.ds(((d * 18 + q) * 2 + x) * ROWS + row, 4, stride=2), :]

    pack_y(yup, ydown, 12, reader(3), reader(2))
    for q in range(12):
        for x in range(2):
            yup[pl.ds(384 + q * 2 + x, 1), :] = links[pl.ds(((18 + q) * 2 + x) * ROWS + 11, 1), :]
            ydown[pl.ds(288 + q * 2 + x, 1), :] = links[pl.ds(((54 + q) * 2 + x) * ROWS, 1), :]
        for d in range(1, 4):
            xdown[pl.ds(((d - 1) * 12 + q) * 8, 8), :] = links[pl.ds((d * 18 + q) * 2 * ROWS + 2, 8), :]
        xdown[pl.ds(288 + q * 2, 2), :] = links[pl.ds((54 + q) * 2 * ROWS, 2), :]
        for d in range(4):
            xup[pl.ds((d * 12 + q) * 8, 8), :] = links[pl.ds(((d * 18 + q) * 2 + 1) * ROWS + 2, 8), :]
        xup[pl.ds(384 + q * 2, 2), :] = links[pl.ds((q * 2 + 1) * ROWS + 10, 2), :]


def pack_corners_body(ynext, yprev, up, down):
    for q in range(12):
        up[pl.ds(q * 4, 4), :] = ynext[pl.ds(q * 8 + 4, 4), :]
        down[pl.ds(q * 4, 4), :] = yprev[pl.ds((12 + q) * 8, 4), :]


def pack_lambda_x_body(lam, ynext, yprev, after, up, down):
    for c in range(32):
        up[pl.ds(c * 8, 8), :] = lam[pl.ds((c * 2 + 1) * 8, 8), :]
        if c >= NA:
            down[pl.ds((c - NA) * 8, 8), :] = lam[pl.ds(c * 16, 8), :]
    for k in range(NA):
        up[pl.ds(256 + k * 4, 4), :] = ynext[pl.ds(k * 8 + 4, 4), :]
        down[pl.ds(192 + k * 4, 4), :] = yprev[pl.ds((NA + k) * 8, 4), :]


def two_rows(read):
    m = [[(read((i * 3 + j) * 2), read((i * 3 + j) * 2 + 1)) for j in range(3)] for i in range(2)]
    return m + [third_row(m)]


def put(write, m):
    for i in range(3):
        for j in range(3):
            for ri in range(2):
                write((i * 3 + j) * 2 + ri, m[i][j][ri])


def roll_z(v, by):
    return pltpu.roll(v, (128 - by) % 128, 1)


def fill_y(bufs, n, dirs_p, dirs_m):
    for x in (1, 2):
        for d in range(4):
            for k in range(n):
                at = place(d * n + k, x)
                if d in dirs_p:
                    bufs[YP][pl.ds(at, 6, stride=2), :] = bufs[O][pl.ds(at + 1, 6, stride=2), :]
                if d in dirs_m:
                    bufs[YM][pl.ds(at + 1, 6, stride=2), :] = bufs[O][pl.ds(at, 6, stride=2), :]


def fill_z(bufs, n):
    for d in range(4):
        for k in range(n):
            c = d * n + k
            for x in (1, 2):
                at = place(c, x)
                zp, zm = bufs[ZP], bufs[ZM]
                if d != 2:
                    zp[pl.ds(at + 2, 8), :] = roll_z(bufs[O][pl.ds(at + 2, 8), :], 1)
                if d == 3:
                    zp[pl.ds(at, 2), :] = roll_z(bufs[O][pl.ds(at, 2), :], 1)
                zm[pl.ds(at + 2, 8), :] = roll_z(bufs[O][pl.ds(at + 2, 8), :], -1)
                if d == 2:
                    zm[pl.ds(at + 10, 2), :] = roll_z(bufs[O][pl.ds(at + 10, 2), :], -1)


def fill_mixed(bufs, n):
    for k in range(n):
        for x in (1, 2):
            bufs[ZPYM][pl.ds(place(k, x) + 2, 8), :] = roll_z(bufs[YM][pl.ds(place(n + k, x) + 2, 8), :], 1)
            bufs[ZMYP][pl.ds(place(k, x) + 2, 8), :] = roll_z(bufs[YP][pl.ds(place(2 * n + k, x) + 2, 8), :], -1)


def fill_high(bufs, n):
    for k in range(n):
        high, side = place(2 * n + k, 3), place(n + k, 3)
        bufs[ZM][pl.ds(high + 2, 8), :] = roll_z(bufs[O][pl.ds(high + 2, 8), :], -1)
        bufs[YM][pl.ds(side + 3, 4, stride=2), :] = bufs[O][pl.ds(side + 2, 4, stride=2), :]


def fill_low(bufs, n):
    for k in range(n):
        low = place(k, 0)
        bufs[ZP][pl.ds(low + 2, 8), :] = roll_z(bufs[O][pl.ds(low + 2, 8), :], 1)
        bufs[YP][pl.ds(low + 2, 4, stride=2), :] = bufs[O][pl.ds(low + 3, 4, stride=2), :]


def fill_links_local(links, bufs):
    for c in range(72):
        for x in range(2):
            source, to = (c * 2 + x) * ROWS, place(c, x + 1)
            bufs[O][pl.ds(to, 8), :] = links[pl.ds(source, 8), :]
            bufs[O][pl.ds(to + 8, 4), :] = links[pl.ds(source + 8, 4), :]
    fill_y(bufs, NC, (0, 2, 3), (0, 1, 2, 3))
    fill_z(bufs, NC)


def fill_links_y(ynext, yprev, bufs):
    for d in range(4):
        for source, buf, off in ((ynext, YP, 3), (yprev, YM, 2)):
            if buf == YP and d == 1:
                continue
            slot = DOWN_Y.index(d) if buf == YP else d
            m = two_rows(lambda q: source[pl.ds((slot * 12 + q) * 8, 8), :])

            def write(q, v):
                for x in range(2):
                    bufs[buf][pl.ds(place(d * NC + q, x + 1) + off, 4, stride=2), :] = v[4 * x : 4 * x + 4]

            put(write, m)
    for source, buf, d, row, at in ((ynext, YP, 3, 1, 288), (yprev, YM, 1, 10, 384)):
        m = two_rows(lambda q: source[pl.ds(at + q * 2, 2), :])

        def write_row(q, v):
            for x in range(2):
                bufs[buf][pl.ds(place(d * NC + q, x + 1) + row, 1), :] = v[x : x + 1]

        put(write_row, m)
    fill_mixed(bufs, NC)


def fill_column(source, slots, bufs, xe, edge):
    for slot, d in enumerate(slots):
        m = two_rows(lambda q: source[pl.ds((slot * 12 + q) * 8, 8), :])

        def write(q, v):
            bufs[O][pl.ds(place(d * NC + q, xe) + 2, 8), :] = v

        put(write, m)
    d, row = edge
    m = two_rows(lambda q: source[pl.ds(len(slots) * 96 + q * 2, 2), :])

    def write_edge(q, v):
        bufs[O][pl.ds(place(d * NC + q, xe) + row, 2), :] = v

    put(write_edge, m)


def fill_corner(corner, buf, d, xe, off, bufs):
    m = two_rows(lambda q: corner[pl.ds(q * 4, 4), :])

    def write_corner(q, v):
        bufs[buf][pl.ds(place(d * NC + q, xe) + off, 4, stride=2), :] = v

    put(write_corner, m)


def fill_links_next(xnext, bufs):
    fill_column(xnext, (1, 2, 3), bufs, 3, (3, 0))
    fill_high(bufs, NC)


def fill_links_prev(xprev, corner, bufs):
    fill_column(xprev, (0, 1, 2, 3), bufs, 0, (0, 10))
    fill_corner(corner, YP, 0, 0, 3, bufs)
    fill_low(bufs, NC)


def fill_lambda_local(lam, bufs):
    zero = jnp.zeros((2, 128), jnp.float32)
    for c in range(32):
        for x in range(2):
            to = place(c, x + 1)
            bufs[O][pl.ds(to + 2, 8), :] = lam[pl.ds((c * 2 + x) * 8, 8), :]
            bufs[O][pl.ds(to, 2), :] = zero
            bufs[O][pl.ds(to + 10, 2), :] = zero
    fill_y(bufs, NA, (0, 2, 3), (0, 1, 2, 3))
    fill_z(bufs, NA)


def fill_lambda_y(ynext, yprev, bufs):
    zero = jnp.zeros((1, 128), jnp.float32)
    for d in range(4):
        for k in range(NA):
            for x in range(2):
                to = place(d * NA + k, x + 1)
                if d != 1:
                    source = pl.ds((DOWN_Y.index(d) * NA + k) * 8 + x * 4, 4)
                    bufs[YP][pl.ds(to + 3, 4, stride=2), :] = ynext[source, :]
                bufs[YM][pl.ds(to + 2, 4, stride=2), :] = yprev[pl.ds((d * NA + k) * 8 + x * 4, 4), :]
                if d == 3:
                    bufs[YP][pl.ds(to + 1, 1), :] = zero
                if d == 1:
                    bufs[YM][pl.ds(to + 10, 1), :] = zero
    fill_mixed(bufs, NA)


def fill_lambda_x(xnext, xprev, bufs):
    zero = jnp.zeros((2, 128), jnp.float32)
    for d in range(4):
        for k in range(NA):
            high, low = place(d * NA + k, 3), place(d * NA + k, 0)
            if d != 0:
                bufs[O][pl.ds(high + 2, 8), :] = xnext[pl.ds(((d - 1) * NA + k) * 8, 8), :]
            bufs[O][pl.ds(low + 2, 8), :] = xprev[pl.ds((d * NA + k) * 8, 8), :]
            if d == 3:
                bufs[O][pl.ds(high, 2), :] = zero
            if d == 0:
                bufs[O][pl.ds(low + 10, 2), :] = zero
    for k in range(NA):
        bufs[YM][pl.ds(place(NA + k, 3) + 2, 4, stride=2), :] = xnext[pl.ds(192 + k * 4, 4), :]
        bufs[YP][pl.ds(place(k, 0) + 3, 4, stride=2), :] = xprev[pl.ds(256 + k * 4, 4), :]
    fill_high(bufs, NA)
    fill_low(bufs, NA)


def step(*signed):
    vector = [0, 0, 0, 0]
    for which, sign in signed:
        vector[which] += sign
    return vector


def where(bufs, n, d, offset, x):
    key = buffer_of[(offset[1], offset[2])]
    row = 2 + 2 * offset[3]
    dd = d - base_dir.get(key, 0)
    shift = (x + 1 + offset[0]) * ROWS

    def read(k):
        return bufs[key][pl.ds(place(dd * n + k, 0) + row + shift, 8), :]

    return read


def link(bufs, d, offset, x):
    read = where(bufs, NC, d, offset, x)
    return load_matrix(lambda i, j, ri: read((i * 3 + j) * 2 + ri))


def lam_at(bufs, d, offset, x):
    read = where(bufs, NA, d, offset, x)
    return unpack8([read(k) for k in range(NA)])


def exponent_force(v, m, target, clow):
    a = v[:3]
    off = [(v[3 + 2 * k], v[4 + 2 * k]) for k in range(3)]
    norm = [r * r + s * s for r, s in off]
    sd = [
        -(a[0] * a[0] + norm[0] + norm[1]),
        -(a[1] * a[1] + norm[0] + norm[2]),
        -(a[2] * a[2] + norm[1] + norm[2]),
    ]
    (r0, s0), (r1, s1), (r2, s2) = off
    so = [
        (a[2] * s0 - (r1 * r2 + s1 * s2), -a[2] * r0 - (s1 * r2 - r1 * s2)),
        (a[1] * s1 + (r0 * r2 - s0 * s2), -a[1] * r1 + (r0 * s2 + s0 * r2)),
        (a[0] * s2 - (r0 * r1 + s0 * s1), -a[0] * r2 - (r0 * s1 - s0 * r1)),
    ]
    c = 0.5 * (sd[0] + sd[1] + sd[2])
    cross = [off[k][1] * so[k][0] - off[k][0] * so[k][1] for k in range(3)]
    dd = (a[0] * sd[0] + a[1] * sd[1] + a[2] * sd[2] + 2.0 * (cross[0] + cross[1] + cross[2])) * (1.0 / 3.0)
    p0r = 1.0 - dd * dd * (1.0 / 720.0)
    p0i = dd * (1.0 / 6.0 + c * (1.0 / 120.0))
    p1r = 1.0 + c * (1.0 / 6.0 + c * (1.0 / 120.0))
    p1i = dd * (1.0 / 24.0 + c * (1.0 / 360.0))
    p2r = 0.5 + c * (1.0 / 24.0 + c * (1.0 / 720.0))
    p2i = dd * (1.0 / 120.0)
    hd = [m[i][i][0] for i in range(3)]
    kd = [m[i][i][1] for i in range(3)]
    ho = [(0.5 * (m[i][j][0] + m[j][i][0]), 0.5 * (m[i][j][1] - m[j][i][1])) for i, j in UPPER]
    ko = [(0.5 * (m[i][j][0] - m[j][i][0]), 0.5 * (m[i][j][1] + m[j][i][1])) for i, j in UPPER]
    t0r = hd[0] + hd[1] + hd[2]
    t0i = -(kd[0] + kd[1] + kd[2])

    def dots(x, y, xo, yo):
        diag = x[0] * y[0] + x[1] * y[1] + x[2] * y[2]
        rest = [xo[k][0] * yo[k][0] + xo[k][1] * yo[k][1] for k in range(3)]
        return diag + 2.0 * (rest[0] + rest[1] + rest[2])

    def crossed(x, y, xo, yo):
        diag = x[0] * y[0] + x[1] * y[1] + x[2] * y[2]
        rest = [yo[k][1] * xo[k][0] - yo[k][0] * xo[k][1] for k in range(3)]
        return diag + 2.0 * (rest[0] + rest[1] + rest[2])

    t1r = dots(kd, a, ko, off)
    t1i = crossed(hd, a, ho, off)
    t2r = dots(hd, sd, ho, so)
    t2i = -crossed(sd, kd, so, ko)
    by_c = (
        t1r * (1.0 / 6.0 + c * (1.0 / 60.0))
        + t2r * (1.0 / 24.0 + c * (1.0 / 360.0))
        - dd * (t0i * (1.0 / 120.0) + t1i * (1.0 / 360.0))
    )
    by_d = -(
        dd * t0r * (1.0 / 360.0)
        + t0i * (1.0 / 6.0 + c * (1.0 / 120.0))
        + t1i * (1.0 / 24.0 + c * (1.0 / 360.0))
        + t2i * (1.0 / 120.0)
    )
    herm = [[None] * 3 for _ in range(3)]
    for i in range(3):
        herm[i][i] = (-(p2r * hd[i] + p2i * kd[i]), None)
    for k, (i, j) in enumerate(UPPER):
        re = -(p2r * ho[k][0] + p2i * ko[k][1])
        im = p2i * ko[k][0] - p2r * ho[k][1]
        herm[i][j] = (re, im)
        herm[j][i] = (re, -im)
    amat = anti(v)
    g = skew(mm(amat, herm))
    lam = [p1r * kd[i] - p1i * hd[i] + g[i] - by_c * a[i] + by_d * sd[i] for i in range(3)]
    for k in range(3):
        lam.append(p1r * ko[k][0] + p1i * ho[k][1] + g[3 + 2 * k] - by_c * off[k][0] - by_d * so[k][1])
        lam.append(p1r * ko[k][1] - p1i * ho[k][0] + g[4 + 2 * k] - by_c * off[k][1] + by_d * so[k][0])
    mean = (lam[0] + lam[1] + lam[2]) * (1.0 / 3.0)
    lam = [smear_weight * (lam[i] - mean) for i in range(3)] + [smear_weight * lam[k] for k in range(3, 9)]
    edag = [[None] * 3 for _ in range(3)]
    for i in range(3):
        edag[i][i] = (p0r - p1i * a[i] + p2r * sd[i], -(p0i + p1r * a[i] + p2i * sd[i]))
    for k, (i, j) in enumerate(UPPER):
        r, s = off[k]
        sr, si = so[k]
        edag[i][j] = (
            (p2r * sr - p1i * s) + (p2i * si - p1r * r),
            (p1i * r - p2i * sr) + (p2r * si - p1r * s),
        )
        edag[j][i] = (
            (p2r * sr - p1i * s) - (p2i * si - p1r * r),
            -(p1i * r + p2i * sr) - (p2r * si + p1r * s),
        )
    direct = msub(mm(edag, target), mm(anti(lam), clow))
    return lam, direct


def plane_fields(m, n):
    here = step()
    return [(m, here), (n, here), (n, step((m, 1))), (m, step((n, 1)))]


def lower_fields(m, n):
    back = step((n, -1))
    return [(n, back), (m, back), (n, step((n, -1), (m, 1)))]


def level(fields, x):
    found = 0
    for _, offset in fields:
        if x + offset[0] == -1:
            found = 3
        elif x + offset[0] == 2:
            found = max(found, 3 if offset[1] else 2)
        elif offset[1]:
            found = max(found, 1)
    return found


LOWERS = [(m, n) for m in range(4) for n in range(4) if n != m]


def items(wanted):
    planes = [(p, m, n, x) for x in range(2) for p, (m, n) in enumerate(PAIRS) if level(plane_fields(m, n), x) == wanted]
    lowers = [(m, n, x) for x in range(2) for m, n in LOWERS if level(lower_fields(m, n), x) == wanted]
    return planes, lowers


def cells(n, k, x):
    return pl.ds((n + k) * 16 + x * 8, 8)


def load_cells(ref, n, x):
    return load_matrix(lambda i, j, ri: ref[cells(n, (i * 3 + j) * 2 + ri, x), :])


def store_cells(ref, n, x, m):
    for i in range(3):
        for j in range(3):
            for ri in range(2):
                ref[cells(n, (i * 3 + j) * 2 + ri, x), :] = m[i][j][ri]


def take_incoming(incoming, inner):
    for c in range(144):
        inner[pl.ds(c * 8, 4, stride=2), :] = incoming[pl.ds(c * 8, 4), :]
        inner[pl.ds(c * 8 + 1, 4, stride=2), :] = incoming[pl.ds(c * 8 + 4, 4), :]


def forward_items(wanted, bufs, omega, loops, low):
    planes, lowers = items(wanted)
    begun = {(m, x) for w in range(wanted) for m, _, x in items(w)[1]}
    for p, m, n, x in planes:
        a, d, b, c = [link(bufs, which, offset, x) for which, offset in plane_fields(m, n)]
        loop = mm(mm(a, b), mm(d, c), False, True)
        store_cells(omega, p * 18, x, loop)
        for k, v in enumerate(skew(loop)):
            loops[cells(p * 9, k, x), :] = v
    for m in range(4):
        for x in range(2):
            value = load_cells(low, m * 18, x) if (m, x) in begun else None
            mine = [n for mm_, n, xx in lowers if (mm_, xx) == (m, x)]
            if not mine:
                continue
            for n in mine:
                e, g, h = [link(bufs, which, offset, x) for which, offset in lower_fields(m, n)]
                term = mm(mm(e, g, True, False), h)
                value = term if value is None else madd(value, term)
            store_cells(low, m * 18, x, value)


def target_products(bufs, inner, moved):
    for x in range(2):
        for m in range(4):
            target = load_cells(inner, m * 18, x)
            store_cells(moved, m * 18, x, mm(target, link(bufs, m, step(), x), False, True))


def finish_forward(bufs, inner, moved, loops, low, lam_out, direct):
    for x in range(2):
        for m in range(4):
            u = link(bufs, m, step(), x)
            below = load_cells(low, m * 18, x)
            v = skew_product(below, u, True)
            for p, (f, s) in enumerate(PAIRS):
                if m == f:
                    v = [v[k] - loops[cells(p * 9, k, x), :] for k in range(9)]
                if m == s:
                    v = [v[k] + loops[cells(p * 9, k, x), :] for k in range(9)]
            mean = (v[0] + v[1] + v[2]) * (1.0 / 3.0)
            v = [(0.5 * smear_weight) * (v[k] - mean) for k in range(3)] + [
                (0.5 * smear_weight) * v[k] for k in range(3, 9)
            ]
            lam, force = exponent_force(v, load_cells(moved, m * 18, x), load_cells(inner, m * 18, x), below)
            for k, v in enumerate(lam[:2] + lam[3:]):
                lam_out[cells(m * NA, k, x), :] = v
            store_cells(direct, m * 18, x, force)


def backward_items(wanted, bufs, lams, omega, sums, acc):
    planes, lowers = items(wanted)
    begun = {(d, x) for w in range(wanted) for _, m, n, x in items(w)[0] for d in (m, n)}

    def gather(d, x, m):
        store_cells(sums, d * 18, x, madd(load_cells(sums, d * 18, x), m) if (d, x) in begun else m)
        begun.add((d, x))

    for p, m, n, x in planes:
        fields = plane_fields(m, n)
        a, d = [link(bufs, which, offset, x) for which, offset in fields[:2]]
        la, ld, lb, lc = [lam_at(lams, which, offset, x) for which, offset in fields]
        lb, lc = carried(a, lb), carried(d, lc)
        loop = load_cells(omega, p * 18, x)
        z = [ld[k] - la[k] for k in range(9)]
        first = anti([z[k] + lc[k] for k in range(9)])
        second = anti([lb[k] - z[k] for k in range(9)])
        gather(m, x, msub(mm(first, loop, False, True), mm(loop, anti(lb), True, False)))
        gather(n, x, msub(mm(second, loop), mm(loop, anti(lc))))
    for m in range(4):
        for x in range(2):
            mine = [n for mm_, n, xx in lowers if (mm_, xx) == (m, x)]
            if not mine:
                continue
            force = load_cells(acc, m * 18, x)
            for n in mine:
                fields = lower_fields(m, n)
                e, g, h = [link(bufs, which, offset, x) for which, offset in fields]
                le, lg, lh = [lam_at(lams, which, offset, x) for which, offset in fields]
                inside = madd(mm(anti([lg[k] - le[k] for k in range(9)]), g), mm(g, anti(lh)))
                force = madd(force, mm(mm(e, inside, True, False), h))
            store_cells(acc, m * 18, x, force)


def add_loops(bufs, sums, acc, m, x):
    f = load_cells(sums, m * 18, x)
    store_cells(acc, m * 18, x, madd(mm(f, link(bufs, m, step(), x)), load_cells(acc, m * 18, x)))


def finish_backward(bufs, sums, acc, out):
    for x in range(2):
        for m in range(4):
            if x == 1:
                add_loops(bufs, sums, acc, m, x)
            for k in range(18):
                at = ((m * 18 + k) * 2 + x) * 8
                out[pl.ds(at, 4), :] = acc[pl.ds(at, 4, stride=2), :]
                out[pl.ds(at + 4, 4), :] = acc[pl.ds(at + 1, 4, stride=2), :]


def links_local_body(*refs):
    links = refs[0]
    bufs, (omega, loops, low) = refs[1:8], refs[8:]
    fill_links_local(links, bufs)
    forward_items(0, bufs, omega, loops, low)


def links_y_body(*refs):
    ynext, yprev, incoming = refs[:3]
    bufs, (omega, loops, low, inner, moved) = refs[13:20], refs[20:]
    fill_links_y(ynext, yprev, bufs)
    take_incoming(incoming, inner)
    forward_items(1, bufs, omega, loops, low)
    target_products(bufs, inner, moved)


def links_next_body(*refs):
    xnext = refs[0]
    bufs, (omega, loops, low) = refs[11:18], refs[18:]
    fill_links_next(xnext, bufs)
    forward_items(2, bufs, omega, loops, low)


def links_x_body(*refs):
    cnext, xprev, cprev, inner, moved = refs[:5]
    bufs, (omega, loops, low, lam, direct, up, down) = refs[15:22], refs[22:]
    fill_corner(cnext, YM, 1, 3, 2, bufs)
    fill_links_prev(xprev, cprev, bufs)
    forward_items(3, bufs, omega, loops, low)
    finish_forward(bufs, inner, moved, loops, low, lam, direct)

    def reader(row):
        return lambda d, q, x: lam[pl.ds(((d * NA + q) * 2 + x) * 8 + row, 4, stride=2), :]

    pack_y(up, down, NA, reader(1), reader(0))


def lambda_local_body(*refs):
    bufs, (omega, lam) = refs[:7], refs[7:9]
    acc, lams, sums = refs[10], refs[11:18], refs[18]
    fill_lambda_local(lam, lams)
    backward_items(0, bufs, lams, omega, sums, acc)


def lambda_y_body(*refs):
    bufs, (omega, ynext, yprev) = refs[:7], refs[7:10]
    acc, lams, sums = refs[19], refs[20:27], refs[27]
    fill_lambda_y(ynext, yprev, lams)
    backward_items(1, bufs, lams, omega, sums, acc)
    for m in range(4):
        add_loops(bufs, sums, acc, m, 0)


def lambda_x_body(*refs):
    bufs, (omega, xnext, xprev) = refs[:7], refs[7:10]
    out, acc, lams, sums = refs[19], refs[20], refs[21:28], refs[28]
    fill_lambda_x(xnext, xprev, lams)
    backward_items(2, bufs, lams, omega, sums, acc)
    backward_items(3, bufs, lams, omega, sums, acc)
    finish_backward(bufs, sums, acc, out)


def rows(n):
    return jax.ShapeDtypeStruct((n, 128), jnp.float32)


def buffer_rows(n):
    return [(n if key in base_dir else 4 * n) * 4 * ROWS for key in range(7)]


def call(body, args, outs, kept=(), cost=0, first=0):
    shapes = [rows(n) for n in outs]
    shapes[first:first] = [rows(a.shape[0]) for a in kept]
    return pl.pallas_call(
        body,
        out_shape=tuple(shapes),
        in_specs=[pl.BlockSpec(memory_space=pltpu.VMEM)] * (len(args) + len(kept)),
        out_specs=(pl.BlockSpec(memory_space=pltpu.VMEM),) * len(shapes),
        input_output_aliases={len(args) + k: first + k for k in range(len(kept))},
        cost_estimate=pl.CostEstimate(flops=cost, bytes_accessed=0, transcendentals=0) if cost else None,
        compiler_params=pltpu.CompilerParams(vmem_limit_bytes=VM),
    )(*args, *kept)


def shifted(shard, axis, by):
    length = lax.axis_size(axis)
    return lax.ppermute(shard, axis, [(i, (i + by) % length) for i in range(length)])


def body(links, incoming):
    links = jnp.transpose(links, (0, 1, 2, 3, 4, 6, 5, 7)).reshape(144 * ROWS, 128)
    shape = incoming.shape
    incoming = incoming.reshape(1152, 128)
    xdown, xup, yup, ydown = call(pack_first_body, (links,), (312, 408, 408, 312))
    xnext, xprev = shifted(xdown, "gx", -1), shifted(xup, "gx", 1)
    yprev, ynext = shifted(yup, "gy", 1), shifted(ydown, "gy", -1)
    cup, cdown = call(pack_corners_body, (ynext, yprev), (48, 48))
    cprev, cnext = shifted(cup, "gx", 1), shifted(cdown, "gx", -1)
    kept = call(links_local_body, (links,), buffer_rows(NC) + [1728, 864, 1152])
    *kept, inner, moved = call(links_y_body, (ynext, yprev, incoming), (1152, 1152), kept)
    kept = call(links_next_body, (xnext,), (), kept)
    r = call(links_x_body, (cnext, xprev, cprev, inner, moved), (512, 1152, 256, 192), kept)
    bufs, omega, (lam, acc, yup, ydown) = r[:7], r[7], r[10:]
    yprev, ynext = shifted(yup, "gy", 1), shifted(ydown, "gy", -1)
    kept = call(lambda_local_body, (*bufs, omega, lam), buffer_rows(NA) + [1152], (acc,))
    xup, xdown = call(pack_lambda_x_body, (lam, ynext, yprev, kept[-1]), (288, 224))
    xprev, xnext = shifted(xup, "gx", 1), shifted(xdown, "gx", -1)
    kept = call(lambda_y_body, (*bufs, omega, ynext, yprev), (), kept)
    out = call(lambda_x_body, (*bufs, omega, xnext, xprev), (1152,), kept, first=1)[0]
    return out.reshape(shape)


def solution(mesh):
    placed = P(None, None, None, None, "gx", "gy", None, None)
    return jax.shard_map(body, mesh=mesh, in_specs=(placed, placed), out_specs=placed, check_vma=False)
```

```python
import jax
import jax.numpy as jnp
from jax import lax
from jax.experimental import pallas as pl
from jax.experimental.pallas import tpu as pltpu
from jax.sharding import PartitionSpec as P

smear_weight = 0.2
NC, NA = 18, 8
ROWS = 12
VM = 8 * 2**20
O, YP, YM, ZP, ZM, ZPYM, ZMYP = range(7)
buffer_of = {(0, 0): O, (1, 0): YP, (-1, 0): YM, (0, 1): ZP, (0, -1): ZM, (-1, 1): ZPYM, (1, -1): ZMYP}
base_dir = {ZPYM: 1, ZMYP: 2}
PAIRS = [(m, n) for m in range(4) for n in range(m + 1, 4)]
DOWN_Y = [0, 2, 3]
UPPER = [(0, 1), (0, 2), (1, 2)]


def total(terms):
    plus = [a * b for s, a, b in terms if s > 0]
    minus = [a * b for s, a, b in terms if s < 0]
    if not plus:
        value = -minus[0]
        minus = minus[1:]
    else:
        value = plus[0]
        for other in plus[1:]:
            value = value + other
    for other in minus:
        value = value - other
    return value


def entry(left, right, i, k, dag_left=False, dag_right=False, want=(True, True)):
    real, imag = [], []
    for j in range(3):
        ar, ai = left[j][i] if dag_left else left[i][j]
        br, bi = right[k][j] if dag_right else right[j][k]
        sa = -1 if dag_left else 1
        sb = -1 if dag_right else 1
        if ar is not None and br is not None:
            real.append((1, ar, br))
        if ai is not None and bi is not None:
            real.append((-sa * sb, ai, bi))
        if ar is not None and bi is not None:
            imag.append((sb, ar, bi))
        if ai is not None and br is not None:
            imag.append((sa, ai, br))
    return (total(real) if want[0] else None, total(imag) if want[1] else None)


def mm(left, right, dag_left=False, dag_right=False):
    return [[entry(left, right, i, k, dag_left, dag_right) for k in range(3)] for i in range(3)]


def madd(a, b):
    return [[(a[i][j][0] + b[i][j][0], a[i][j][1] + b[i][j][1]) for j in range(3)] for i in range(3)]


def msub(a, b):
    return [[(a[i][j][0] - b[i][j][0], a[i][j][1] - b[i][j][1]) for j in range(3)] for i in range(3)]


def skew(m):
    out = [m[i][i][1] + m[i][i][1] for i in range(3)]
    for i, j in UPPER:
        out += [m[i][j][0] - m[j][i][0], m[i][j][1] + m[j][i][1]]
    return out


def skew_product(left, right, dag_right=False):
    return skew(mm(left, right, False, dag_right))


def unpack8(v):
    return [v[0], v[1], -v[0] - v[1]] + list(v[2:])


def anti(v):
    out = [[None] * 3 for _ in range(3)]
    for i in range(3):
        out[i][i] = (None, v[i])
    for k, (i, j) in enumerate(UPPER):
        r, s = v[3 + 2 * k], v[4 + 2 * k]
        out[i][j] = (r, s)
        out[j][i] = (-r, s)
    return out


def carried(u, v):
    half = mm(u, anti(v))
    diag = [entry(half, u, i, i, False, True, (False, True))[1] for i in range(2)]
    out = [diag[0], diag[1], -diag[0] - diag[1]]
    for i, j in UPPER:
        out += list(entry(half, u, i, j, False, True))
    return out


def carried_back(u, v):
    half = mm(u, anti(v), True, False)
    diag = [entry(half, u, i, i, False, False, (False, True))[1] for i in range(2)]
    out = [diag[0], diag[1], -diag[0] - diag[1]]
    for i, j in UPPER:
        out += list(entry(half, u, i, j))
    return out


def first_rows():
    return lax.broadcasted_iota(jnp.int32, (8, 128), 0) % 2 == 0


def third_row(m):
    row = []
    for j in range(3):
        p, q = (j + 1) % 3, (j + 2) % 3
        ar, ai = m[0][p]
        br, bi = m[1][q]
        cr, ci = m[0][q]
        dr, di = m[1][p]
        row.append(
            (ar * br - ai * bi - cr * dr + ci * di, cr * di + ci * dr - ar * bi - ai * br)
        )
    return row


def comp(d, i, j, ri):
    return ((d * 3 + i) * 3 + j) * 2 + ri


def place(c, xe):
    return (c * 4 + xe) * ROWS


def load_matrix(read):
    return [[(read(i, j, 0), read(i, j, 1)) for j in range(3)] for i in range(3)]


def pack_y(up, down, n, read_up, read_down):
    for d in range(4):
        for q in range(n):
            for x in range(2):
                up[pl.ds(((d * n + q) * 2 + x) * 4, 4), :] = read_up(d, q, x)
                if d != 1:
                    down[pl.ds(((DOWN_Y.index(d) * n + q) * 2 + x) * 4, 4), :] = read_down(d, q, x)


def pack_first_body(links, xup, xdown, yup, ydown):
    def reader(row):
        return lambda d, q, x: links[pl.ds(((d * 18 + q) * 2 + x) * ROWS + row, 4, stride=2), :]

    pack_y(yup, ydown, 12, reader(3), reader(2))
    pack_up(links, xup)
    xup[pl.ds(288, 32), :] = jnp.zeros((32, 128), jnp.float32)
    for q in range(12):
        for x in range(2):
            yup[pl.ds(384 + q * 2 + x, 1), :] = links[pl.ds(((18 + q) * 2 + x) * ROWS + 11, 1), :]
            ydown[pl.ds(288 + q * 2 + x, 1), :] = links[pl.ds(((54 + q) * 2 + x) * ROWS, 1), :]
        for d in range(1, 4):
            xdown[pl.ds(((d - 1) * 12 + q) * 8, 8), :] = links[pl.ds((d * 18 + q) * 2 * ROWS + 2, 8), :]
        xdown[pl.ds(288 + q * 2, 2), :] = links[pl.ds((54 + q) * 2 * ROWS, 2), :]


def pack_up(links, up):
    def read(d, row):
        return load_matrix(lambda i, j, ri: links[pl.ds((comp(d, i, j, ri) * 2 + 1) * ROWS + row, 8), :])

    across = read(0, 2)
    for m in (1, 2, 3):
        side = read(m, 2)
        half = [[entry(across, side, i, k, True, False) for k in range(3)] for i in range(2)]
        if m == 2:
            last = [[(roll_z(v[0], 1), roll_z(v[1], 1)) for v in row] for row in across]
        else:
            last = read(0, 3 if m == 1 else 4)
        for i in range(2):
            for j in range(3):
                value = entry(half, last, i, j)
                for ri in range(2):
                    out = jnp.where(first_rows(), value[ri], half[i][j][ri]) if m == 1 else value[ri]
                    up[pl.ds(((m - 1) * 12 + (i * 3 + j) * 2 + ri) * 8, 8), :] = out


def pack_corners_body(ynext, yprev, up, down):
    for q in range(12):
        up[pl.ds(q * 4, 4), :] = ynext[pl.ds(q * 8 + 4, 4), :]
        down[pl.ds(q * 4, 4), :] = yprev[pl.ds((12 + q) * 8, 4), :]


def pack_lambda_down(lam, yprev, down):
    for c in range(24):
        down[pl.ds(c * 8, 8), :] = lam[pl.ds((c + NA) * 16, 8), :]
    for k in range(NA):
        down[pl.ds(192 + k * 4, 4), :] = yprev[pl.ds((NA + k) * 8, 4), :]


def two_rows(read):
    m = [[(read((i * 3 + j) * 2), read((i * 3 + j) * 2 + 1)) for j in range(3)] for i in range(2)]
    return m + [third_row(m)]


def put(write, m):
    for i in range(3):
        for j in range(3):
            for ri in range(2):
                write((i * 3 + j) * 2 + ri, m[i][j][ri])


def roll_z(v, by):
    return pltpu.roll(v, (128 - by) % 128, 1)


def fill_y(bufs, n, dirs_p, dirs_m):
    for x in (1, 2):
        for d in range(4):
            for k in range(n):
                at = place(d * n + k, x)
                if d in dirs_p:
                    bufs[YP][pl.ds(at, 6, stride=2), :] = bufs[O][pl.ds(at + 1, 6, stride=2), :]
                if d in dirs_m:
                    bufs[YM][pl.ds(at + 1, 6, stride=2), :] = bufs[O][pl.ds(at, 6, stride=2), :]


def fill_z(bufs, n):
    for d in range(4):
        for k in range(n):
            c = d * n + k
            for x in (1, 2):
                at = place(c, x)
                zp, zm = bufs[ZP], bufs[ZM]
                if d != 2:
                    zp[pl.ds(at + 2, 8), :] = roll_z(bufs[O][pl.ds(at + 2, 8), :], 1)
                if d == 3:
                    zp[pl.ds(at, 2), :] = roll_z(bufs[O][pl.ds(at, 2), :], 1)
                zm[pl.ds(at + 2, 8), :] = roll_z(bufs[O][pl.ds(at + 2, 8), :], -1)
                if d == 2:
                    zm[pl.ds(at + 10, 2), :] = roll_z(bufs[O][pl.ds(at + 10, 2), :], -1)


def fill_mixed(bufs, n):
    for k in range(n):
        for x in (1, 2):
            bufs[ZPYM][pl.ds(place(k, x) + 2, 8), :] = roll_z(bufs[YM][pl.ds(place(n + k, x) + 2, 8), :], 1)
            bufs[ZMYP][pl.ds(place(k, x) + 2, 8), :] = roll_z(bufs[YP][pl.ds(place(2 * n + k, x) + 2, 8), :], -1)


def fill_high(bufs, n):
    for k in range(n):
        high, side = place(2 * n + k, 3), place(n + k, 3)
        bufs[ZM][pl.ds(high + 2, 8), :] = roll_z(bufs[O][pl.ds(high + 2, 8), :], -1)
        bufs[YM][pl.ds(side + 3, 4, stride=2), :] = bufs[O][pl.ds(side + 2, 4, stride=2), :]


def fill_links_local(links, bufs):
    for c in range(72):
        for x in range(2):
            source, to = (c * 2 + x) * ROWS, place(c, x + 1)
            bufs[O][pl.ds(to, 8), :] = links[pl.ds(source, 8), :]
            bufs[O][pl.ds(to + 8, 4), :] = links[pl.ds(source + 8, 4), :]
    fill_y(bufs, NC, (0, 2, 3), (0, 1, 2, 3))
    fill_z(bufs, NC)


def fill_links_y(ynext, yprev, bufs):
    for d in range(4):
        for source, buf, off in ((ynext, YP, 3), (yprev, YM, 2)):
            if buf == YP and d == 1:
                continue
            slot = DOWN_Y.index(d) if buf == YP else d
            m = two_rows(lambda q: source[pl.ds((slot * 12 + q) * 8, 8), :])

            def write(q, v):
                for x in range(2):
                    bufs[buf][pl.ds(place(d * NC + q, x + 1) + off, 4, stride=2), :] = v[4 * x : 4 * x + 4]

            put(write, m)
    for source, buf, d, row, at in ((ynext, YP, 3, 1, 288), (yprev, YM, 1, 10, 384)):
        m = two_rows(lambda q: source[pl.ds(at + q * 2, 2), :])

        def write_row(q, v):
            for x in range(2):
                bufs[buf][pl.ds(place(d * NC + q, x + 1) + row, 1), :] = v[x : x + 1]

        put(write_row, m)
    fill_mixed(bufs, NC)


def fill_links_next(xnext, bufs):
    for d in (1, 2, 3):
        m = two_rows(lambda q: xnext[pl.ds(((d - 1) * 12 + q) * 8, 8), :])

        def write(q, v):
            bufs[O][pl.ds(place(d * NC + q, 3) + 2, 8), :] = v

        put(write, m)
    m = two_rows(lambda q: xnext[pl.ds(288 + q * 2, 2), :])

    def write_edge(q, v):
        bufs[O][pl.ds(place(3 * NC + q, 3), 2), :] = v

    put(write_edge, m)
    fill_high(bufs, NC)


def fill_corner(corner, buf, d, xe, off, bufs):
    m = two_rows(lambda q: corner[pl.ds(q * 4, 4), :])

    def write_corner(q, v):
        bufs[buf][pl.ds(place(d * NC + q, xe) + off, 4, stride=2), :] = v

    put(write_corner, m)


def take_staples(xprev, bufs, ready):
    for m in (1, 2, 3):
        staple = two_rows(lambda q: xprev[pl.ds(((m - 1) * 12 + q) * 8, 8), :])
        if m == 1:
            whole = mm(staple, link(bufs, 0, step((0, -1), (1, 1)), 0))
            staple = [
                [tuple(jnp.where(first_rows(), staple[i][j][ri], whole[i][j][ri]) for ri in range(2)) for j in range(3)]
                for i in range(3)
            ]
        for i in range(3):
            for j in range(3):
                for ri in range(2):
                    ready[pl.ds(comp(m - 1, i, j, ri) * 8, 8), :] = staple[i][j][ri]


def ready_staple(ready, m):
    return load_matrix(lambda i, j, ri: ready[pl.ds(comp(m - 1, i, j, ri) * 8, 8), :])


def fill_lambda_local(lam, bufs):
    zero = jnp.zeros((2, 128), jnp.float32)
    for c in range(32):
        for x in range(2):
            to = place(c, x + 1)
            bufs[O][pl.ds(to + 2, 8), :] = lam[pl.ds((c * 2 + x) * 8, 8), :]
            bufs[O][pl.ds(to, 2), :] = zero
            bufs[O][pl.ds(to + 10, 2), :] = zero
    fill_y(bufs, NA, (0, 2, 3), (0, 1, 2, 3))
    fill_z(bufs, NA)


def fill_lambda_y(ynext, yprev, bufs):
    zero = jnp.zeros((1, 128), jnp.float32)
    for d in range(4):
        for k in range(NA):
            for x in range(2):
                to = place(d * NA + k, x + 1)
                if d != 1:
                    source = pl.ds((DOWN_Y.index(d) * NA + k) * 8 + x * 4, 4)
                    bufs[YP][pl.ds(to + 3, 4, stride=2), :] = ynext[source, :]
                bufs[YM][pl.ds(to + 2, 4, stride=2), :] = yprev[pl.ds((d * NA + k) * 8 + x * 4, 4), :]
                if d == 3:
                    bufs[YP][pl.ds(to + 1, 1), :] = zero
                if d == 1:
                    bufs[YM][pl.ds(to + 10, 1), :] = zero
    fill_mixed(bufs, NA)


def fill_lambda_next(xnext, bufs):
    zero = jnp.zeros((2, 128), jnp.float32)
    for c in range(24):
        bufs[O][pl.ds(place(NA + c, 3) + 2, 8), :] = xnext[pl.ds(c * 8, 8), :]
    for k in range(NA):
        bufs[O][pl.ds(place(3 * NA + k, 3), 2), :] = zero
        bufs[YM][pl.ds(place(NA + k, 3) + 2, 4, stride=2), :] = xnext[pl.ds(192 + k * 4, 4), :]
    fill_high(bufs, NA)


def step(*signed):
    vector = [0, 0, 0, 0]
    for which, sign in signed:
        vector[which] += sign
    return vector


def where(bufs, n, d, offset, x):
    key = buffer_of[(offset[1], offset[2])]
    row = 2 + 2 * offset[3]
    dd = d - base_dir.get(key, 0)
    shift = (x + 1 + offset[0]) * ROWS

    def read(k):
        return bufs[key][pl.ds(place(dd * n + k, 0) + row + shift, 8), :]

    return read


def link(bufs, d, offset, x):
    read = where(bufs, NC, d, offset, x)
    return load_matrix(lambda i, j, ri: read((i * 3 + j) * 2 + ri))


def lam_at(bufs, d, offset, x):
    read = where(bufs, NA, d, offset, x)
    return unpack8([read(k) for k in range(NA)])


def exponent_force(v, m):
    a = v[:3]
    off = [(v[3 + 2 * k], v[4 + 2 * k]) for k in range(3)]
    norm = [r * r + s * s for r, s in off]
    sd = [
        -(a[0] * a[0] + norm[0] + norm[1]),
        -(a[1] * a[1] + norm[0] + norm[2]),
        -(a[2] * a[2] + norm[1] + norm[2]),
    ]
    (r0, s0), (r1, s1), (r2, s2) = off
    so = [
        (a[2] * s0 - (r1 * r2 + s1 * s2), -a[2] * r0 - (s1 * r2 - r1 * s2)),
        (a[1] * s1 + (r0 * r2 - s0 * s2), -a[1] * r1 + (r0 * s2 + s0 * r2)),
        (a[0] * s2 - (r0 * r1 + s0 * s1), -a[0] * r2 - (r0 * s1 - s0 * r1)),
    ]
    c = 0.5 * (sd[0] + sd[1] + sd[2])
    cross = [off[k][1] * so[k][0] - off[k][0] * so[k][1] for k in range(3)]
    dd = (a[0] * sd[0] + a[1] * sd[1] + a[2] * sd[2] + 2.0 * (cross[0] + cross[1] + cross[2])) * (1.0 / 3.0)
    p0r = 1.0 - dd * dd * (1.0 / 720.0)
    p0i = dd * (1.0 / 6.0 + c * (1.0 / 120.0))
    p1r = 1.0 + c * (1.0 / 6.0 + c * (1.0 / 120.0))
    p1i = dd * (1.0 / 24.0 + c * (1.0 / 360.0))
    p2r = 0.5 + c * (1.0 / 24.0 + c * (1.0 / 720.0))
    p2i = dd * (1.0 / 120.0)
    hd = [m[i][i][0] for i in range(3)]
    kd = [m[i][i][1] for i in range(3)]
    ho = [(0.5 * (m[i][j][0] + m[j][i][0]), 0.5 * (m[i][j][1] - m[j][i][1])) for i, j in UPPER]
    ko = [(0.5 * (m[i][j][0] - m[j][i][0]), 0.5 * (m[i][j][1] + m[j][i][1])) for i, j in UPPER]
    t0r = hd[0] + hd[1] + hd[2]
    t0i = -(kd[0] + kd[1] + kd[2])

    def dots(x, y, xo, yo):
        diag = x[0] * y[0] + x[1] * y[1] + x[2] * y[2]
        rest = [xo[k][0] * yo[k][0] + xo[k][1] * yo[k][1] for k in range(3)]
        return diag + 2.0 * (rest[0] + rest[1] + rest[2])

    def crossed(x, y, xo, yo):
        diag = x[0] * y[0] + x[1] * y[1] + x[2] * y[2]
        rest = [yo[k][1] * xo[k][0] - yo[k][0] * xo[k][1] for k in range(3)]
        return diag + 2.0 * (rest[0] + rest[1] + rest[2])

    t1r = dots(kd, a, ko, off)
    t1i = crossed(hd, a, ho, off)
    t2r = dots(hd, sd, ho, so)
    t2i = -crossed(sd, kd, so, ko)
    by_c = (
        t1r * (1.0 / 6.0 + c * (1.0 / 60.0))
        + t2r * (1.0 / 24.0 + c * (1.0 / 360.0))
        - dd * (t0i * (1.0 / 120.0) + t1i * (1.0 / 360.0))
    )
    by_d = -(
        dd * t0r * (1.0 / 360.0)
        + t0i * (1.0 / 6.0 + c * (1.0 / 120.0))
        + t1i * (1.0 / 24.0 + c * (1.0 / 360.0))
        + t2i * (1.0 / 120.0)
    )
    herm = [[None] * 3 for _ in range(3)]
    for i in range(3):
        herm[i][i] = (-(p2r * hd[i] + p2i * kd[i]), None)
    for k, (i, j) in enumerate(UPPER):
        re = -(p2r * ho[k][0] + p2i * ko[k][1])
        im = p2i * ko[k][0] - p2r * ho[k][1]
        herm[i][j] = (re, im)
        herm[j][i] = (re, -im)
    amat = anti(v)
    g = skew(mm(amat, herm))
    lam = [p1r * kd[i] - p1i * hd[i] + g[i] - by_c * a[i] + by_d * sd[i] for i in range(3)]
    for k in range(3):
        lam.append(p1r * ko[k][0] + p1i * ho[k][1] + g[3 + 2 * k] - by_c * off[k][0] - by_d * so[k][1])
        lam.append(p1r * ko[k][1] - p1i * ho[k][0] + g[4 + 2 * k] - by_c * off[k][1] + by_d * so[k][0])
    mean = (lam[0] + lam[1] + lam[2]) * (1.0 / 3.0)
    lam = [smear_weight * (lam[i] - mean) for i in range(3)] + [smear_weight * lam[k] for k in range(3, 9)]
    edag = [[None] * 3 for _ in range(3)]
    for i in range(3):
        edag[i][i] = (p0r - p1i * a[i] + p2r * sd[i], -(p0i + p1r * a[i] + p2i * sd[i]))
    for k, (i, j) in enumerate(UPPER):
        r, s = off[k]
        sr, si = so[k]
        edag[i][j] = (
            (p2r * sr - p1i * s) + (p2i * si - p1r * r),
            (p1i * r - p2i * sr) + (p2r * si - p1r * s),
        )
        edag[j][i] = (
            (p2r * sr - p1i * s) - (p2i * si - p1r * r),
            -(p1i * r + p2i * sr) - (p2r * si + p1r * s),
        )
    return lam, edag


def plane_fields(m, n):
    here = step()
    return [(m, here), (n, here), (n, step((m, 1))), (m, step((n, 1)))]


def lower_fields(m, n):
    back = step((n, -1))
    return [(n, back), (m, back), (n, step((n, -1), (m, 1)))]


def level(fields, x):
    found = 0
    for _, offset in fields:
        if x + offset[0] == -1:
            found = 3
        elif x + offset[0] == 2:
            found = max(found, 3 if offset[1] else 2)
        elif offset[1]:
            found = max(found, 1)
    return found


LOWERS = [(m, n) for m in range(4) for n in range(4) if n != m]


def items(wanted):
    planes = [(p, m, n, x) for x in range(2) for p, (m, n) in enumerate(PAIRS) if level(plane_fields(m, n), x) == wanted]
    lowers = [(m, n, x) for x in range(2) for m, n in LOWERS if level(lower_fields(m, n), x) == wanted]
    return planes, lowers


def cells(n, k, x):
    return pl.ds((n + k) * 16 + x * 8, 8)


def load_cells(ref, n, x):
    return load_matrix(lambda i, j, ri: ref[cells(n, (i * 3 + j) * 2 + ri, x), :])


def store_cells(ref, n, x, m):
    for i in range(3):
        for j in range(3):
            for ri in range(2):
                ref[cells(n, (i * 3 + j) * 2 + ri, x), :] = m[i][j][ri]


def take_incoming(incoming, inner):
    for c in range(144):
        inner[pl.ds(c * 8, 4, stride=2), :] = incoming[pl.ds(c * 8, 4), :]
        inner[pl.ds(c * 8 + 1, 4, stride=2), :] = incoming[pl.ds(c * 8 + 4, 4), :]


def forward_items(wanted, bufs, omega, loops, low, ready=None):
    planes, lowers = items(wanted)
    begun = {(m, x) for w in range(wanted) for m, _, x in items(w)[1]}
    for p, m, n, x in planes:
        a, d, b, c = [link(bufs, which, offset, x) for which, offset in plane_fields(m, n)]
        loop = mm(mm(a, b), mm(d, c), False, True)
        store_cells(omega, p * 18, x, loop)
        for k, v in enumerate(skew(loop)):
            loops[cells(p * 9, k, x), :] = v
    for m in range(4):
        for x in range(2):
            value = load_cells(low, m * 18, x) if (m, x) in begun else None
            mine = [n for mm_, n, xx in lowers if (mm_, xx) == (m, x)]
            if not mine:
                continue
            for n in mine:
                if n == 0 and x == 0:
                    term = ready_staple(ready, m)
                else:
                    e, g, h = [link(bufs, which, offset, x) for which, offset in lower_fields(m, n)]
                    term = mm(mm(e, g, True, False), h)
                value = term if value is None else madd(value, term)
            store_cells(low, m * 18, x, value)


def target_products(bufs, inner, moved):
    for x in range(2):
        for m in range(4):
            target = load_cells(inner, m * 18, x)
            store_cells(moved, m * 18, x, mm(target, link(bufs, m, step(), x), False, True))


def finish_forward(bufs, moved, loops, low, lam_out, edag):
    for x in range(2):
        for m in range(4):
            u = link(bufs, m, step(), x)
            below = load_cells(low, m * 18, x)
            v = skew_product(below, u, True)
            for p, (f, s) in enumerate(PAIRS):
                if m == f:
                    v = [v[k] - loops[cells(p * 9, k, x), :] for k in range(9)]
                if m == s:
                    v = [v[k] + loops[cells(p * 9, k, x), :] for k in range(9)]
            mean = (v[0] + v[1] + v[2]) * (1.0 / 3.0)
            v = [(0.5 * smear_weight) * (v[k] - mean) for k in range(3)] + [
                (0.5 * smear_weight) * v[k] for k in range(3, 9)
            ]
            lam, smearing = exponent_force(v, load_cells(moved, m * 18, x))
            for k, v in enumerate(lam[:2] + lam[3:]):
                lam_out[cells(m * NA, k, x), :] = v
            store_cells(edag, m * 18, x, smearing)


def backward_items(wanted, bufs, lams, omega, sums, acc, ready=None, xprev=None):
    planes, lowers = items(wanted)
    begun = {(d, x) for w in range(wanted) for _, m, n, x in items(w)[0] for d in (m, n)}

    def gather(d, x, m):
        store_cells(sums, d * 18, x, madd(load_cells(sums, d * 18, x), m) if (d, x) in begun else m)
        begun.add((d, x))

    for p, m, n, x in planes:
        fields = plane_fields(m, n)
        a, d = [link(bufs, which, offset, x) for which, offset in fields[:2]]
        la, ld, lb, lc = [lam_at(lams, which, offset, x) for which, offset in fields]
        lb, lc = carried(a, lb), carried(d, lc)
        loop = load_cells(omega, p * 18, x)
        z = [ld[k] - la[k] for k in range(9)]
        first = anti([z[k] + lc[k] for k in range(9)])
        second = anti([lb[k] - z[k] for k in range(9)])
        gather(m, x, msub(mm(first, loop, False, True), mm(loop, anti(lb), True, False)))
        gather(n, x, msub(mm(second, loop), mm(loop, anti(lc))))
    for m in range(4):
        for x in range(2):
            mine = [n for mm_, n, xx in lowers if (mm_, xx) == (m, x)]
            if not mine:
                continue
            force = load_cells(acc, m * 18, x)
            for n in mine:
                if n == 0 and x == 0:
                    y = unpack8([xprev[pl.ds(((m - 1) * NA + k) * 8, 8), :] for k in range(NA)])
                    force = madd(force, mm(anti(y), ready_staple(ready, m)))
                    continue
                fields = lower_fields(m, n)
                e, g, h = [link(bufs, which, offset, x) for which, offset in fields]
                le, lg, lh = [lam_at(lams, which, offset, x) for which, offset in fields]
                inside = madd(mm(anti([lg[k] - le[k] for k in range(9)]), g), mm(g, anti(lh)))
                force = madd(force, mm(mm(e, inside, True, False), h))
            store_cells(acc, m * 18, x, force)


def add_loops(bufs, sums, acc, m, x):
    f = load_cells(sums, m * 18, x)
    store_cells(acc, m * 18, x, madd(mm(f, link(bufs, m, step(), x)), load_cells(acc, m * 18, x)))


def finish_backward(bufs, sums, acc, out):
    for x in range(2):
        for m in range(4):
            if x == 1:
                add_loops(bufs, sums, acc, m, x)
            for k in range(18):
                at = ((m * 18 + k) * 2 + x) * 8
                out[pl.ds(at, 4), :] = acc[pl.ds(at, 4, stride=2), :]
                out[pl.ds(at + 4, 4), :] = acc[pl.ds(at + 1, 4, stride=2), :]


def links_local_body(*refs):
    links = refs[0]
    bufs, (omega, loops, low) = refs[1:8], refs[8:]
    fill_links_local(links, bufs)
    forward_items(0, bufs, omega, loops, low)


def links_y_body(*refs):
    ynext, yprev, incoming = refs[:3]
    bufs, (omega, loops, low, inner, moved) = refs[13:20], refs[20:]
    fill_links_y(ynext, yprev, bufs)
    take_incoming(incoming, inner)
    forward_items(1, bufs, omega, loops, low)
    target_products(bufs, inner, moved)


def links_next_body(*refs):
    xnext = refs[0]
    bufs, (omega, loops, low) = refs[11:18], refs[18:]
    fill_links_next(xnext, bufs)
    forward_items(2, bufs, omega, loops, low)


def links_x_body(*refs):
    cnext, xprev, cprev, moved = refs[:4]
    bufs, (omega, loops, low, lam, edag, up, down, ready) = refs[14:21], refs[21:]
    fill_corner(cnext, YM, 1, 3, 2, bufs)
    fill_corner(cprev, YP, 0, 0, 3, bufs)
    take_staples(xprev, bufs, ready)
    forward_items(3, bufs, omega, loops, low, ready)
    finish_forward(bufs, moved, loops, low, lam, edag)

    def reader(row):
        return lambda d, q, x: lam[pl.ds(((d * NA + q) * 2 + x) * 8 + row, 4, stride=2), :]

    pack_y(up, down, NA, reader(1), reader(0))


def lambda_local_body(*refs):
    bufs, (omega, lam, inner, low) = refs[:7], refs[7:11]
    acc, lams, sums = refs[12], refs[13:20], refs[20]
    fill_lambda_local(lam, lams)
    for x in range(2):
        for m in range(4):
            own = anti(unpack8([lam[cells(m * NA, k, x), :] for k in range(NA)]))
            force = mm(load_cells(acc, m * 18, x), load_cells(inner, m * 18, x))
            store_cells(acc, m * 18, x, msub(force, mm(own, load_cells(low, m * 18, x))))
    backward_items(0, bufs, lams, omega, sums, acc)


def lambda_up_body(*refs):
    ynext, yprev, links, lam = refs[:4]
    lams, (up, down) = refs[11:18], refs[18:]
    pack_lambda_down(lam, yprev, down)
    fill_lambda_y(ynext, yprev, lams)
    here = step()
    for m in (1, 2, 3):
        a, d = link([links], 0, here, 1), link([links], m, here, 1)
        la, ld, lc = lam_at(lams, 0, here, 1), lam_at(lams, m, here, 1), lam_at(lams, 0, step((m, 1)), 1)
        lc = carried(d, lc)
        y = carried_back(a, [ld[k] - la[k] + lc[k] for k in range(9)])
        for k, v in enumerate(y[:2] + y[3:]):
            up[pl.ds(((m - 1) * NA + k) * 8, 8), :] = v


def lambda_y_body(*refs):
    bufs, omega, lams = refs[:7], refs[7], refs[8:15]
    acc, sums = refs[17:]
    backward_items(1, bufs, lams, omega, sums, acc)
    for m in range(4):
        add_loops(bufs, sums, acc, m, 0)


def lambda_x_body(*refs):
    bufs, (omega, ready, xnext, xprev) = refs[:7], refs[7:11]
    out, acc, lams, sums = refs[20], refs[21], refs[22:29], refs[29]
    fill_lambda_next(xnext, lams)
    backward_items(2, bufs, lams, omega, sums, acc)
    backward_items(3, bufs, lams, omega, sums, acc, ready, xprev)
    finish_backward(bufs, sums, acc, out)


def rows(n):
    return jax.ShapeDtypeStruct((n, 128), jnp.float32)


def buffer_rows(n):
    return [(n if key in base_dir else 4 * n) * 4 * ROWS for key in range(7)]


def call(body, args, outs, kept=(), cost=0, first=0):
    shapes = [rows(n) for n in outs]
    shapes[first:first] = [rows(a.shape[0]) for a in kept]
    return pl.pallas_call(
        body,
        out_shape=tuple(shapes),
        in_specs=[pl.BlockSpec(memory_space=pltpu.VMEM)] * (len(args) + len(kept)),
        out_specs=(pl.BlockSpec(memory_space=pltpu.VMEM),) * len(shapes),
        input_output_aliases={len(args) + k: first + k for k in range(len(kept))},
        cost_estimate=pl.CostEstimate(flops=cost, bytes_accessed=0, transcendentals=0) if cost else None,
        compiler_params=pltpu.CompilerParams(vmem_limit_bytes=VM),
    )(*args, *kept)


def shifted(shard, axis, by):
    length = lax.axis_size(axis)
    return lax.ppermute(shard, axis, [(i, (i + by) % length) for i in range(length)])


def body(links, incoming):
    links = jnp.transpose(links, (0, 1, 2, 3, 4, 6, 5, 7)).reshape(144 * ROWS, 128)
    shape = incoming.shape
    incoming = incoming.reshape(1152, 128)
    xup, xdown, yup, ydown = call(pack_first_body, (links,), (320, 312, 408, 312))
    xprev, xnext = shifted(xup, "gx", 1), shifted(xdown, "gx", -1)
    yprev, ynext = shifted(yup, "gy", 1), shifted(ydown, "gy", -1)
    cup, cdown = call(pack_corners_body, (ynext, yprev), (48, 48))
    cprev, cnext = shifted(cup, "gx", 1), shifted(cdown, "gx", -1)
    kept = call(links_local_body, (links,), buffer_rows(NC) + [1728, 864, 1152])
    *kept, inner, moved = call(links_y_body, (ynext, yprev, incoming), (1152, 1152), kept)
    kept = call(links_next_body, (xnext,), (), kept)
    r = call(links_x_body, (cnext, xprev, cprev, moved), (512, 1152, 256, 192, 432), kept)
    bufs, omega, low, (lam, acc, yup, ydown, ready) = r[:7], r[7], r[9], r[10:]
    yprev, ynext = shifted(yup, "gy", 1), shifted(ydown, "gy", -1)
    acc, *lams, sums = call(lambda_local_body, (*bufs, omega, lam, inner, low), buffer_rows(NA) + [1152], (acc,))
    *lams, xup, xdown = call(lambda_up_body, (ynext, yprev, bufs[O], lam), (192, 224), lams)
    xprev, xnext = shifted(xup, "gx", 1), shifted(xdown, "gx", -1)
    acc, sums = call(lambda_y_body, (*bufs, omega, *lams), (), (acc, sums))
    out = call(lambda_x_body, (*bufs, omega, ready, xnext, xprev), (1152,), (acc, *lams, sums), first=1)[0]
    return out.reshape(shape)


def solution(mesh):
    placed = P(None, None, None, None, "gx", "gy", None, None)
    return jax.shard_map(body, mesh=mesh, in_specs=(placed, placed), out_specs=placed, check_vma=False)
```

```python
import jax
import jax.numpy as jnp
from jax import lax
from jax.experimental import pallas as pl
from jax.experimental.pallas import tpu as pltpu
from jax.sharding import PartitionSpec as P

smear_weight = 0.2
NC, NA = 18, 8
ROWS = 12
VM = 8 * 2**20
O, YP, YM, ZP, ZM, ZPYM, ZMYP = range(7)
buffer_of = {(0, 0): O, (1, 0): YP, (-1, 0): YM, (0, 1): ZP, (0, -1): ZM, (-1, 1): ZPYM, (1, -1): ZMYP}
base_dir = {ZPYM: 1, ZMYP: 2}
PAIRS = [(m, n) for m in range(4) for n in range(m + 1, 4)]
DOWN_Y = [0, 2, 3]
UPPER = [(0, 1), (0, 2), (1, 2)]


def total(terms):
    plus = [a * b for s, a, b in terms if s > 0]
    minus = [a * b for s, a, b in terms if s < 0]
    if not plus:
        value = -minus[0]
        minus = minus[1:]
    else:
        value = plus[0]
        for other in plus[1:]:
            value = value + other
    for other in minus:
        value = value - other
    return value


def entry(left, right, i, k, dag_left=False, dag_right=False, want=(True, True)):
    real, imag = [], []
    for j in range(3):
        ar, ai = left[j][i] if dag_left else left[i][j]
        br, bi = right[k][j] if dag_right else right[j][k]
        sa = -1 if dag_left else 1
        sb = -1 if dag_right else 1
        if ar is not None and br is not None:
            real.append((1, ar, br))
        if ai is not None and bi is not None:
            real.append((-sa * sb, ai, bi))
        if ar is not None and bi is not None:
            imag.append((sb, ar, bi))
        if ai is not None and br is not None:
            imag.append((sa, ai, br))
    return (total(real) if want[0] else None, total(imag) if want[1] else None)


def mm(left, right, dag_left=False, dag_right=False):
    return [[entry(left, right, i, k, dag_left, dag_right) for k in range(3)] for i in range(3)]


def madd(a, b):
    return [[(a[i][j][0] + b[i][j][0], a[i][j][1] + b[i][j][1]) for j in range(3)] for i in range(3)]


def msub(a, b):
    return [[(a[i][j][0] - b[i][j][0], a[i][j][1] - b[i][j][1]) for j in range(3)] for i in range(3)]


def skew(m):
    out = [m[i][i][1] + m[i][i][1] for i in range(3)]
    for i, j in UPPER:
        out += [m[i][j][0] - m[j][i][0], m[i][j][1] + m[j][i][1]]
    return out


def skew_product(left, right, dag_right=False):
    return skew(mm(left, right, False, dag_right))


def unpack8(v):
    return [v[0], v[1], -v[0] - v[1]] + list(v[2:])


def anti(v):
    out = [[None] * 3 for _ in range(3)]
    for i in range(3):
        out[i][i] = (None, v[i])
    for k, (i, j) in enumerate(UPPER):
        r, s = v[3 + 2 * k], v[4 + 2 * k]
        out[i][j] = (r, s)
        out[j][i] = (-r, s)
    return out


def carried(u, v):
    half = mm(u, anti(v))
    diag = [entry(half, u, i, i, False, True, (False, True))[1] for i in range(2)]
    out = [diag[0], diag[1], -diag[0] - diag[1]]
    for i, j in UPPER:
        out += list(entry(half, u, i, j, False, True))
    return out


def carried_back(u, v):
    half = mm(u, anti(v), True, False)
    diag = [entry(half, u, i, i, False, False, (False, True))[1] for i in range(2)]
    out = [diag[0], diag[1], -diag[0] - diag[1]]
    for i, j in UPPER:
        out += list(entry(half, u, i, j))
    return out


def first_rows():
    return lax.broadcasted_iota(jnp.int32, (8, 128), 0) % 2 == 0


def third_row(m):
    row = []
    for j in range(3):
        p, q = (j + 1) % 3, (j + 2) % 3
        ar, ai = m[0][p]
        br, bi = m[1][q]
        cr, ci = m[0][q]
        dr, di = m[1][p]
        row.append(
            (ar * br - ai * bi - cr * dr + ci * di, cr * di + ci * dr - ar * bi - ai * br)
        )
    return row


def comp(d, i, j, ri):
    return ((d * 3 + i) * 3 + j) * 2 + ri


def place(c, xe):
    return (c * 4 + xe) * ROWS


def load_matrix(read):
    return [[(read(i, j, 0), read(i, j, 1)) for j in range(3)] for i in range(3)]


def pack_y(up, down, n, read_up, read_down):
    for d in range(4):
        for q in range(n):
            for x in range(2):
                up[pl.ds(((d * n + q) * 2 + x) * 4, 4), :] = read_up(d, q, x)
                if d != 1:
                    down[pl.ds(((DOWN_Y.index(d) * n + q) * 2 + x) * 4, 4), :] = read_down(d, q, x)


def pack_first_body(links, xup, xdown, yup, ydown):
    def reader(row):
        return lambda d, q, x: links[pl.ds(((d * 18 + q) * 2 + x) * ROWS + row, 4, stride=2), :]

    pack_y(yup, ydown, 12, reader(3), reader(2))
    pack_up(links, xup)
    for q in range(12):
        for x in range(2):
            yup[pl.ds(384 + q * 2 + x, 1), :] = links[pl.ds(((18 + q) * 2 + x) * ROWS + 11, 1), :]
            ydown[pl.ds(288 + q * 2 + x, 1), :] = links[pl.ds(((54 + q) * 2 + x) * ROWS, 1), :]
        for d in range(1, 4):
            xdown[pl.ds(((d - 1) * 12 + q) * 8, 8), :] = links[pl.ds((d * 18 + q) * 2 * ROWS + 2, 8), :]
        xdown[pl.ds(288 + q * 2, 2), :] = links[pl.ds((54 + q) * 2 * ROWS, 2), :]


def pack_up(links, up):
    def read(d, row):
        return load_matrix(lambda i, j, ri: links[pl.ds((comp(d, i, j, ri) * 2 + 1) * ROWS + row, 8), :])

    across = read(0, 2)
    for m in (1, 2, 3):
        side = read(m, 2)
        half = [[entry(across, side, i, k, True, False) for k in range(3)] for i in range(2)]
        if m == 2:
            last = [[(roll_z(v[0], 1), roll_z(v[1], 1)) for v in row] for row in across]
        else:
            last = read(0, 3 if m == 1 else 4)
        for i in range(2):
            for j in range(3):
                value = entry(half, last, i, j)
                for ri in range(2):
                    out = jnp.where(first_rows(), value[ri], half[i][j][ri]) if m == 1 else value[ri]
                    up[pl.ds(((m - 1) * 12 + (i * 3 + j) * 2 + ri) * 8, 8), :] = out


def pack_corners_body(ynext, yprev, up, down):
    for q in range(12):
        up[pl.ds(q * 4, 4), :] = ynext[pl.ds(q * 8 + 4, 4), :]
        down[pl.ds(q * 4, 4), :] = yprev[pl.ds((12 + q) * 8, 4), :]


def pack_lambda_down(lam, yprev, down):
    for c in range(24):
        down[pl.ds(c * 8, 8), :] = lam[pl.ds((c + NA) * 16, 8), :]
    for k in range(NA):
        down[pl.ds(192 + k * 4, 4), :] = yprev[pl.ds((NA + k) * 8, 4), :]


def two_rows(read):
    m = [[(read((i * 3 + j) * 2), read((i * 3 + j) * 2 + 1)) for j in range(3)] for i in range(2)]
    return m + [third_row(m)]


def put(write, m):
    for i in range(3):
        for j in range(3):
            for ri in range(2):
                write((i * 3 + j) * 2 + ri, m[i][j][ri])


def roll_z(v, by):
    return pltpu.roll(v, (128 - by) % 128, 1)


def fill_y(bufs, n, dirs_p, dirs_m):
    for x in (1, 2):
        for d in range(4):
            for k in range(n):
                at = place(d * n + k, x)
                if d in dirs_p:
                    bufs[YP][pl.ds(at, 6, stride=2), :] = bufs[O][pl.ds(at + 1, 6, stride=2), :]
                if d in dirs_m:
                    bufs[YM][pl.ds(at + 1, 6, stride=2), :] = bufs[O][pl.ds(at, 6, stride=2), :]


def fill_z(bufs, n):
    for d in range(4):
        for k in range(n):
            c = d * n + k
            for x in (1, 2):
                at = place(c, x)
                zp, zm = bufs[ZP], bufs[ZM]
                if d != 2:
                    zp[pl.ds(at + 2, 8), :] = roll_z(bufs[O][pl.ds(at + 2, 8), :], 1)
                if d == 3:
                    zp[pl.ds(at, 2), :] = roll_z(bufs[O][pl.ds(at, 2), :], 1)
                zm[pl.ds(at + 2, 8), :] = roll_z(bufs[O][pl.ds(at + 2, 8), :], -1)
                if d == 2:
                    zm[pl.ds(at + 10, 2), :] = roll_z(bufs[O][pl.ds(at + 10, 2), :], -1)


def fill_mixed(bufs, n):
    for k in range(n):
        for x in (1, 2):
            bufs[ZPYM][pl.ds(place(k, x) + 2, 8), :] = roll_z(bufs[YM][pl.ds(place(n + k, x) + 2, 8), :], 1)
            bufs[ZMYP][pl.ds(place(k, x) + 2, 8), :] = roll_z(bufs[YP][pl.ds(place(2 * n + k, x) + 2, 8), :], -1)


def fill_high(bufs, n):
    for k in range(n):
        high, side = place(2 * n + k, 3), place(n + k, 3)
        bufs[ZM][pl.ds(high + 2, 8), :] = roll_z(bufs[O][pl.ds(high + 2, 8), :], -1)
        bufs[YM][pl.ds(side + 3, 4, stride=2), :] = bufs[O][pl.ds(side + 2, 4, stride=2), :]


def fill_links_local(links, bufs):
    for c in range(72):
        for x in range(2):
            source, to = (c * 2 + x) * ROWS, place(c, x + 1)
            bufs[O][pl.ds(to, 8), :] = links[pl.ds(source, 8), :]
            bufs[O][pl.ds(to + 8, 4), :] = links[pl.ds(source + 8, 4), :]
    fill_y(bufs, NC, (0, 2, 3), (0, 1, 2, 3))
    fill_z(bufs, NC)


def fill_links_y(ynext, yprev, bufs):
    for d in range(4):
        for source, buf, off in ((ynext, YP, 3), (yprev, YM, 2)):
            if buf == YP and d == 1:
                continue
            slot = DOWN_Y.index(d) if buf == YP else d
            m = two_rows(lambda q: source[pl.ds((slot * 12 + q) * 8, 8), :])

            def write(q, v):
                for x in range(2):
                    bufs[buf][pl.ds(place(d * NC + q, x + 1) + off, 4, stride=2), :] = v[4 * x : 4 * x + 4]

            put(write, m)
    for source, buf, d, row, at in ((ynext, YP, 3, 1, 288), (yprev, YM, 1, 10, 384)):
        m = two_rows(lambda q: source[pl.ds(at + q * 2, 2), :])

        def write_row(q, v):
            for x in range(2):
                bufs[buf][pl.ds(place(d * NC + q, x + 1) + row, 1), :] = v[x : x + 1]

        put(write_row, m)
    fill_mixed(bufs, NC)


def fill_links_next(xnext, bufs):
    for d in (1, 2, 3):
        m = two_rows(lambda q: xnext[pl.ds(((d - 1) * 12 + q) * 8, 8), :])

        def write(q, v):
            bufs[O][pl.ds(place(d * NC + q, 3) + 2, 8), :] = v

        put(write, m)
    m = two_rows(lambda q: xnext[pl.ds(288 + q * 2, 2), :])

    def write_edge(q, v):
        bufs[O][pl.ds(place(3 * NC + q, 3), 2), :] = v

    put(write_edge, m)
    fill_high(bufs, NC)


def fill_corner(corner, buf, d, xe, off, bufs):
    m = two_rows(lambda q: corner[pl.ds(q * 4, 4), :])

    def write_corner(q, v):
        bufs[buf][pl.ds(place(d * NC + q, xe) + off, 4, stride=2), :] = v

    put(write_corner, m)


def take_staples(xprev, bufs, ready):
    for m in (1, 2, 3):
        staple = two_rows(lambda q: xprev[pl.ds(((m - 1) * 12 + q) * 8, 8), :])
        if m == 1:
            whole = mm(staple, link(bufs, 0, step((0, -1), (1, 1)), 0))
            staple = [
                [tuple(jnp.where(first_rows(), staple[i][j][ri], whole[i][j][ri]) for ri in range(2)) for j in range(3)]
                for i in range(3)
            ]
        for i in range(3):
            for j in range(3):
                for ri in range(2):
                    ready[pl.ds(comp(m - 1, i, j, ri) * 8, 8), :] = staple[i][j][ri]


def ready_staple(ready, m):
    return load_matrix(lambda i, j, ri: ready[pl.ds(comp(m - 1, i, j, ri) * 8, 8), :])


def fill_lambda_local(lam, bufs):
    zero = jnp.zeros((2, 128), jnp.float32)
    for c in range(32):
        for x in range(2):
            to = place(c, x + 1)
            bufs[O][pl.ds(to + 2, 8), :] = lam[pl.ds((c * 2 + x) * 8, 8), :]
            bufs[O][pl.ds(to, 2), :] = zero
            bufs[O][pl.ds(to + 10, 2), :] = zero
    fill_y(bufs, NA, (0, 2, 3), (0, 1, 2, 3))
    fill_z(bufs, NA)


def fill_lambda_y(ynext, yprev, bufs):
    zero = jnp.zeros((1, 128), jnp.float32)
    for d in range(4):
        for k in range(NA):
            for x in range(2):
                to = place(d * NA + k, x + 1)
                if d != 1:
                    source = pl.ds((DOWN_Y.index(d) * NA + k) * 8 + x * 4, 4)
                    bufs[YP][pl.ds(to + 3, 4, stride=2), :] = ynext[source, :]
                bufs[YM][pl.ds(to + 2, 4, stride=2), :] = yprev[pl.ds((d * NA + k) * 8 + x * 4, 4), :]
                if d == 3:
                    bufs[YP][pl.ds(to + 1, 1), :] = zero
                if d == 1:
                    bufs[YM][pl.ds(to + 10, 1), :] = zero
    fill_mixed(bufs, NA)


def fill_lambda_next(xnext, bufs):
    zero = jnp.zeros((2, 128), jnp.float32)
    for c in range(24):
        bufs[O][pl.ds(place(NA + c, 3) + 2, 8), :] = xnext[pl.ds(c * 8, 8), :]
    for k in range(NA):
        bufs[O][pl.ds(place(3 * NA + k, 3), 2), :] = zero
        bufs[YM][pl.ds(place(NA + k, 3) + 2, 4, stride=2), :] = xnext[pl.ds(192 + k * 4, 4), :]
    fill_high(bufs, NA)


def step(*signed):
    vector = [0, 0, 0, 0]
    for which, sign in signed:
        vector[which] += sign
    return vector


def where(bufs, n, d, offset, x):
    key = buffer_of[(offset[1], offset[2])]
    row = 2 + 2 * offset[3]
    dd = d - base_dir.get(key, 0)
    shift = (x + 1 + offset[0]) * ROWS

    def read(k):
        return bufs[key][pl.ds(place(dd * n + k, 0) + row + shift, 8), :]

    return read


def link(bufs, d, offset, x):
    read = where(bufs, NC, d, offset, x)
    return load_matrix(lambda i, j, ri: read((i * 3 + j) * 2 + ri))


def lam_at(bufs, d, offset, x):
    read = where(bufs, NA, d, offset, x)
    return unpack8([read(k) for k in range(NA)])


def exponent_force(v, m):
    a = v[:3]
    off = [(v[3 + 2 * k], v[4 + 2 * k]) for k in range(3)]
    norm = [r * r + s * s for r, s in off]
    sd = [
        -(a[0] * a[0] + norm[0] + norm[1]),
        -(a[1] * a[1] + norm[0] + norm[2]),
        -(a[2] * a[2] + norm[1] + norm[2]),
    ]
    (r0, s0), (r1, s1), (r2, s2) = off
    so = [
        (a[2] * s0 - (r1 * r2 + s1 * s2), -a[2] * r0 - (s1 * r2 - r1 * s2)),
        (a[1] * s1 + (r0 * r2 - s0 * s2), -a[1] * r1 + (r0 * s2 + s0 * r2)),
        (a[0] * s2 - (r0 * r1 + s0 * s1), -a[0] * r2 - (r0 * s1 - s0 * r1)),
    ]
    c = 0.5 * (sd[0] + sd[1] + sd[2])
    cross = [off[k][1] * so[k][0] - off[k][0] * so[k][1] for k in range(3)]
    dd = (a[0] * sd[0] + a[1] * sd[1] + a[2] * sd[2] + 2.0 * (cross[0] + cross[1] + cross[2])) * (1.0 / 3.0)
    p0r = 1.0 - dd * dd * (1.0 / 720.0)
    p0i = dd * (1.0 / 6.0 + c * (1.0 / 120.0))
    p1r = 1.0 + c * (1.0 / 6.0 + c * (1.0 / 120.0))
    p1i = dd * (1.0 / 24.0 + c * (1.0 / 360.0))
    p2r = 0.5 + c * (1.0 / 24.0 + c * (1.0 / 720.0))
    p2i = dd * (1.0 / 120.0)
    hd = [m[i][i][0] for i in range(3)]
    kd = [m[i][i][1] for i in range(3)]
    ho = [(0.5 * (m[i][j][0] + m[j][i][0]), 0.5 * (m[i][j][1] - m[j][i][1])) for i, j in UPPER]
    ko = [(0.5 * (m[i][j][0] - m[j][i][0]), 0.5 * (m[i][j][1] + m[j][i][1])) for i, j in UPPER]
    t0r = hd[0] + hd[1] + hd[2]
    t0i = -(kd[0] + kd[1] + kd[2])

    def dots(x, y, xo, yo):
        diag = x[0] * y[0] + x[1] * y[1] + x[2] * y[2]
        rest = [xo[k][0] * yo[k][0] + xo[k][1] * yo[k][1] for k in range(3)]
        return diag + 2.0 * (rest[0] + rest[1] + rest[2])

    def crossed(x, y, xo, yo):
        diag = x[0] * y[0] + x[1] * y[1] + x[2] * y[2]
        rest = [yo[k][1] * xo[k][0] - yo[k][0] * xo[k][1] for k in range(3)]
        return diag + 2.0 * (rest[0] + rest[1] + rest[2])

    t1r = dots(kd, a, ko, off)
    t1i = crossed(hd, a, ho, off)
    t2r = dots(hd, sd, ho, so)
    t2i = -crossed(sd, kd, so, ko)
    by_c = (
        t1r * (1.0 / 6.0 + c * (1.0 / 60.0))
        + t2r * (1.0 / 24.0 + c * (1.0 / 360.0))
        - dd * (t0i * (1.0 / 120.0) + t1i * (1.0 / 360.0))
    )
    by_d = -(
        dd * t0r * (1.0 / 360.0)
        + t0i * (1.0 / 6.0 + c * (1.0 / 120.0))
        + t1i * (1.0 / 24.0 + c * (1.0 / 360.0))
        + t2i * (1.0 / 120.0)
    )
    herm = [[None] * 3 for _ in range(3)]
    for i in range(3):
        herm[i][i] = (-(p2r * hd[i] + p2i * kd[i]), None)
    for k, (i, j) in enumerate(UPPER):
        re = -(p2r * ho[k][0] + p2i * ko[k][1])
        im = p2i * ko[k][0] - p2r * ho[k][1]
        herm[i][j] = (re, im)
        herm[j][i] = (re, -im)
    amat = anti(v)
    g = skew(mm(amat, herm))
    lam = [p1r * kd[i] - p1i * hd[i] + g[i] - by_c * a[i] + by_d * sd[i] for i in range(3)]
    for k in range(3):
        lam.append(p1r * ko[k][0] + p1i * ho[k][1] + g[3 + 2 * k] - by_c * off[k][0] - by_d * so[k][1])
        lam.append(p1r * ko[k][1] - p1i * ho[k][0] + g[4 + 2 * k] - by_c * off[k][1] + by_d * so[k][0])
    mean = (lam[0] + lam[1] + lam[2]) * (1.0 / 3.0)
    lam = [smear_weight * (lam[i] - mean) for i in range(3)] + [smear_weight * lam[k] for k in range(3, 9)]
    edag = [[None] * 3 for _ in range(3)]
    for i in range(3):
        edag[i][i] = (p0r - p1i * a[i] + p2r * sd[i], -(p0i + p1r * a[i] + p2i * sd[i]))
    for k, (i, j) in enumerate(UPPER):
        r, s = off[k]
        sr, si = so[k]
        edag[i][j] = (
            (p2r * sr - p1i * s) + (p2i * si - p1r * r),
            (p1i * r - p2i * sr) + (p2r * si - p1r * s),
        )
        edag[j][i] = (
            (p2r * sr - p1i * s) - (p2i * si - p1r * r),
            -(p1i * r + p2i * sr) - (p2r * si + p1r * s),
        )
    return lam, edag


def plane_fields(m, n):
    here = step()
    return [(m, here), (n, here), (n, step((m, 1))), (m, step((n, 1)))]


def lower_fields(m, n):
    back = step((n, -1))
    return [(n, back), (m, back), (n, step((n, -1), (m, 1)))]


def level(fields, x):
    found = 0
    for _, offset in fields:
        if x + offset[0] == -1:
            found = 3
        elif x + offset[0] == 2:
            found = max(found, 3 if offset[1] else 2)
        elif offset[1]:
            found = max(found, 1)
    return found


LOWERS = [(m, n) for m in range(4) for n in range(4) if n != m]


def items(wanted):
    planes = [(p, m, n, x) for x in range(2) for p, (m, n) in enumerate(PAIRS) if level(plane_fields(m, n), x) == wanted]
    lowers = [(m, n, x) for x in range(2) for m, n in LOWERS if level(lower_fields(m, n), x) == wanted]
    return planes, lowers


def cells(n, k, x):
    return pl.ds((n + k) * 16 + x * 8, 8)


def load_cells(ref, n, x):
    return load_matrix(lambda i, j, ri: ref[cells(n, (i * 3 + j) * 2 + ri, x), :])


def store_cells(ref, n, x, m):
    for i in range(3):
        for j in range(3):
            for ri in range(2):
                ref[cells(n, (i * 3 + j) * 2 + ri, x), :] = m[i][j][ri]


def take_incoming(incoming, inner):
    for c in range(144):
        inner[pl.ds(c * 8, 4, stride=2), :] = incoming[pl.ds(c * 8, 4), :]
        inner[pl.ds(c * 8 + 1, 4, stride=2), :] = incoming[pl.ds(c * 8 + 4, 4), :]


def forward_items(wanted, bufs, omega, loops, low, ready=None):
    planes, lowers = items(wanted)
    begun = {(m, x) for w in range(wanted) for m, _, x in items(w)[1]}
    for p, m, n, x in planes:
        a, d, b, c = [link(bufs, which, offset, x) for which, offset in plane_fields(m, n)]
        loop = mm(mm(a, b), mm(d, c), False, True)
        store_cells(omega, p * 18, x, loop)
        for k, v in enumerate(skew(loop)):
            loops[cells(p * 9, k, x), :] = v
    for m in range(4):
        for x in range(2):
            value = load_cells(low, m * 18, x) if (m, x) in begun else None
            mine = [n for mm_, n, xx in lowers if (mm_, xx) == (m, x)]
            if not mine:
                continue
            for n in mine:
                if n == 0 and x == 0:
                    term = ready_staple(ready, m)
                else:
                    e, g, h = [link(bufs, which, offset, x) for which, offset in lower_fields(m, n)]
                    term = mm(mm(e, g, True, False), h)
                value = term if value is None else madd(value, term)
            store_cells(low, m * 18, x, value)


def target_products(bufs, inner, moved):
    for x in range(2):
        for m in range(4):
            target = load_cells(inner, m * 18, x)
            store_cells(moved, m * 18, x, mm(target, link(bufs, m, step(), x), False, True))


def finish_forward(bufs, moved, loops, low, lam_out, edag):
    for x in range(2):
        for m in range(4):
            u = link(bufs, m, step(), x)
            below = load_cells(low, m * 18, x)
            v = skew_product(below, u, True)
            for p, (f, s) in enumerate(PAIRS):
                if m == f:
                    v = [v[k] - loops[cells(p * 9, k, x), :] for k in range(9)]
                if m == s:
                    v = [v[k] + loops[cells(p * 9, k, x), :] for k in range(9)]
            mean = (v[0] + v[1] + v[2]) * (1.0 / 3.0)
            v = [(0.5 * smear_weight) * (v[k] - mean) for k in range(3)] + [
                (0.5 * smear_weight) * v[k] for k in range(3, 9)
            ]
            lam, smearing = exponent_force(v, load_cells(moved, m * 18, x))
            for k, v in enumerate(lam[:2] + lam[3:]):
                lam_out[cells(m * NA, k, x), :] = v
            store_cells(edag, m * 18, x, smearing)


def backward_items(wanted, bufs, lams, omega, sums, acc, ready=None, xprev=None):
    planes, lowers = items(wanted)
    begun = {(d, x) for w in range(wanted) for _, m, n, x in items(w)[0] for d in (m, n)}

    def gather(d, x, m):
        store_cells(sums, d * 18, x, madd(load_cells(sums, d * 18, x), m) if (d, x) in begun else m)
        begun.add((d, x))

    for p, m, n, x in planes:
        fields = plane_fields(m, n)
        a, d = [link(bufs, which, offset, x) for which, offset in fields[:2]]
        la, ld, lb, lc = [lam_at(lams, which, offset, x) for which, offset in fields]
        lb, lc = carried(a, lb), carried(d, lc)
        loop = load_cells(omega, p * 18, x)
        z = [ld[k] - la[k] for k in range(9)]
        first = anti([z[k] + lc[k] for k in range(9)])
        second = anti([lb[k] - z[k] for k in range(9)])
        gather(m, x, msub(mm(first, loop, False, True), mm(loop, anti(lb), True, False)))
        gather(n, x, msub(mm(second, loop), mm(loop, anti(lc))))
    for m in range(4):
        for x in range(2):
            mine = [n for mm_, n, xx in lowers if (mm_, xx) == (m, x)]
            if not mine:
                continue
            force = load_cells(acc, m * 18, x)
            for n in mine:
                if n == 0 and x == 0:
                    y = unpack8([xprev[pl.ds(((m - 1) * NA + k) * 8, 8), :] for k in range(NA)])
                    force = madd(force, mm(anti(y), ready_staple(ready, m)))
                    continue
                fields = lower_fields(m, n)
                e, g, h = [link(bufs, which, offset, x) for which, offset in fields]
                le, lg, lh = [lam_at(lams, which, offset, x) for which, offset in fields]
                inside = madd(mm(anti([lg[k] - le[k] for k in range(9)]), g), mm(g, anti(lh)))
                force = madd(force, mm(mm(e, inside, True, False), h))
            store_cells(acc, m * 18, x, force)


def add_loops(bufs, sums, acc, m, x):
    f = load_cells(sums, m * 18, x)
    store_cells(acc, m * 18, x, madd(mm(f, link(bufs, m, step(), x)), load_cells(acc, m * 18, x)))


def finish_backward(bufs, sums, acc, out):
    for x in range(2):
        for m in range(4):
            if x == 1:
                add_loops(bufs, sums, acc, m, x)
            for k in range(18):
                at = ((m * 18 + k) * 2 + x) * 8
                out[pl.ds(at, 4), :] = acc[pl.ds(at, 4, stride=2), :]
                out[pl.ds(at + 4, 4), :] = acc[pl.ds(at + 1, 4, stride=2), :]


def links_local_body(*refs):
    links = refs[0]
    bufs, (omega, loops, low) = refs[1:8], refs[8:]
    fill_links_local(links, bufs)
    forward_items(0, bufs, omega, loops, low)


def links_y_body(*refs):
    ynext, yprev, incoming = refs[:3]
    bufs, (omega, loops, low, inner, moved) = refs[13:20], refs[20:]
    fill_links_y(ynext, yprev, bufs)
    take_incoming(incoming, inner)
    forward_items(1, bufs, omega, loops, low)
    target_products(bufs, inner, moved)


def links_next_body(*refs):
    xnext = refs[0]
    bufs, (omega, loops, low) = refs[11:18], refs[18:]
    fill_links_next(xnext, bufs)
    forward_items(2, bufs, omega, loops, low)


def links_x_body(*refs):
    cnext, xprev, cprev, moved = refs[:4]
    bufs, (omega, loops, low, lam, edag, up, down, ready) = refs[14:21], refs[21:]
    fill_corner(cnext, YM, 1, 3, 2, bufs)
    fill_corner(cprev, YP, 0, 0, 3, bufs)
    take_staples(xprev, bufs, ready)
    forward_items(3, bufs, omega, loops, low, ready)
    finish_forward(bufs, moved, loops, low, lam, edag)

    def reader(row):
        return lambda d, q, x: lam[pl.ds(((d * NA + q) * 2 + x) * 8 + row, 4, stride=2), :]

    pack_y(up, down, NA, reader(1), reader(0))


def lambda_local_body(*refs):
    bufs, (omega, lam, inner, low) = refs[:7], refs[7:11]
    acc, lams, sums = refs[12], refs[13:20], refs[20]
    fill_lambda_local(lam, lams)
    for x in range(2):
        for m in range(4):
            own = anti(unpack8([lam[cells(m * NA, k, x), :] for k in range(NA)]))
            force = mm(load_cells(acc, m * 18, x), load_cells(inner, m * 18, x))
            store_cells(acc, m * 18, x, msub(force, mm(own, load_cells(low, m * 18, x))))
    backward_items(0, bufs, lams, omega, sums, acc)


def lambda_up_body(*refs):
    ynext, yprev, links, lam = refs[:4]
    lams, (up, down) = refs[11:18], refs[18:]
    pack_lambda_down(lam, yprev, down)
    fill_lambda_y(ynext, yprev, lams)
    here = step()
    for m in (1, 2, 3):
        a, d = link([links], 0, here, 1), link([links], m, here, 1)
        la, ld, lc = lam_at(lams, 0, here, 1), lam_at(lams, m, here, 1), lam_at(lams, 0, step((m, 1)), 1)
        lc = carried(d, lc)
        y = carried_back(a, [ld[k] - la[k] + lc[k] for k in range(9)])
        for k, v in enumerate(y[:2] + y[3:]):
            up[pl.ds(((m - 1) * NA + k) * 8, 8), :] = v


def lambda_y_body(*refs):
    bufs, omega, lams = refs[:7], refs[7], refs[8:15]
    acc, sums = refs[17:]
    backward_items(1, bufs, lams, omega, sums, acc)
    for m in range(4):
        add_loops(bufs, sums, acc, m, 0)


def lambda_x_body(*refs):
    bufs, (omega, ready, xnext, xprev) = refs[:7], refs[7:11]
    out, acc, lams, sums = refs[20], refs[21], refs[22:29], refs[29]
    fill_lambda_next(xnext, lams)
    backward_items(2, bufs, lams, omega, sums, acc)
    backward_items(3, bufs, lams, omega, sums, acc, ready, xprev)
    finish_backward(bufs, sums, acc, out)


def rows(n):
    return jax.ShapeDtypeStruct((n, 128), jnp.float32)


def buffer_rows(n):
    return [(n if key in base_dir else 4 * n) * 4 * ROWS for key in range(7)]


def call(body, args, outs, kept=(), cost=0, first=0):
    shapes = [rows(n) for n in outs]
    shapes[first:first] = [rows(a.shape[0]) for a in kept]
    return pl.pallas_call(
        body,
        out_shape=tuple(shapes),
        in_specs=[pl.BlockSpec(memory_space=pltpu.VMEM)] * (len(args) + len(kept)),
        out_specs=(pl.BlockSpec(memory_space=pltpu.VMEM),) * len(shapes),
        input_output_aliases={len(args) + k: first + k for k in range(len(kept))},
        cost_estimate=pl.CostEstimate(flops=cost, bytes_accessed=0, transcendentals=0) if cost else None,
        compiler_params=pltpu.CompilerParams(vmem_limit_bytes=VM),
    )(*args, *kept)


def shifted(shard, axis, by):
    length = lax.axis_size(axis)
    return lax.ppermute(shard, axis, [(i, (i + by) % length) for i in range(length)])


def body(links, incoming):
    links = jnp.transpose(links, (0, 1, 2, 3, 4, 6, 5, 7)).reshape(144 * ROWS, 128)
    shape = incoming.shape
    incoming = incoming.reshape(1152, 128)
    xup, xdown, yup, ydown = call(pack_first_body, (links,), (288, 312, 408, 312))
    xprev, xnext = shifted(xup, "gx", 1), shifted(xdown, "gx", -1)
    yprev, ynext = shifted(yup, "gy", 1), shifted(ydown, "gy", -1)
    cup, cdown = call(pack_corners_body, (ynext, yprev), (48, 48))
    cprev, cnext = shifted(cup, "gx", 1), shifted(cdown, "gx", -1)
    kept = call(links_local_body, (links,), buffer_rows(NC) + [1728, 864, 1152])
    *kept, inner, moved = call(links_y_body, (ynext, yprev, incoming), (1152, 1152), kept)
    kept = call(links_next_body, (xnext,), (), kept)
    r = call(links_x_body, (cnext, xprev, cprev, moved), (512, 1152, 256, 192, 432), kept)
    bufs, omega, low, (lam, acc, yup, ydown, ready) = r[:7], r[7], r[9], r[10:]
    yprev, ynext = shifted(yup, "gy", 1), shifted(ydown, "gy", -1)
    acc, *lams, sums = call(lambda_local_body, (*bufs, omega, lam, inner, low), buffer_rows(NA) + [1152], (acc,))
    *lams, xup, xdown = call(lambda_up_body, (ynext, yprev, bufs[O], lam), (192, 224), lams)
    xprev, xnext = shifted(xup, "gx", 1), shifted(xdown, "gx", -1)
    acc, sums = call(lambda_y_body, (*bufs, omega, *lams), (), (acc, sums))
    out = call(lambda_x_body, (*bufs, omega, ready, xnext, xprev), (1152,), (acc, *lams, sums), first=1)[0]
    return out.reshape(shape)


def solution(mesh):
    placed = P(None, None, None, None, "gx", "gy", None, None)
    return jax.shard_map(body, mesh=mesh, in_specs=(placed, placed), out_specs=placed, check_vma=False)
```
